128 devices in a mesh: dp: 16 (over x_lo, z, core), tensor: 8 (over y, x_hi).
Axes of the slice: x: 4 (x_hi: 2, x_lo: 2; x = x_hi * 2 + x_lo), y: 4, z: 4, core: 2. Of those that a mesh axis runs over, the one named last changes fastest.
Arguments:
- tokens: bfloat16 [16384, 2048], P(('dp', 'tensor')), may hold values from -6 to 6
- cotangent: bfloat16 [16384, 2048], P(('dp', 'tensor')), may hold values from -6 to 6
- row_lengths: int32 [3], replicated, may hold values from 1 to 15872, as said below
- gains: float32 [2, 2048], P(None, 'dp'), may hold values from 0.5 to 1.5
- gain_first: float32 [2, 2048], P(None, 'dp'), may hold values from -768 to 768
- gain_second: float32 [2, 2048], P(None, 'dp'), may hold values from 8192 to 131072
- feature_weight: float32 [2048, 2, 256], P('dp', None, 'tensor'), may hold values from -0.125 to 0.125
- feature_first: float32 [2048, 2, 256], P('dp', None, 'tensor'), may hold values from -80 to 80
- feature_second: float32 [2048, 2, 256], P('dp', None, 'tensor'), may hold values from 81.92 to 1310.72
- value_weight: float32 [2048, 2048], P('dp', 'tensor'), may hold values from -0.125 to 0.125
- value_first: float32 [2048, 2048], P('dp', 'tensor'), may hold values from -80 to 80
- value_second: float32 [2048, 2048], P('dp', 'tensor'), may hold values from 81.92 to 1310.72
- output_weight: float32 [2048, 2048], P('tensor', 'dp'), may hold values from -1 to 1
- output_first: float32 [2048, 2048], P('tensor', 'dp'), may hold values from -24 to 24
- output_second: float32 [2048, 2048], P('tensor', 'dp'), may hold values from 8.192 to 131.072
- gateup_weight: float32 [2048, 2, 5504], P('dp', None, 'tensor'), may hold values from -0.125 to 0.125
- gateup_first: float32 [2048, 2, 5504], P('dp', None, 'tensor'), may hold values from -384 to 384
- gateup_second: float32 [2048, 2, 5504], P('dp', None, 'tensor'), may hold values from 2048 to 32768
- down_weight: float32 [5504, 2048], P('tensor', 'dp'), may hold values from -0.078125 to 0.078125
- down_first: float32 [5504, 2048], P('tensor', 'dp'), may hold values from -384 to 384
- down_second: float32 [5504, 2048], P('tensor', 'dp'), may hold values from 2048 to 32768
Outputs:
- mixed: bfloat16 [16384, 2048], P(('dp', 'tensor'))
- grad_tokens: float32 [16384, 2048], P(('dp', 'tensor'))
- den_mean: float32 [], replicated
- gain_moment: float32 [2, 2048], P(None, 'dp')
- gain_square: float32 [2, 2048], P(None, 'dp')
- gain_master: float32 [2, 2048], P(None, 'dp')
- feature_moment: float32 [2048, 2, 256], P('dp', None, 'tensor')
- feature_square: float32 [2048, 2, 256], P('dp', None, 'tensor')
- feature_master: float32 [2048, 2, 256], P('dp', None, 'tensor')
- value_moment: float32 [2048, 2048], P('dp', 'tensor')
- value_square: float32 [2048, 2048], P('dp', 'tensor')
- value_master: float32 [2048, 2048], P('dp', 'tensor')
- output_moment: float32 [2048, 2048], P('tensor', 'dp')
- output_square: float32 [2048, 2048], P('tensor', 'dp')
- output_master: float32 [2048, 2048], P('tensor', 'dp')
- gateup_moment: float32 [2048, 2, 5504], P('dp', None, 'tensor')
- gateup_square: float32 [2048, 2, 5504], P('dp', None, 'tensor')
- gateup_master: float32 [2048, 2, 5504], P('dp', None, 'tensor')
- down_moment: float32 [5504, 2048], P('tensor', 'dp')
- down_square: float32 [5504, 2048], P('tensor', 'dp')
- down_master: float32 [5504, 2048], P('tensor', 'dp')
The draws below stay inside these ranges and needn't reach their ends.
Inputs may be any that keep to these rules, and one draw needn't show every extreme that they name: `row_lengths`: three rows are packed in order: a short row, a row of 15872 tokens, and a short row; the two short rows hold 512 tokens together.
All inputs are finite; a program needn't handle non-finite values.
Results may differ from the reference program's by a relative error of at most 0.035.
Values may be sent and summed in bfloat16 or wider, within the bound.
No kernel may reach another device: no remote copies, remote signals or barrier semaphores. Data moves between devices by JAX's collectives and lax.ppermute only.
A program may use at most 192 MiB of HBM per device.

```python
import math
import jax
import jax.numpy as jnp
from jax import lax

D = 2048
HEADS = 16
FEAT = 16
DV = 128
FF = 5504
BLOCK = 512
SHORT = 512
STEP = 10
TOKENS = 16384


def draw_row_lengths(key, part):
    key = jax.random.fold_in(key, 11)
    head_len = jax.random.randint(key, (1,), 1, SHORT, dtype=jnp.int32)
    middle = jnp.full((1,), TOKENS - SHORT, jnp.int32)
    return jnp.concatenate([head_len, middle, SHORT - head_len]).astype(jnp.int32)


def block_scale(rng, extent, cuts, low, top_value):
    def one(position, blocks):
        draws = jax.random.uniform(jax.random.fold_in(jax.random.fold_in(rng, 6), position), (blocks,), jnp.float32, low / len(cuts), top_value / len(cuts))
        return jnp.repeat(jnp.exp(draws), extent[position] // blocks).reshape((-1,) + (1,) * (len(extent) - position - 1))

    factor_of = one(*cuts[0])
    for cut in cuts[1:]:
        factor_of = factor_of * one(*cut)
    return factor_of


def normal_values(rng, extent, spread, bound, cuts=(), held_as=jnp.bfloat16):
    values = spread * jax.random.normal(rng, extent, jnp.float32)
    if cuts:
        values = values * block_scale(rng, extent, cuts, -0.22, 0.18)
    return jnp.clip(values, -bound, bound).astype(held_as)


def setup_inputs(seed: int = 0) -> dict:
    streams_of = jax.random.split(jax.random.key(seed), 22)
    tokens = normal_values(streams_of[0], (TOKENS, D), 1.0, 6.0, ((0, 128),))
    cotangent = normal_values(streams_of[1], (TOKENS, D), 1.0, 6.0, ((0, 128),))
    row_lengths = draw_row_lengths(jax.random.fold_in(streams_of[21], 71), 0)
    gains = jnp.clip(1.0 + 0.1 * jax.random.normal(streams_of[3], (2, D), jnp.float32), 0.5, 1.5)
    gain_first = normal_values(streams_of[4], (2, D), (TOKENS ** 0.5), 768.0, ((1, 16),), jnp.float32)
    gain_second = jnp.clip(jnp.exp(math.log(131072.0) - 2.7725887 * jax.random.uniform(streams_of[5], (2, D), jnp.float32) ** block_scale(streams_of[5], (2, D), ((1, 16),), -0.2, 0.2)), 8192.0, 131072.0)
    feature_weight = normal_values(streams_of[6], (D, 2, HEADS * FEAT), D ** -0.5, 0.125, ((0, 16), (2, 8)), jnp.float32)
    feature_first = normal_values(streams_of[7], (D, 2, HEADS * FEAT), (0.1 * TOKENS ** 0.5), 80.0, ((0, 16), (2, 8)), jnp.float32)
    feature_second = jnp.clip(jnp.exp(math.log(1310.72) - 2.7725887 * jax.random.uniform(streams_of[8], (D, 2, HEADS * FEAT), jnp.float32) ** block_scale(streams_of[8], (D, 2, HEADS * FEAT), ((0, 16), (2, 8)), -0.2, 0.2)), 81.92, 1310.72)
    value_weight = normal_values(streams_of[9], (D, HEADS * DV), D ** -0.5, 0.125, ((0, 16), (1, 8)), jnp.float32)
    value_first = normal_values(streams_of[10], (D, HEADS * DV), (0.1 * TOKENS ** 0.5), 80.0, ((0, 16), (1, 8)), jnp.float32)
    value_second = jnp.clip(jnp.exp(math.log(1310.72) - 2.7725887 * jax.random.uniform(streams_of[11], (D, HEADS * DV), jnp.float32) ** block_scale(streams_of[11], (D, HEADS * DV), ((0, 16), (1, 8)), -0.2, 0.2)), 81.92, 1310.72)
    output_weight = normal_values(streams_of[12], (HEADS * DV, D), (HEADS * DV // 64) ** -0.5, 1.0, ((0, 8), (1, 16)), jnp.float32)
    output_first = normal_values(streams_of[13], (HEADS * DV, D), (0.03 * TOKENS ** 0.5), 24.0, ((0, 8), (1, 16)), jnp.float32)
    output_second = jnp.clip(jnp.exp(math.log(131.072) - 2.7725887 * jax.random.uniform(streams_of[14], (HEADS * DV, D), jnp.float32) ** block_scale(streams_of[14], (HEADS * DV, D), ((0, 8), (1, 16)), -0.2, 0.2)), 8.192, 131.072)
    gateup_weight = normal_values(streams_of[15], (D, 2, FF), D ** -0.5, 0.125, ((0, 16), (2, 8)), jnp.float32)
    gateup_first = normal_values(streams_of[16], (D, 2, FF), (0.5 * TOKENS ** 0.5), 384.0, ((0, 16), (2, 8)), jnp.float32)
    gateup_second = jnp.clip(jnp.exp(math.log(32768.0) - 2.7725887 * jax.random.uniform(streams_of[17], (D, 2, FF), jnp.float32) ** block_scale(streams_of[17], (D, 2, FF), ((0, 16), (2, 8)), -0.2, 0.2)), 2048.0, 32768.0)
    down_weight = normal_values(streams_of[18], (FF, D), FF ** -0.5, 0.078125, ((0, 8), (1, 16)), jnp.float32)
    down_first = normal_values(streams_of[19], (FF, D), (0.5 * TOKENS ** 0.5), 384.0, ((0, 8), (1, 16)), jnp.float32)
    down_second = jnp.clip(jnp.exp(math.log(32768.0) - 2.7725887 * jax.random.uniform(streams_of[20], (FF, D), jnp.float32) ** block_scale(streams_of[20], (FF, D), ((0, 8), (1, 16)), -0.2, 0.2)), 2048.0, 32768.0)
    return {"tokens": tokens, "cotangent": cotangent, "row_lengths": row_lengths, "gains": gains, "gain_first": gain_first, "gain_second": gain_second, "feature_weight": feature_weight, "feature_first": feature_first, "feature_second": feature_second, "value_weight": value_weight, "value_first": value_first, "value_second": value_second, "output_weight": output_weight, "output_first": output_first, "output_second": output_second, "gateup_weight": gateup_weight, "gateup_first": gateup_first, "gateup_second": gateup_second, "down_weight": down_weight, "down_first": down_first, "down_second": down_second}


@jax.custom_vjp
def low(v):
    return lax.optimization_barrier(v.astype(jnp.bfloat16)).astype(jnp.float32)

@jax.custom_vjp
def low_back(v):
    return v

def low_keep(v):
    return (low(v), None)

def low_pass(kept, grad):
    return (grad,)

def back_keep(v):
    return (v, None)

def back_low(kept, grad):
    return (low(grad),)
low.defvjp(low_keep, low_pass)
low_back.defvjp(back_keep, back_low)
norm_eps = 1e-05
beta_one = 0.5
beta_two = 0.5
adam_eps = 1e-08
weight_decay = 0.01
gain_rate = 0.5
highest = lax.Precision.HIGHEST

def doc_index(positions, row_lengths):
    ends = jnp.cumsum(row_lengths).astype(jnp.int32)
    return lax.optimization_barrier(jnp.sum((positions[:, None] >= ends[None, :]).astype(jnp.int32), axis=1)).astype(jnp.int32)

def features(values, feat_dim):
    leading = values.shape[:-1]
    outer_pairs = (values[..., :, None] * values[..., None, :]).reshape(leading + (feat_dim * feat_dim,))
    constant = jnp.ones(leading + (1,), jnp.float32)
    return jnp.concatenate([constant, values * feat_dim ** (-0.25), outer_pairs * (2.0 * feat_dim) ** (-0.5)], axis=-1)

def rms_norm(inputs, gain_row):
    inv_rms = lax.rsqrt(lax.optimization_barrier(jnp.mean(inputs * inputs, axis=-1, keepdims=True)) + norm_eps)
    return inputs * inv_rms * gain_row

def attend_block(query_blk, key_blk, value_blk, doc_blk, previous, kv_state, norm_state):
    block_len = query_blk.shape[0]
    scores = low_back(jnp.einsum('thf,jhf->htj', query_blk, key_blk, precision=highest) * FEAT ** (-0.5))
    row_pos = lax.broadcasted_iota(jnp.int32, (block_len, block_len), 0)
    col_pos = lax.broadcasted_iota(jnp.int32, (block_len, block_len), 1)
    allowed = (col_pos <= row_pos) & (doc_blk[None, :] == doc_blk[:, None])
    kernel = jnp.where(allowed[None], 1.0 + scores + 0.5 * scores * scores, 0.0)
    inner_sum = low_back(jnp.einsum('htj,jhv->thv', low(kernel), value_blk, precision=highest))
    continues = (doc_blk == previous).astype(jnp.float32)[:, None]
    query_feats = features(query_blk, FEAT)
    carried = jnp.einsum('thp,hpv->thv', query_feats, kv_state, precision=highest)
    numerator = inner_sum + continues[:, :, None] * carried
    denominator = lax.optimization_barrier(jnp.sum(kernel, axis=-1)).T + continues * jnp.einsum('thp,hp->th', query_feats, norm_state, precision=highest)
    result = numerator / denominator[:, :, None]
    last_doc = doc_blk[block_len - 1]
    carry_on = (last_doc == previous).astype(jnp.float32)
    in_last = (doc_blk == last_doc).astype(jnp.float32)[:, None, None]
    key_feats = features(key_blk, FEAT) * in_last
    new_state = carry_on * kv_state + jnp.einsum('thp,thv->hpv', key_feats, value_blk, precision=highest)
    new_norm = carry_on * norm_state + lax.optimization_barrier(jnp.sum(key_feats, axis=0))
    return (result, denominator, new_state, new_norm)

def attention(queries, keys_all, values_all, doc_ids):
    blocks = TOKENS // BLOCK
    previous = jnp.concatenate([jnp.full((1,), -1, jnp.int32), doc_ids[BLOCK - 1::BLOCK][:blocks - 1].astype(jnp.int32)])
    block_items = (queries.reshape(blocks, BLOCK, HEADS, FEAT), keys_all.reshape(blocks, BLOCK, HEADS, FEAT), values_all.reshape(blocks, BLOCK, HEADS, DV), doc_ids.reshape(blocks, BLOCK), previous)

    def step_fn(carried, block_item):
        query_blk, key_blk, value_blk, doc_blk, prev_doc = block_item
        result, denominator, new_state, new_norm = attend_block(query_blk, key_blk, value_blk, doc_blk, prev_doc, carried[0], carried[1])
        return ((new_state, new_norm), (result, denominator))
    width_phi = 1 + FEAT + FEAT * FEAT
    initial = (jnp.zeros((HEADS, width_phi, DV), jnp.float32), jnp.zeros((HEADS, width_phi), jnp.float32))
    unused, (results, denoms) = lax.scan(jax.checkpoint(step_fn), initial, block_items)
    return (results.reshape(TOKENS, HEADS * DV), denoms)

def adam_step(weight, moment_one, moment_two, reduced, step_rate):
    new_one = beta_one * moment_one + (1.0 - beta_one) * reduced
    new_two = beta_two * moment_two + (1.0 - beta_two) * reduced * reduced
    corrected_one = new_one / (1.0 - beta_one ** STEP)
    corrected_two = new_two / (1.0 - beta_two ** STEP)
    master = weight - step_rate * (corrected_one / (jnp.sqrt(corrected_two) + adam_eps) + weight_decay * weight)
    return (new_one, new_two, master)

def reference(tokens, cotangent, row_lengths, gains, gain_first, gain_second, feature_weight, feature_first, feature_second, value_weight, value_first, value_second, output_weight, output_first, output_second, gateup_weight, gateup_first, gateup_second, down_weight, down_first, down_second):
    positions = jnp.arange(TOKENS, dtype=jnp.int32)
    doc_ids = doc_index(positions, row_lengths)

    def forward(inputs, gain_vals, feature_mat, value_mat, output_mat, gateup_mat, down_mat):
        gain_low = low(gain_vals)
        acts_one = low(rms_norm(inputs, gain_low[0]))
        projected = low_back(low(jnp.einsum('td,dcf->tcf', acts_one, low(feature_mat), precision=highest)))
        queries = projected[:, 0].reshape(TOKENS, HEADS, FEAT)
        keys_all = projected[:, 1].reshape(TOKENS, HEADS, FEAT)
        values_all = low_back(low(jnp.dot(acts_one, low(value_mat), precision=highest))).reshape(TOKENS, HEADS, DV)
        attended, denoms = attention(queries, keys_all, values_all, doc_ids)
        attn_rows = low_back(low(attended))
        middle = inputs + low_back(jnp.dot(attn_rows, low(output_mat), precision=highest))
        acts_two = low(rms_norm(middle, gain_low[1]))
        gate_up = jnp.einsum('td,dcf->tcf', acts_two, low(gateup_mat), precision=highest)
        gate_vals = low_back(gate_up[:, 0])
        up_vals = low_back(gate_up[:, 1])
        hidden = low(jax.nn.silu(gate_vals) * up_vals)
        mixed_rows = middle + low_back(jnp.dot(hidden, low(down_mat), precision=highest))
        return (mixed_rows, jnp.mean(jnp.abs(denoms)))
    inputs = tokens.astype(jnp.float32)
    mixed, pull_back, den_mean = jax.vjp(forward, inputs, gains, feature_weight, value_weight, output_weight, gateup_weight, down_weight, has_aux=True)
    grad_tokens, gain_grad, feature_grad, value_grad, output_grad, gateup_grad, down_grad = pull_back(cotangent.astype(jnp.float32))
    gain_new = adam_step(gains, gain_first, gain_second, gain_grad, gain_rate)
    feature_new = adam_step(feature_weight, feature_first, feature_second, feature_grad, D ** (-0.5))
    value_new = adam_step(value_weight, value_first, value_second, value_grad, D ** (-0.5))
    output_new = adam_step(output_weight, output_first, output_second, output_grad, (HEADS * DV // 64) ** (-0.5))
    gateup_new = adam_step(gateup_weight, gateup_first, gateup_second, gateup_grad, D ** (-0.5))
    down_new = adam_step(down_weight, down_first, down_second, down_grad, FF ** (-0.5))
    return (mixed.astype(jnp.bfloat16), grad_tokens, den_mean, gain_new[0], gain_new[1], gain_new[2], feature_new[0], feature_new[1], feature_new[2], value_new[0], value_new[1], value_new[2], output_new[0], output_new[1], output_new[2], gateup_new[0], gateup_new[1], gateup_new[2], down_new[0], down_new[1], down_new[2])
```

```python
import functools

import jax
import jax.numpy as jnp
import numpy as np
from jax import lax
from jax.experimental import pallas as pl
from jax.experimental.pallas import tpu as pltpu
from jax.sharding import PartitionSpec as P

D = 2048
HEADS = 16
FEAT = 16
DV = 128
FF = 5504
STEP = 10
FINE = ("x_lo", "z", "core", "y", "x_hi")
GROUPS = ("x_lo", "z", "x_hi")
N_GROUPS = 16
ROWS = 1024
CHUNK = 128
LOCAL_HEADS = 2
QK = 2 * LOCAL_HEADS * FEAT
VW = LOCAL_HEADS * DV
PW = VW + QK
FFL = 688
FFP = 768
PHI = 256
PHI_ROWS = 160
HEAD_ROWS = 192
STATE_ROWS = LOCAL_HEADS * HEAD_ROWS
TILE = 256

norm_eps = 1e-05
beta_one = 0.5
beta_two = 0.5
adam_eps = 1e-08
weight_decay = 0.01
gain_rate = 0.5

f32 = jnp.float32
bf16 = jnp.bfloat16


def ring(step):
    return [(i, (i + step) % 4) for i in range(4)]


FLIP = [(0, 1), (1, 0)]
CROSS = [(0, 0), (1, 2), (2, 1), (3, 3)]


def cross(a):
    return lax.ppermute(a, ("core", "x_hi"), CROSS)


def from_y(a, step):
    return lax.ppermute(a, "y", ring(-step))


def to_y(a, step):
    return lax.ppermute(a, "y", ring(step))


def swap_core(a):
    return lax.ppermute(a, "core", FLIP)


def gather_rows(mine):
    pieces = [mine, from_y(mine, 1), from_y(mine, 2), from_y(mine, 3)]
    others = [swap_core(piece) for piece in pieces]
    return jnp.concatenate(pieces + others, axis=0)


def scatter_rows(partial_of):
    send = partial_of(1).astype(bf16)
    got = swap_core(send)
    kept = partial_of(0)
    total = kept + got.astype(f32)
    low = total.astype(bf16)
    parts = [to_y(low[d * CHUNK : (d + 1) * CHUNK], d) for d in (1, 2, 3)]
    out = total[:CHUNK]
    for part in parts:
        out = out + part.astype(f32)
    return out


def matmul(a, b, dims=((1,), (0,))):
    return lax.dot_general(a, b, (dims, ((), ())), preferred_element_type=f32)


def feature_tables():
    pairs = [(a, b) for a in range(FEAT) for b in range(a, FEAT)]
    left = np.zeros((4, QK, PHI), np.float32)
    right = np.zeros((4, QK, PHI), np.float32)
    rows = np.zeros((8, PHI), np.float32)
    rows[0, 0] = 1.0
    rows[1, : 1 + FEAT] = 1.0
    rows[2, 0] = 1.0
    rows[2, 1 : 1 + FEAT] = FEAT ** (-0.25)
    for i, (a, b) in enumerate(pairs):
        rows[2, 1 + FEAT + i] = (1.0 if a == b else 2.0**0.5) * (2.0 * FEAT) ** (-0.5)
    move = np.zeros((4, QK, QK), np.float32)
    for kind in range(2):
        for head in range(LOCAL_HEADS):
            base = kind * LOCAL_HEADS * FEAT + head * FEAT
            other = (1 - kind) * LOCAL_HEADS * FEAT + head * FEAT
            n = kind * LOCAL_HEADS + head
            for a in range(FEAT):
                left[n, base + a, 1 + a] = 1.0
                move[n, base + a, other + a] = FEAT ** (-0.5)
            for i, (a, b) in enumerate(pairs):
                left[n, base + a, 1 + FEAT + i] = 1.0
                right[n, base + b, 1 + FEAT + i] = 1.0
    return (
        jnp.asarray(left, bf16),
        jnp.asarray(right, bf16),
        jnp.asarray(rows, f32),
        jnp.asarray(move, bf16),
    )


def split(a):
    hi = a.astype(bf16)
    return hi, (a - hi.astype(f32)).astype(bf16)


def dot_low(a, b, dims):
    hi, lo = split(a)
    return matmul(hi, b, dims) + matmul(lo, b, dims)


def dot_full(a, b, dims):
    ah, al = split(a)
    bh, bl = split(b)
    return matmul(ah, bh, dims) + (matmul(al, bh, dims) + matmul(ah, bl, dims))


def side(u, left, right, rows):
    return matmul(u, left) + rows[0:1], matmul(u, right) + rows[1:2]


def to_order(idx_ref, src_ref, dst):
    for i in range(8):
        dst[pl.ds(i * CHUNK, CHUNK), :] = src_ref[
            pl.ds(pl.multiple_of(idx_ref[i] * CHUNK, CHUNK), CHUNK), :
        ]


def from_order(idx_ref, i, dst_ref, block):
    dst_ref[pl.ds(pl.multiple_of(idx_ref[i] * CHUNK, CHUNK), CHUNK), :] = block


def state_rows(ref, head):
    base = head * HEAD_ROWS
    mat = jnp.concatenate(
        [ref[base : base + PHI_ROWS, :], jnp.zeros((PHI - PHI_ROWS, DV), f32)], axis=0
    )
    vec = jnp.concatenate(
        [ref[base + PHI_ROWS : base + PHI_ROWS + 1, :], ref[base + PHI_ROWS + 1 : base + PHI_ROWS + 2, :]],
        axis=1,
    )
    return mat, vec


def store_state(ref, head, mat, vec):
    base = head * HEAD_ROWS
    ref[base : base + PHI_ROWS, :] = mat[:PHI_ROWS]
    tail = jnp.concatenate(
        [vec[:, :DV], vec[:, DV:], jnp.zeros((HEAD_ROWS - PHI_ROWS - 2, DV), f32)], axis=0
    )
    ref[base + PHI_ROWS : base + HEAD_ROWS, :] = tail


def key_state_kernel(idx_ref, p_ref, masks_ref, left_ref, right_ref, rows_ref, out_ref, scr):
    to_order(idx_ref, p_ref, scr)
    in_last = masks_ref[:, 0:1]
    rows = rows_ref[...]
    for head in range(LOCAL_HEADS):
        n = LOCAL_HEADS + head
        mat = jnp.zeros((PHI, DV), f32)
        vec = jnp.zeros((1, PHI), f32)
        for r in range(0, ROWS, TILE):
            u = scr[r : r + TILE, VW:PW]
            v = scr[r : r + TILE, head * DV : (head + 1) * DV]
            one, two = side(u, left_ref[n], right_ref[n], rows)
            phi = one * two * rows[2:3] * in_last[r : r + TILE]
            mat = mat + dot_low(phi, v, ((0,), (0,)))
            vec = vec + jnp.sum(phi, axis=0, keepdims=True)
        store_state(out_ref, head, mat, vec)


def attend_kernel(
    idx_ref, p_ref, masks_ref, doc_row_ref, state_ref, left_ref, right_ref, rows_ref, move_ref,
    att_ref, den_ref, low_ref, scr,
):
    to_order(idx_ref, p_ref, scr)
    rows = rows_ref[...]
    u_all = scr[:, VW:PW]
    for head in range(LOCAL_HEADS):
        mat, vec = state_rows(state_ref, head)
        v_all = scr[:, head * DV : (head + 1) * DV]
        for r in range(0, ROWS, TILE):
            end = r + TILE
            u = scr[r:end, VW:PW]
            cont = masks_ref[r:end, 1:2]
            doc_col = masks_ref[r:end, 2:3]
            one, two = side(u, left_ref[head], right_ref[head], rows)
            phi = one * two * rows[2:3]
            num = cont * dot_full(phi, mat, ((1,), (0,)))
            den = cont * jnp.sum(phi * vec, axis=1, keepdims=True)
            moved = matmul(u, move_ref[head]).astype(bf16)
            s = matmul(moved, u_all[:end], ((1,), (1,)))
            at = r + lax.broadcasted_iota(jnp.int32, (TILE, end), 0)
            of = lax.broadcasted_iota(jnp.int32, (TILE, end), 1)
            allowed = (of <= at) & (doc_col == doc_row_ref[:, :end])
            kern = jnp.where(allowed, 1.0 + s + 0.5 * s * s, 0.0)
            num = num + matmul(kern.astype(bf16), v_all[:end])
            den = den + jnp.sum(kern, axis=1, keepdims=True)
            att = num / den
            att_ref[r:end, head * DV : (head + 1) * DV] = att
            den_ref[r:end, head : head + 1] = den
    for i in range(8):
        from_order(idx_ref, i, low_ref, att_ref[i * CHUNK : (i + 1) * CHUNK, :].astype(bf16))


def query_state_kernel(
    idx_ref, p_ref, ga_ref, masks_ref, att_ref, den_ref, left_ref, right_ref, rows_ref,
    out_ref, gn_ref, gd_ref, scr, gscr,
):
    to_order(idx_ref, p_ref, scr)
    to_order(idx_ref, ga_ref, gscr)
    rows = rows_ref[...]
    for head in range(LOCAL_HEADS):
        mat = jnp.zeros((PHI, DV), f32)
        vec = jnp.zeros((1, PHI), f32)
        cols = slice(head * DV, (head + 1) * DV)
        for r in range(0, ROWS, TILE):
            end = r + TILE
            den = den_ref[r:end, head : head + 1]
            ga = gscr[r:end, cols].astype(f32)
            gn = ga / den
            gd = -jnp.sum(ga * att_ref[r:end, cols], axis=1, keepdims=True) / den
            gn_ref[r:end, cols] = gn
            gd_ref[r:end, head : head + 1] = gd
            one, two = side(scr[r:end, VW:PW], left_ref[head], right_ref[head], rows)
            phi = one * two * rows[2:3] * masks_ref[r:end, 1:2]
            mat = mat + dot_full(phi, gn, ((0,), (0,)))
            vec = vec + jnp.sum(phi * gd, axis=0, keepdims=True)
        store_state(out_ref, head, mat, vec)


def attend_back_kernel(
    idx_ref, p_ref, gn_ref, gd_ref, masks_ref, doc_row_ref, state_ref, grad_state_ref,
    left_ref, right_ref, rows_ref, move_ref, out_ref, scr, gqk, gv,
):
    to_order(idx_ref, p_ref, scr)
    rows = rows_ref[...]
    u_all = scr[:, VW:PW]
    for head in range(LOCAL_HEADS):
        key = LOCAL_HEADS + head
        cols = slice(head * DV, (head + 1) * DV)
        mat, vec = state_rows(state_ref, head)
        gmat, gvec = state_rows(grad_state_ref, head)
        v_all = scr[:, cols]
        back_all = matmul(u_all, move_ref[key]).astype(bf16)
        for r in range(0, ROWS, TILE):
            end = r + TILE
            u = scr[r:end, VW:PW]
            cont = masks_ref[r:end, 1:2]
            in_last = masks_ref[r:end, 0:1]
            gn = gn_ref[r:end, cols]
            gd = gd_ref[r:end, head : head + 1]
            one, two = side(u, left_ref[head], right_ref[head], rows)
            grad = (dot_full(gn, mat, ((1,), (1,))) + gd * vec) * cont * rows[2:3]
            acc = dot_low(grad * two, left_ref[head], ((1,), (1,)))
            acc = acc + dot_low(grad * one, right_ref[head], ((1,), (1,)))
            one, two = side(u, left_ref[key], right_ref[key], rows)
            grad = (dot_low_right(v_all[r:end], gmat) + gvec) * in_last * rows[2:3]
            acc = acc + dot_low(grad * two, left_ref[key], ((1,), (1,)))
            acc = acc + dot_low(grad * one, right_ref[key], ((1,), (1,)))
            phi = one * two * rows[2:3] * in_last
            if head == 0:
                gqk[r:end, :] = acc
            else:
                gqk[r:end, :] = gqk[r:end, :] + acc
            gv[r:end, cols] = dot_full(phi, gmat, ((1,), (0,)))
        for r in range(0, ROWS, TILE):
            end = r + TILE
            u = scr[r:end, VW:PW]
            doc_col = masks_ref[r:end, 2:3]
            low_gn = gn_ref[r:end, cols].astype(bf16)
            gd = gd_ref[r:end, head : head + 1]
            moved = matmul(u, move_ref[head]).astype(bf16)
            s = matmul(moved, u_all[:end], ((1,), (1,)))
            at = r + lax.broadcasted_iota(jnp.int32, (TILE, end), 0)
            of = lax.broadcasted_iota(jnp.int32, (TILE, end), 1)
            allowed = (of <= at) & (doc_col == doc_row_ref[:, :end])
            kern = jnp.where(allowed, 1.0 + s + 0.5 * s * s, 0.0).astype(bf16)
            gk = matmul(low_gn, v_all[:end], ((1,), (1,))) + gd
            gs = jnp.where(allowed, gk * (1.0 + s), 0.0).astype(bf16)
            gqk[r:end, :] = gqk[r:end, :] + matmul(gs, back_all[:end])
            gqk[:end, :] = gqk[:end, :] + matmul(gs, moved, ((0,), (0,)))
            gv[:end, cols] = gv[:end, cols] + matmul(kern, low_gn, ((0,), (0,)))
    for i in range(8):
        chunk = slice(i * CHUNK, (i + 1) * CHUNK)
        from_order(
            idx_ref, i, out_ref,
            jnp.concatenate([gv[chunk, :], gqk[chunk, :]], axis=1).astype(bf16),
        )


def dot_low_right(a, b):
    hi, lo = split(b)
    return matmul(a, hi, ((1,), (1,))) + matmul(a, lo, ((1,), (1,)))


def call(kernel, outs, scratch, n_in):
    return pl.pallas_call(
        kernel,
        out_shape=outs,
        in_specs=[pl.BlockSpec(memory_space=pltpu.SMEM)]
        + [pl.BlockSpec(memory_space=pltpu.VMEM)] * (n_in - 1),
        out_specs=[pl.BlockSpec(memory_space=pltpu.VMEM)] * len(outs),
        scratch_shapes=scratch,
        compiler_params=pltpu.CompilerParams(vmem_limit_bytes=48 * 1024 * 1024),
    )


def adam_step(weight, moment_one, moment_two, reduced, step_rate):
    new_one = beta_one * moment_one + (1.0 - beta_one) * reduced
    new_two = beta_two * moment_two + (1.0 - beta_two) * reduced * reduced
    corrected_one = new_one / (1.0 - beta_one**STEP)
    corrected_two = new_two / (1.0 - beta_two**STEP)
    master = weight - step_rate * (
        corrected_one / (jnp.sqrt(corrected_two) + adam_eps) + weight_decay * weight
    )
    return (new_one, new_two, master)


def unit_norm(rows):
    inv = lax.rsqrt(jnp.mean(rows * rows, axis=-1, keepdims=True) + norm_eps)
    return rows * inv, inv


def unit_norm_back(shaped, unit, inv):
    return inv * (shaped - unit * jnp.mean(shaped * unit, axis=-1, keepdims=True))


def exchange(a):
    return lax.all_to_all(a, GROUPS, 0, 0)


def pad_cols(a, width):
    return jnp.pad(a, ((0, 0), (0, width - a.shape[1])))


def shards(
    tokens, cotangent, row_lengths, gains, gain_first, gain_second,
    feature_weight, feature_first, feature_second,
    value_weight, value_first, value_second,
    output_weight, output_first, output_second,
    gateup_weight, gateup_first, gateup_second,
    down_weight, down_first, down_second,
):
    core = lax.axis_index("core")
    y = lax.axis_index("y")
    group = (lax.axis_index("x_lo") * 4 + lax.axis_index("z")) * 2 + lax.axis_index("x_hi")
    gain_low = gains.astype(bf16).astype(f32)

    value_low = value_weight.astype(bf16)
    feature_low = feature_weight.reshape(128, QK).astype(bf16)
    gate_low = gateup_weight[:, 0].astype(bf16)
    up_low = gateup_weight[:, 1].astype(bf16)
    scale_one = gain_low[0][:, None]
    scale_two = gain_low[1][:, None]
    first_part = (jnp.concatenate([value_low, feature_low], axis=1).astype(f32) * scale_one).astype(bf16)
    second_part = jnp.concatenate(
        [
            output_weight.astype(bf16).T,
            pad_cols((gate_low.astype(f32) * scale_two).astype(bf16), FFP),
            pad_cols((up_low.astype(f32) * scale_two).astype(bf16), FFP),
        ],
        axis=1,
    )
    third_part = pad_cols(down_weight.astype(bf16).T, FFP)

    tokens = cross(tokens)
    first_part = cross(first_part)
    second_part = cross(second_part)
    third_part = cross(third_part)
    cot = cross(cotangent)

    inputs = tokens.astype(f32)
    unit_one, inv_one = unit_norm(inputs)
    acts_one = gather_rows(unit_one.astype(bf16))
    proj_w = exchange(jnp.broadcast_to(first_part[None], (N_GROUPS, CHUNK, PW))).reshape(D, PW)
    wide_w = lax.all_gather(second_part, GROUPS, axis=0, tiled=True)
    down_w = lax.all_gather(third_part, GROUPS, axis=0, tiled=True)
    out_w = wide_w[:, :VW]
    gateup_w = wide_w[:, VW:]
    grad_mlp = gather_rows(cot)

    ends = jnp.cumsum(row_lengths)

    def doc_of(pos):
        return jnp.sum((pos[..., None] >= ends).astype(jnp.int32), axis=-1)

    positions = group * ROWS + jnp.arange(ROWS, dtype=jnp.int32)
    docs = doc_of(positions)
    group_ids = jnp.arange(N_GROUPS, dtype=jnp.int32)
    doc_end = doc_of(group_ids * ROWS + (ROWS - 1))
    doc_before = jnp.where(group_ids > 0, doc_of(group_ids * ROWS - 1), -1)
    last_doc = docs[ROWS - 1]
    before = jnp.where(group > 0, doc_of(group * ROWS - 1), -1)
    masks = jnp.stack(
        [
            (docs == last_doc).astype(f32),
            (docs == before).astype(f32),
            docs.astype(f32),
        ],
        axis=1,
    )
    doc_row = docs.astype(f32)[None]
    carry = ((group_ids[None, :] < group_ids[:, None]) & (doc_end[None, :] == doc_before[:, None])).astype(f32)
    back = ((group_ids[None, :] > group_ids[:, None]) & (doc_before[None, :] == doc_end[:, None])).astype(f32)
    chunk_ids = jnp.arange(8, dtype=jnp.int32)
    idx = ((chunk_ids % 2) ^ core) * 4 + (chunk_ids // 2 - y) % 4

    left, right, rows, move = feature_tables()
    proj = matmul(acts_one, proj_w).astype(bf16)
    own_state = call(
        key_state_kernel,
        [jax.ShapeDtypeStruct((STATE_ROWS, DV), f32)],
        [pltpu.VMEM((ROWS, PW), bf16)],
        6,
    )(idx, proj, masks, left, right, rows)[0]
    slices = exchange(own_state.reshape(N_GROUPS, STATE_ROWS // N_GROUPS, DV))
    slices = jnp.sum(carry[:, :, None, None] * slices[None], axis=1)
    state = exchange(slices).reshape(STATE_ROWS, DV)
    att, den, attn_rows = call(
        attend_kernel,
        [
            jax.ShapeDtypeStruct((ROWS, VW), f32),
            jax.ShapeDtypeStruct((ROWS, LOCAL_HEADS), f32),
            jax.ShapeDtypeStruct((ROWS, VW), bf16),
        ],
        [pltpu.VMEM((ROWS, PW), bf16)],
        9,
    )(idx, proj, masks, doc_row, state, left, right, rows, move)
    half = ROWS // 2

    def of_half(a, h):
        return a[h * half : (h + 1) * half]

    middle = inputs + scatter_rows(
        lambda h: matmul(of_half(attn_rows, h), out_w, ((1,), (1,)))
    )
    unit_two, inv_two = unit_norm(middle)
    acts_two = gather_rows(unit_two.astype(bf16))
    gate_up = matmul(acts_two, gateup_w)
    grad_hidden = matmul(grad_mlp, down_w)
    gate = gate_up[:, :FFP]
    up = gate_up[:, FFP:]
    sigmoid = jax.nn.sigmoid(gate)
    silu = gate * sigmoid
    hidden = (silu * up).astype(bf16)
    dsilu = sigmoid * (1.0 + gate * (1.0 - sigmoid))
    grad_gate_up = jnp.concatenate([grad_hidden * up * dsilu, grad_hidden * silu], axis=1).astype(bf16)

    shaped_two = scatter_rows(lambda h: matmul(of_half(grad_gate_up, h), gateup_w, ((1,), (1,))))
    grad_out = cot.astype(f32)
    grad_mid = grad_out + unit_norm_back(shaped_two, unit_two, inv_two)
    grad_attn = gather_rows(grad_mid.astype(bf16))

    gateup_grad = matmul(acts_two, grad_gate_up, ((0,), (0,))).astype(bf16)
    down_grad = matmul(grad_mlp, hidden, ((0,), (0,))).astype(bf16)
    mlp_grad = lax.psum_scatter(
        jnp.concatenate([gateup_grad, down_grad], axis=1), GROUPS, scatter_dimension=0, tiled=True
    )
    mixed = middle + scatter_rows(lambda h: matmul(of_half(hidden, h), down_w, ((1,), (1,))))
    mixed = cross(mixed.astype(bf16))

    grad_low = matmul(grad_attn, out_w).astype(bf16)
    own_grad, gn, gd = call(
        query_state_kernel,
        [
            jax.ShapeDtypeStruct((STATE_ROWS, DV), f32),
            jax.ShapeDtypeStruct((ROWS, VW), f32),
            jax.ShapeDtypeStruct((ROWS, LOCAL_HEADS), f32),
        ],
        [pltpu.VMEM((ROWS, PW), bf16), pltpu.VMEM((ROWS, VW), bf16)],
        9,
    )(idx, proj, grad_low, masks, att, den, left, right, rows)
    den_part = jnp.sum(jnp.abs(den))
    slices = exchange(
        jnp.concatenate(
            [
                own_grad.reshape(N_GROUPS, STATE_ROWS // N_GROUPS, DV),
                jnp.full((N_GROUPS, 8, DV), den_part, f32),
            ],
            axis=1,
        )
    )
    den_group = jnp.sum(slices[:, STATE_ROWS // N_GROUPS :], axis=0)
    slices = jnp.sum(back[:, :, None, None] * slices[None, :, : STATE_ROWS // N_GROUPS], axis=1)
    grad_state = exchange(slices).reshape(STATE_ROWS, DV)
    grad_proj = call(
        attend_back_kernel,
        [jax.ShapeDtypeStruct((ROWS, PW), bf16)],
        [pltpu.VMEM((ROWS, PW), bf16), pltpu.VMEM((ROWS, QK), f32), pltpu.VMEM((ROWS, VW), f32)],
        12,
    )(idx, proj, gn, gd, masks, doc_row, state, grad_state, left, right, rows, move)[0]

    shaped_one = scatter_rows(lambda h: matmul(of_half(grad_proj, h), proj_w, ((1,), (1,))))
    grad_tokens = grad_mid + unit_norm_back(shaped_one, unit_one, inv_one)
    grad_tokens = cross(grad_tokens.astype(bf16)).astype(f32)

    output_grad = matmul(grad_attn, attn_rows, ((0,), (0,))).astype(bf16)
    proj_grad = matmul(acts_one, grad_proj, ((0,), (0,))).astype(bf16)
    attn_grad = exchange(
        jnp.concatenate([output_grad, proj_grad], axis=1).reshape(N_GROUPS, CHUNK, VW + PW)
    )
    attn_grad = cross(jnp.sum(attn_grad.astype(f32), axis=0).astype(bf16)).astype(f32)
    mlp_grad = cross(mlp_grad).astype(f32)
    den_group = cross(den_group)

    output_sum = attn_grad[:, :VW].T
    unit_value = attn_grad[:, VW : 2 * VW]
    unit_feature = attn_grad[:, 2 * VW :]
    unit_gate = mlp_grad[:, :FFL]
    unit_up = mlp_grad[:, FFP : FFP + FFL]
    down_sum = mlp_grad[:, 2 * FFP : 2 * FFP + FFL].T
    gain_one = jnp.sum(unit_value * value_low.astype(f32), axis=1) + jnp.sum(
        unit_feature * feature_low.astype(f32), axis=1
    )
    gain_two = jnp.sum(unit_gate * gate_low.astype(f32), axis=1) + jnp.sum(
        unit_up * up_low.astype(f32), axis=1
    )
    small = jnp.concatenate([gain_one[None], gain_two[None], den_group[:6]], axis=0)
    small = jnp.sum(
        lax.all_to_all(jnp.broadcast_to(small[None], (8, 8, CHUNK)), ("y", "x_hi"), 0, 0), axis=0
    )
    gain_total = small[:2]
    den_mean = small[2, 0] / (N_GROUPS * ROWS * HEADS)
    value_sum = unit_value * scale_one
    feature_sum = (unit_feature * scale_one).reshape(CHUNK, 2, QK // 2)
    gateup_sum = jnp.stack([unit_gate * scale_two, unit_up * scale_two], axis=1)
    news = [
        adam_step(gains, gain_first, gain_second, gain_total, gain_rate),
        adam_step(feature_weight, feature_first, feature_second, feature_sum, D ** (-0.5)),
        adam_step(value_weight, value_first, value_second, value_sum, D ** (-0.5)),
        adam_step(
            output_weight, output_first, output_second, output_sum, (HEADS * DV // 64) ** (-0.5)
        ),
        adam_step(gateup_weight, gateup_first, gateup_second, gateup_sum, D ** (-0.5)),
        adam_step(down_weight, down_first, down_second, down_sum, FF ** (-0.5)),
    ]
    return (mixed, grad_tokens, den_mean) + tuple(a for new in news for a in new)


def solution(mesh):
    fine = jax.sharding.Mesh(mesh.devices.reshape(2, 4, 2, 4, 2), FINE)
    dp = ("x_lo", "z", "core")
    tensor = ("y", "x_hi")
    rows = P(FINE, None)
    gain = P(None, dp)
    deep = P(dp, None, tensor)
    down = P(dp, tensor)
    across = P(tensor, dp)
    return jax.shard_map(
        shards,
        mesh=fine,
        in_specs=(rows, rows, P())
        + (gain,) * 3
        + (deep,) * 3
        + (down,) * 3
        + (across,) * 3
        + (deep,) * 3
        + (across,) * 3,
        out_specs=(rows, rows, P())
        + (gain,) * 3
        + (deep,) * 3
        + (down,) * 3
        + (across,) * 3
        + (deep,) * 3
        + (across,) * 3,
        check_vma=False,
    )
```

```python
import functools

import jax
import jax.numpy as jnp
import numpy as np
from jax import lax
from jax.experimental import pallas as pl
from jax.experimental.pallas import tpu as pltpu
from jax.sharding import PartitionSpec as P

D = 2048
HEADS = 16
FEAT = 16
DV = 128
FF = 5504
STEP = 10
FINE = ("x_lo", "z", "core", "y", "x_hi")
GROUPS = ("x_hi", "x_lo", "z")
N_GROUPS = 16
ROWS = 1024
CHUNK = 128
HALF = ROWS // 2
LOCAL_HEADS = 2
QK = 2 * LOCAL_HEADS * FEAT
VW = LOCAL_HEADS * DV
PW = VW + QK
FFL = 688
FFP = 768
AW = 640
PHI = 256
PHI_ROWS = 160
HEAD_ROWS = 192
STATE_ROWS = LOCAL_HEADS * HEAD_ROWS
TILE = 256

norm_eps = 1e-05
beta_one = 0.5
beta_two = 0.5
adam_eps = 1e-08
weight_decay = 0.01
gain_rate = 0.5

f32 = jnp.float32
bf16 = jnp.bfloat16


FLIP = [(0, 1), (1, 0)]
CROSS = [(0, 0), (1, 2), (2, 1), (3, 3)]


def cross(a):
    return lax.ppermute(a, ("core", "x_hi"), CROSS)


def swap_core(a):
    return lax.ppermute(a, "core", FLIP)


def over_y(a):
    return lax.all_to_all(a, "y", 0, 0)


def spread(mine):
    return jnp.broadcast_to(mine[None], (4,) + mine.shape)


def to_y(a, step):
    return lax.ppermute(a, "y", [(i, (i + step) % 4) for i in range(4)])


def gather_rows(mine):
    own = over_y(spread(mine)).reshape(HALF, -1)
    return own, swap_core(own)


def gather_rows_apart(mine):
    y = lax.axis_index("y")
    own = jnp.zeros((HALF, D), mine.dtype)
    for step in range(4):
        piece = to_y(mine, step) if step else mine
        own = lax.dynamic_update_slice(own, piece, ((y - step) % 4 * CHUNK, 0))
    return own, swap_core(own)


def sum_rows(low):
    return jnp.sum(over_y(low.reshape(4, CHUNK, D)).astype(f32), axis=0)


def sum_rows_apart(low):
    y = lax.axis_index("y")

    def part(step):
        return lax.dynamic_slice(low, ((y + step) % 4 * CHUNK, 0), (CHUNK, D))

    parts = [to_y(part(step), step) for step in (1, 2, 3)]
    out = part(0).astype(f32)
    for a in parts:
        out = out + a.astype(f32)
    return out


def scatter_rows(partial, between=None, total=sum_rows):
    send = partial(1, None)
    got = swap_core(send)
    low = partial(0, got)
    if between is not None:
        between(send, low)
    return total(low)


def rows_of(halves, weight, dims):
    def partial(half, more):
        total = matmul(halves[half], weight, dims)
        if more is not None:
            total = total + more.astype(f32)
        return total.astype(bf16)

    return partial


def halves_of(a):
    return a[:HALF], a[HALF:]


def matmul(a, b, dims=((1,), (0,))):
    return lax.dot_general(a, b, (dims, ((), ())), preferred_element_type=f32)


def feature_tables():
    pairs = [(a, b) for a in range(FEAT) for b in range(a, FEAT)]
    left = np.zeros((4, QK, PHI), np.float32)
    right = np.zeros((4, QK, PHI), np.float32)
    rows = np.zeros((8, PHI), np.float32)
    rows[0, 0] = 1.0
    rows[1, : 1 + FEAT] = 1.0
    rows[2, 0] = 1.0
    rows[2, 1 : 1 + FEAT] = FEAT ** (-0.25)
    for i, (a, b) in enumerate(pairs):
        rows[2, 1 + FEAT + i] = (1.0 if a == b else 2.0**0.5) * (2.0 * FEAT) ** (-0.5)
    move = np.zeros((4, QK, QK), np.float32)
    for kind in range(2):
        for head in range(LOCAL_HEADS):
            base = kind * LOCAL_HEADS * FEAT + head * FEAT
            other = (1 - kind) * LOCAL_HEADS * FEAT + head * FEAT
            n = kind * LOCAL_HEADS + head
            for a in range(FEAT):
                left[n, base + a, 1 + a] = 1.0
                move[n, base + a, other + a] = FEAT ** (-0.5)
            for i, (a, b) in enumerate(pairs):
                left[n, base + a, 1 + FEAT + i] = 1.0
                right[n, base + b, 1 + FEAT + i] = 1.0
    return (
        jnp.asarray(left, bf16),
        jnp.asarray(right, bf16),
        jnp.asarray(rows, f32),
        jnp.asarray(move, bf16),
    )


def split(a):
    hi = a.astype(bf16)
    return hi, (a - hi.astype(f32)).astype(bf16)


def dot_low(a, b, dims):
    hi, lo = split(a)
    return matmul(hi, b, dims) + matmul(lo, b, dims)


def dot_full(a, b, dims):
    ah, al = split(a)
    bh, bl = split(b)
    return matmul(ah, bh, dims) + (matmul(al, bh, dims) + matmul(ah, bl, dims))


def side(u, left, right, rows):
    return matmul(u, left) + rows[0:1], matmul(u, right) + rows[1:2]


def to_order(idx_ref, src_ref, dst):
    for i in range(8):
        dst[pl.ds(i * CHUNK, CHUNK), :] = src_ref[
            pl.ds(pl.multiple_of(idx_ref[i] * CHUNK, CHUNK), CHUNK), :
        ]


def from_order(idx_ref, i, dst_ref, block):
    dst_ref[pl.ds(pl.multiple_of(idx_ref[i] * CHUNK, CHUNK), CHUNK), :] = block


def state_rows(ref, head):
    base = head * HEAD_ROWS
    mat = jnp.concatenate(
        [ref[base : base + PHI_ROWS, :], jnp.zeros((PHI - PHI_ROWS, DV), f32)], axis=0
    )
    vec = jnp.concatenate(
        [ref[base + PHI_ROWS : base + PHI_ROWS + 1, :], ref[base + PHI_ROWS + 1 : base + PHI_ROWS + 2, :]],
        axis=1,
    )
    return mat, vec


def store_state(ref, head, mat, vec):
    base = head * HEAD_ROWS
    ref[base : base + PHI_ROWS, :] = mat[:PHI_ROWS]
    tail = jnp.concatenate(
        [vec[:, :DV], vec[:, DV:], jnp.zeros((HEAD_ROWS - PHI_ROWS - 2, DV), f32)], axis=0
    )
    ref[base + PHI_ROWS : base + HEAD_ROWS, :] = tail


def key_state_kernel(idx_ref, p_ref, masks_ref, left_ref, right_ref, rows_ref, out_ref, scr):
    to_order(idx_ref, p_ref, scr)
    in_last = masks_ref[:, 0:1]
    rows = rows_ref[...]
    for head in range(LOCAL_HEADS):
        n = LOCAL_HEADS + head
        mat = jnp.zeros((PHI, DV), f32)
        vec = jnp.zeros((1, PHI), f32)
        for r in range(0, ROWS, TILE):
            u = scr[r : r + TILE, VW:PW]
            v = scr[r : r + TILE, head * DV : (head + 1) * DV]
            one, two = side(u, left_ref[n], right_ref[n], rows)
            phi = one * two * rows[2:3] * in_last[r : r + TILE]
            mat = mat + dot_low(phi, v, ((0,), (0,)))
            vec = vec + jnp.sum(phi, axis=0, keepdims=True)
        store_state(out_ref, head, mat, vec)


def attend_kernel(
    idx_ref, p_ref, masks_ref, doc_row_ref, state_ref, left_ref, right_ref, rows_ref, move_ref,
    att_ref, den_ref, low_ref, scr,
):
    to_order(idx_ref, p_ref, scr)
    rows = rows_ref[...]
    u_all = scr[:, VW:PW]
    for head in range(LOCAL_HEADS):
        mat, vec = state_rows(state_ref, head)
        v_all = scr[:, head * DV : (head + 1) * DV]
        for r in range(0, ROWS, TILE):
            end = r + TILE
            u = scr[r:end, VW:PW]
            cont = masks_ref[r:end, 1:2]
            doc_col = masks_ref[r:end, 2:3]
            one, two = side(u, left_ref[head], right_ref[head], rows)
            phi = one * two * rows[2:3]
            num = cont * dot_full(phi, mat, ((1,), (0,)))
            den = cont * jnp.sum(phi * vec, axis=1, keepdims=True)
            moved = matmul(u, move_ref[head]).astype(bf16)
            s = matmul(moved, u_all[:end], ((1,), (1,)))
            at = r + lax.broadcasted_iota(jnp.int32, (TILE, end), 0)
            of = lax.broadcasted_iota(jnp.int32, (TILE, end), 1)
            allowed = (of <= at) & (doc_col == doc_row_ref[:, :end])
            kern = jnp.where(allowed, 1.0 + s + 0.5 * s * s, 0.0)
            num = num + matmul(kern.astype(bf16), v_all[:end])
            den = den + jnp.sum(kern, axis=1, keepdims=True)
            att = num / den
            att_ref[r:end, head * DV : (head + 1) * DV] = att
            den_ref[r:end, head : head + 1] = den
    for i in range(8):
        from_order(idx_ref, i, low_ref, att_ref[i * CHUNK : (i + 1) * CHUNK, :].astype(bf16))


def query_state_kernel(
    idx_ref, p_ref, ga_ref, masks_ref, att_ref, den_ref, left_ref, right_ref, rows_ref,
    out_ref, gn_ref, gd_ref, scr, gscr,
):
    to_order(idx_ref, p_ref, scr)
    to_order(idx_ref, ga_ref, gscr)
    rows = rows_ref[...]
    for head in range(LOCAL_HEADS):
        mat = jnp.zeros((PHI, DV), f32)
        vec = jnp.zeros((1, PHI), f32)
        cols = slice(head * DV, (head + 1) * DV)
        for r in range(0, ROWS, TILE):
            end = r + TILE
            den = den_ref[r:end, head : head + 1]
            ga = gscr[r:end, cols].astype(f32)
            gn = ga / den
            gd = -jnp.sum(ga * att_ref[r:end, cols], axis=1, keepdims=True) / den
            gn_ref[r:end, cols] = gn
            gd_ref[r:end, head : head + 1] = gd
            one, two = side(scr[r:end, VW:PW], left_ref[head], right_ref[head], rows)
            phi = one * two * rows[2:3] * masks_ref[r:end, 1:2]
            mat = mat + dot_full(phi, gn, ((0,), (0,)))
            vec = vec + jnp.sum(phi * gd, axis=0, keepdims=True)
        store_state(out_ref, head, mat, vec)


def attend_back_kernel(
    idx_ref, p_ref, gn_ref, gd_ref, masks_ref, doc_row_ref, state_ref, grad_state_ref,
    left_ref, right_ref, rows_ref, move_ref, out_ref, scr, gqk, gv,
):
    to_order(idx_ref, p_ref, scr)
    rows = rows_ref[...]
    u_all = scr[:, VW:PW]
    for head in range(LOCAL_HEADS):
        key = LOCAL_HEADS + head
        cols = slice(head * DV, (head + 1) * DV)
        mat, vec = state_rows(state_ref, head)
        gmat, gvec = state_rows(grad_state_ref, head)
        v_all = scr[:, cols]
        back_all = matmul(u_all, move_ref[key]).astype(bf16)
        for r in range(0, ROWS, TILE):
            end = r + TILE
            u = scr[r:end, VW:PW]
            cont = masks_ref[r:end, 1:2]
            in_last = masks_ref[r:end, 0:1]
            gn = gn_ref[r:end, cols]
            gd = gd_ref[r:end, head : head + 1]
            one, two = side(u, left_ref[head], right_ref[head], rows)
            grad = (dot_full(gn, mat, ((1,), (1,))) + gd * vec) * cont * rows[2:3]
            acc = dot_low(grad * two, left_ref[head], ((1,), (1,)))
            acc = acc + dot_low(grad * one, right_ref[head], ((1,), (1,)))
            one, two = side(u, left_ref[key], right_ref[key], rows)
            grad = (dot_low_right(v_all[r:end], gmat) + gvec) * in_last * rows[2:3]
            acc = acc + dot_low(grad * two, left_ref[key], ((1,), (1,)))
            acc = acc + dot_low(grad * one, right_ref[key], ((1,), (1,)))
            phi = one * two * rows[2:3] * in_last
            if head == 0:
                gqk[r:end, :] = acc
            else:
                gqk[r:end, :] = gqk[r:end, :] + acc
            gv[r:end, cols] = dot_full(phi, gmat, ((1,), (0,)))
        for r in range(0, ROWS, TILE):
            end = r + TILE
            u = scr[r:end, VW:PW]
            doc_col = masks_ref[r:end, 2:3]
            low_gn = gn_ref[r:end, cols].astype(bf16)
            gd = gd_ref[r:end, head : head + 1]
            moved = matmul(u, move_ref[head]).astype(bf16)
            s = matmul(moved, u_all[:end], ((1,), (1,)))
            at = r + lax.broadcasted_iota(jnp.int32, (TILE, end), 0)
            of = lax.broadcasted_iota(jnp.int32, (TILE, end), 1)
            allowed = (of <= at) & (doc_col == doc_row_ref[:, :end])
            kern = jnp.where(allowed, 1.0 + s + 0.5 * s * s, 0.0).astype(bf16)
            gk = matmul(low_gn, v_all[:end], ((1,), (1,))) + gd
            gs = jnp.where(allowed, gk * (1.0 + s), 0.0).astype(bf16)
            gqk[r:end, :] = gqk[r:end, :] + matmul(gs, back_all[:end])
            gqk[:end, :] = gqk[:end, :] + matmul(gs, moved, ((0,), (0,)))
            gv[:end, cols] = gv[:end, cols] + matmul(kern, low_gn, ((0,), (0,)))
    for i in range(8):
        chunk = slice(i * CHUNK, (i + 1) * CHUNK)
        from_order(
            idx_ref, i, out_ref,
            jnp.concatenate([gv[chunk, :], gqk[chunk, :]], axis=1).astype(bf16),
        )


def dot_low_right(a, b):
    hi, lo = split(b)
    return matmul(a, hi, ((1,), (1,))) + matmul(a, lo, ((1,), (1,)))


def call(kernel, outs, scratch, n_in):
    return pl.pallas_call(
        kernel,
        out_shape=outs,
        in_specs=[pl.BlockSpec(memory_space=pltpu.SMEM)]
        + [pl.BlockSpec(memory_space=pltpu.VMEM)] * (n_in - 1),
        out_specs=[pl.BlockSpec(memory_space=pltpu.VMEM)] * len(outs),
        scratch_shapes=scratch,
        compiler_params=pltpu.CompilerParams(vmem_limit_bytes=48 * 1024 * 1024),
    )


def adam_step(weight, moment_one, moment_two, reduced, step_rate):
    new_one = beta_one * moment_one + (1.0 - beta_one) * reduced
    new_two = beta_two * moment_two + (1.0 - beta_two) * reduced * reduced
    corrected_one = new_one / (1.0 - beta_one**STEP)
    corrected_two = new_two / (1.0 - beta_two**STEP)
    master = weight - step_rate * (
        corrected_one / (jnp.sqrt(corrected_two) + adam_eps) + weight_decay * weight
    )
    return (new_one, new_two, master)


def nothing_kernel(other_ref, a_ref, out_ref):
    pass


def after(a, other):
    return pl.pallas_call(
        nothing_kernel,
        out_shape=jax.ShapeDtypeStruct(a.shape, a.dtype),
        in_specs=[pl.BlockSpec(memory_space=pl.ANY)] * 2,
        out_specs=pl.BlockSpec(memory_space=pl.ANY),
        input_output_aliases={1: 0},
    )(other, a)


def feature_blocks(forward):
    order = [(k % 8) * 2 + k // 8 for k in range(N_GROUPS)]
    return order if forward else [order.index(k) for k in range(N_GROUPS)]


def reorder_kernel(blocks, *refs):
    n = len(refs) // 2
    for src, dst in zip(refs[:n], refs[n:]):
        for to, of in enumerate(blocks):
            dst[:, to * CHUNK : (to + 1) * CHUNK] = src[:, of * CHUNK : (of + 1) * CHUNK].astype(dst.dtype)


def reorder(blocks, arrays, dtype):
    return pl.pallas_call(
        functools.partial(reorder_kernel, blocks),
        out_shape=[jax.ShapeDtypeStruct(a.shape, dtype) for a in arrays],
    )(*arrays)


def to_group_order(*arrays):
    return reorder(feature_blocks(True), arrays, bf16)


def from_group_order(rows, dtype):
    return reorder(feature_blocks(False), (rows,), dtype)[0]


def pack_first_kernel(value_ref, feature_ref, output_ref, gain_row_ref, gain_col_ref, out_ref):
    def low(a):
        return a.astype(bf16).astype(f32)

    out_ref[:, :VW] = low(output_ref[...]).T.astype(bf16)
    out_ref[:, VW : 2 * VW] = (low(value_ref[...]) * gain_col_ref[:, 0:1]).astype(bf16)
    out_ref[:, 2 * VW : VW + PW] = (low(feature_ref[...]) * gain_row_ref[0:1]).T.astype(bf16)
    out_ref[:, VW + PW :] = jnp.zeros((CHUNK, AW - VW - PW), bf16)


def pack_mlp_kernel(gateup_ref, down_ref, gain_row_ref, out_ref):
    def low(a):
        return a.astype(bf16).astype(f32)

    def wide(a):
        return jnp.concatenate([a, jnp.zeros((FFP - FFL, CHUNK), f32)], axis=0).T.astype(bf16)

    out_ref[:, :FFP] = wide(low(gateup_ref[0]) * gain_row_ref[1:2])
    out_ref[:, FFP : 2 * FFP] = wide(low(gateup_ref[1]) * gain_row_ref[1:2])
    out_ref[:, 2 * FFP :] = wide(low(down_ref[...]))


def adam_store(weight, first, second, grad, rate, outs, at=()):
    place = at if at else (slice(None), slice(None))
    for ref, new in zip(outs, adam_step(weight[place], first[place], second[place], grad, rate)):
        ref[place] = new


def adam_mlp_kernel(
    grad_ref, gain_row_ref, gw, gf, gs, dw, df, ds, g1, g2, g3, d1, d2, d3
):
    for part in range(2):
        grad = grad_ref[:, part * FFP : (part + 1) * FFP].astype(f32).T[:FFL]
        adam_store(
            gw, gf, gs, grad * gain_row_ref[1:2], D ** (-0.5), (g1, g2, g3),
            (part, slice(None), slice(None)),
        )
    grad = grad_ref[:, 2 * FFP :].astype(f32).T[:FFL]
    adam_store(dw, df, ds, grad, FF ** (-0.5), (d1, d2, d3))


def adam_attn_kernel(
    grad_ref, gain_row_ref, gain_col_ref,
    fw, ff, fs, vw, vf, vs, ow, of, os, f1, f2, f3, v1, v2, v3, o1, o2, o3,
):
    grad = grad_ref[:, VW : 2 * VW].astype(f32) * gain_col_ref[:, 0:1]
    adam_store(vw, vf, vs, grad, D ** (-0.5), (v1, v2, v3))
    grad = grad_ref[:, 2 * VW : VW + PW].astype(f32).T * gain_row_ref[0:1]
    adam_store(fw, ff, fs, grad, D ** (-0.5), (f1, f2, f3))
    grad = grad_ref[:, :VW].astype(f32).T
    adam_store(ow, of, os, grad, (HEADS * DV // 64) ** (-0.5), (o1, o2, o3))


def grad_tile(left, right):
    return sum(matmul(a[...], b, ((0,), (0,))) for a, b in zip(left, right)).astype(bf16)


def mlp_grads_kernel(other_ref, a0, a1, g0, g1, gu0, gu1, h0, h1, out_ref):
    out_ref[:, : 2 * FFP] = grad_tile((a0, a1), (gu0[...], gu1[...]))
    out_ref[:, 2 * FFP :] = grad_tile((g0, g1), (h0[...], h1[...]))


def attn_grads_kernel(other_ref, a0, a1, g0, g1, proj_ref, rows_ref, out_ref):
    one = grad_tile((g0, g1), (rows_ref[:HALF], rows_ref[HALF:]))
    two = grad_tile((a0, a1), (proj_ref[:HALF], proj_ref[HALF:]))
    for k in range(2):
        part = slice(k * CHUNK, (k + 1) * CHUNK)
        out_ref[k, :, :VW] = one[part]
        out_ref[k, :, VW : VW + PW] = two[part]
        out_ref[k, :, VW + PW :] = jnp.zeros((CHUNK, AW - VW - PW), bf16)


def grads(kernel, out_shape, out_block, other, tiled, whole):
    def full(a):
        return pl.BlockSpec(a.shape, lambda i: (0, 0))

    return pl.pallas_call(
        kernel,
        grid=(D // TILE,),
        out_shape=jax.ShapeDtypeStruct(out_shape, bf16),
        in_specs=[pl.BlockSpec(memory_space=pl.ANY)]
        + [pl.BlockSpec((HALF, TILE), lambda i: (0, i))] * len(tiled)
        + [full(a) for a in whole],
        out_specs=pl.BlockSpec(out_block, lambda i: (i,) + (0,) * (len(out_block) - 1)),
        compiler_params=pltpu.CompilerParams(vmem_limit_bytes=48 * 1024 * 1024),
    )(other, *tiled, *whole)


def plain(kernel, outs, *args):
    return pl.pallas_call(
        kernel,
        out_shape=outs,
        compiler_params=pltpu.CompilerParams(vmem_limit_bytes=48 * 1024 * 1024),
    )(*args)


def same(*arrays):
    return [jax.ShapeDtypeStruct(a.shape, f32) for a in arrays]


def unit_norm(rows):
    inv = lax.rsqrt(jnp.mean(rows * rows, axis=-1, keepdims=True) + norm_eps)
    return rows * inv, inv


def unit_norm_back(shaped, unit, inv):
    return inv * (shaped - unit * jnp.mean(shaped * unit, axis=-1, keepdims=True))


def exchange(a):
    return lax.all_to_all(a, GROUPS, 0, 0)


def shards(
    tokens, cotangent, row_lengths, gains, gain_first, gain_second,
    feature_weight, feature_first, feature_second,
    value_weight, value_first, value_second,
    output_weight, output_first, output_second,
    gateup_weight, gateup_first, gateup_second,
    down_weight, down_first, down_second,
):
    core = lax.axis_index("core")
    group = (lax.axis_index("x_lo") * 4 + lax.axis_index("z")) * 2 + lax.axis_index("x_hi")
    gain_low = gains.astype(bf16).astype(f32)

    gain_col = gain_low.T
    flat = [jnp.transpose(a, (1, 2, 0)) for a in (gateup_weight, gateup_first, gateup_second)]
    thin = [
        jnp.transpose(a, (1, 2, 0)).reshape(QK, CHUNK)
        for a in (feature_weight, feature_first, feature_second)
    ]
    first_part = plain(
        pack_first_kernel,
        jax.ShapeDtypeStruct((CHUNK, AW), bf16),
        value_weight, thin[0], output_weight, gain_low, gain_col,
    )
    gateup_part = plain(
        pack_mlp_kernel,
        jax.ShapeDtypeStruct((CHUNK, 3 * FFP), bf16),
        flat[0], down_weight, gain_low,
    )
    tokens, cot = to_group_order(tokens, cotangent)

    first_part = cross(first_part)
    tokens = cross(tokens)
    inputs = tokens.astype(f32)
    unit_one, inv_one = unit_norm(inputs)
    acts_one = gather_rows(unit_one.astype(bf16))
    attn_w = lax.all_gather(first_part, GROUPS, axis=0, tiled=True)
    out_w = attn_w[:, :VW]
    proj_w = attn_w[:, VW : VW + PW]
    gateup_part = cross(after(gateup_part, acts_one[0]))
    mlp_w = lax.all_gather(gateup_part, GROUPS, axis=0, tiled=True)
    gateup_w = mlp_w[:, : 2 * FFP]
    down_w = mlp_w[:, 2 * FFP :]
    proj = jnp.concatenate([matmul(a, proj_w).astype(bf16) for a in acts_one])
    cot = cross(after(cot, gateup_part))
    grad_mlp = gather_rows_apart(after(cot, proj))

    ends = jnp.cumsum(row_lengths)

    def doc_of(pos):
        return jnp.sum((pos[..., None] >= ends).astype(jnp.int32), axis=-1)

    positions = group * ROWS + jnp.arange(ROWS, dtype=jnp.int32)
    docs = doc_of(positions)
    places = jnp.arange(N_GROUPS, dtype=jnp.int32)
    group_ids = (places % 8) * 2 + places // 8
    doc_end = doc_of(group_ids * ROWS + (ROWS - 1))
    doc_before = jnp.where(group_ids > 0, doc_of(group_ids * ROWS - 1), -1)
    last_doc = docs[ROWS - 1]
    before = jnp.where(group > 0, doc_of(group * ROWS - 1), -1)
    masks = jnp.stack(
        [
            (docs == last_doc).astype(f32),
            (docs == before).astype(f32),
            docs.astype(f32),
        ],
        axis=1,
    )
    doc_row = docs.astype(f32)[None]
    carry = ((group_ids[None, :] < group_ids[:, None]) & (doc_end[None, :] == doc_before[:, None])).astype(f32)
    back = ((group_ids[None, :] > group_ids[:, None]) & (doc_before[None, :] == doc_end[:, None])).astype(f32)
    chunk_ids = jnp.arange(8, dtype=jnp.int32)
    idx = ((chunk_ids % 2) ^ core) * 4 + chunk_ids // 2

    left, right, rows, move = feature_tables()
    own_state = call(
        key_state_kernel,
        [jax.ShapeDtypeStruct((STATE_ROWS, DV), f32)],
        [pltpu.VMEM((ROWS, PW), bf16)],
        6,
    )(idx, proj, masks, left, right, rows)[0]
    slices = exchange(own_state.reshape(N_GROUPS, STATE_ROWS // N_GROUPS, DV))
    slices = jnp.sum(carry[:, :, None, None] * slices[None], axis=1)
    state = exchange(slices).reshape(STATE_ROWS, DV)
    att, den, attn_rows = call(
        attend_kernel,
        [
            jax.ShapeDtypeStruct((ROWS, VW), f32),
            jax.ShapeDtypeStruct((ROWS, LOCAL_HEADS), f32),
            jax.ShapeDtypeStruct((ROWS, VW), bf16),
        ],
        [pltpu.VMEM((ROWS, PW), bf16)],
        9,
    )(idx, proj, masks, doc_row, state, left, right, rows, move)

    middle = inputs + scatter_rows(
        rows_of(halves_of(after(attn_rows, grad_mlp[1])), out_w, ((1,), (1,)))
    )
    unit_two, inv_two = unit_norm(middle)
    acts_two = gather_rows(unit_two.astype(bf16))
    hidden = []
    grad_gate_up = []
    for acts, grad in zip(acts_two, grad_mlp):
        gate_up = matmul(acts, gateup_w)
        grad_hidden = matmul(grad, down_w)
        gate = gate_up[:, :FFP]
        up = gate_up[:, FFP:]
        sigmoid = jax.nn.sigmoid(gate)
        silu = gate * sigmoid
        hidden.append((silu * up).astype(bf16))
        dsilu = sigmoid * (1.0 + gate * (1.0 - sigmoid))
        grad_gate_up.append(
            jnp.concatenate([grad_hidden * up * dsilu, grad_hidden * silu], axis=1).astype(bf16)
        )

    late = []

    def mlp_grads(send, low):
        mlp_grad = grads(
            mlp_grads_kernel, (D, 3 * FFP), (TILE, 3 * FFP), low,
            acts_two + grad_mlp, (*grad_gate_up, *hidden),
        )
        late.append(mlp_grad)

    shaped_two = scatter_rows(rows_of(grad_gate_up, gateup_w, ((1,), (1,))), mlp_grads)
    mlp_grad = lax.psum_scatter(after(late[0], shaped_two), GROUPS, scatter_dimension=0, tiled=True)
    grad_out = cot.astype(f32)
    grad_mid = grad_out + unit_norm_back(shaped_two, unit_two, inv_two)
    grad_attn = gather_rows(grad_mid.astype(bf16))

    last_hidden = [after(a, grad_attn[1]) for a in hidden]
    mixed = middle + scatter_rows(rows_of(last_hidden, down_w, ((1,), (1,))), total=sum_rows_apart)
    mixed = mixed.astype(bf16)

    grad_low = jnp.concatenate([matmul(a, out_w).astype(bf16) for a in grad_attn])
    own_grad, gn, gd = call(
        query_state_kernel,
        [
            jax.ShapeDtypeStruct((STATE_ROWS, DV), f32),
            jax.ShapeDtypeStruct((ROWS, VW), f32),
            jax.ShapeDtypeStruct((ROWS, LOCAL_HEADS), f32),
        ],
        [pltpu.VMEM((ROWS, PW), bf16), pltpu.VMEM((ROWS, VW), bf16)],
        9,
    )(idx, proj, grad_low, masks, att, den, left, right, rows)
    den_part = jnp.sum(jnp.abs(den))
    slices = exchange(
        jnp.concatenate(
            [
                own_grad.reshape(N_GROUPS, STATE_ROWS // N_GROUPS, DV),
                jnp.full((N_GROUPS, 8, DV), den_part, f32),
            ],
            axis=1,
        )
    )
    den_group = jnp.sum(slices[:, STATE_ROWS // N_GROUPS :], axis=0)
    slices = jnp.sum(back[:, :, None, None] * slices[None, :, : STATE_ROWS // N_GROUPS], axis=1)
    grad_state = exchange(slices).reshape(STATE_ROWS, DV)
    grad_proj = call(
        attend_back_kernel,
        [jax.ShapeDtypeStruct((ROWS, PW), bf16)],
        [pltpu.VMEM((ROWS, PW), bf16), pltpu.VMEM((ROWS, QK), f32), pltpu.VMEM((ROWS, VW), f32)],
        12,
    )(idx, proj, gn, after(gd, mixed), masks, doc_row, state, grad_state, left, right, rows, move)[0]

    def proj_grads(send, low):
        attn_grad = grads(
            attn_grads_kernel, (N_GROUPS, CHUNK, AW), (2, CHUNK, AW), send,
            acts_one + grad_attn, (grad_proj, attn_rows),
        )
        late.append(exchange(attn_grad))

    mixed = from_group_order(cross(mixed), bf16)
    shaped_one = scatter_rows(rows_of(halves_of(grad_proj), proj_w, ((1,), (1,))), proj_grads, sum_rows_apart)
    grad_tokens = grad_mid + unit_norm_back(shaped_one, unit_one, inv_one)
    grad_tokens = from_group_order(cross(grad_tokens.astype(bf16)), f32)
    attn_grad = jnp.sum(late[1].astype(f32), axis=0)
    gain_one = jnp.sum((attn_grad * first_part.astype(f32))[:, VW:], axis=1)
    gain_two = jnp.sum(
        (mlp_grad.astype(f32) * gateup_part.astype(f32))[:, : 2 * FFP], axis=1
    )
    small = jnp.concatenate([gain_one[None], gain_two[None], den_group[:6]], axis=0)
    small = jnp.sum(
        lax.all_to_all(jnp.broadcast_to(small[None], (8, 8, CHUNK)), ("y", "core"), 0, 0), axis=0
    )
    small = cross(small)
    attn_grad = cross(attn_grad.astype(bf16))
    mlp_grad = cross(mlp_grad)

    gain_total = small[:2] / gain_low
    den_mean = small[2, 0] / (N_GROUPS * ROWS * HEADS)
    deep = plain(
        adam_mlp_kernel,
        same(*flat, down_weight, down_first, down_second),
        mlp_grad, gain_low, *flat, down_weight, down_first, down_second,
    )
    near = (*thin, value_weight, value_first, value_second, output_weight, output_first, output_second)
    near = plain(adam_attn_kernel, same(*near), attn_grad, gain_low, gain_col, *near)
    news = list(adam_step(gains, gain_first, gain_second, gain_total, gain_rate))
    news += [jnp.transpose(a.reshape(2, QK // 2, CHUNK), (2, 0, 1)) for a in near[:3]]
    news += near[3:]
    news += [jnp.transpose(a, (2, 0, 1)) for a in deep[:3]]
    news += deep[3:]
    return (mixed, grad_tokens, den_mean) + tuple(news)


def solution(mesh):
    fine = jax.sharding.Mesh(mesh.devices.reshape(2, 4, 2, 4, 2), FINE)
    dp = ("x_lo", "z", "core")
    tensor = ("y", "x_hi")
    rows = P(FINE, None)
    gain = P(None, dp)
    deep = P(dp, None, tensor)
    down = P(dp, tensor)
    across = P(tensor, dp)
    return jax.shard_map(
        shards,
        mesh=fine,
        in_specs=(rows, rows, P())
        + (gain,) * 3
        + (deep,) * 3
        + (down,) * 3
        + (across,) * 3
        + (deep,) * 3
        + (across,) * 3,
        out_specs=(rows, rows, P())
        + (gain,) * 3
        + (deep,) * 3
        + (down,) * 3
        + (across,) * 3
        + (deep,) * 3
        + (across,) * 3,
        check_vma=False,
    )
```

```python
import functools

import jax
import jax.numpy as jnp
import numpy as np
from jax import lax
from jax.experimental import pallas as pl
from jax.experimental.pallas import tpu as pltpu
from jax.sharding import PartitionSpec as P

D = 2048
HEADS = 16
FEAT = 16
DV = 128
FF = 5504
STEP = 10
FINE = ("x_lo", "z", "core", "y", "x_hi")
GROUPS = ("x_hi", "x_lo", "z")
N_GROUPS = 16
ROWS = 1024
CHUNK = 128
HALF = ROWS // 2
LOCAL_HEADS = 2
QK = 2 * LOCAL_HEADS * FEAT
VW = LOCAL_HEADS * DV
PW = VW + QK
FFL = 688
FFP = 768
AW = 640
PHI = 256
PHI_ROWS = 160
HEAD_ROWS = 192
STATE_ROWS = LOCAL_HEADS * HEAD_ROWS
TILE = 256

norm_eps = 1e-05
beta_one = 0.5
beta_two = 0.5
adam_eps = 1e-08
weight_decay = 0.01
gain_rate = 0.5

f32 = jnp.float32
bf16 = jnp.bfloat16


FLIP = [(0, 1), (1, 0)]
CROSS = [(0, 0), (1, 2), (2, 1), (3, 3)]


def cross(a):
    return lax.ppermute(a, ("core", "x_hi"), CROSS)


def swap_core(a):
    return lax.ppermute(a, "core", FLIP)


def over_y(a):
    return lax.all_to_all(a, "y", 0, 0)


def spread(mine):
    return jnp.broadcast_to(mine[None], (4,) + mine.shape)


def to_y(a, step):
    return lax.ppermute(a, "y", [(i, (i + step) % 4) for i in range(4)])


def gather_rows(mine):
    own = over_y(spread(mine)).reshape(HALF, -1)
    return own, swap_core(own)


def sum_rows(low):
    return jnp.sum(over_y(low.reshape(4, CHUNK, D)).astype(f32), axis=0)


def sum_rows_apart(low):
    y = lax.axis_index("y")

    def part(step):
        return lax.dynamic_slice(low, ((y + step) % 4 * CHUNK, 0), (CHUNK, D))

    parts = [to_y(part(step), step) for step in (1, 2, 3)]
    out = part(0).astype(f32)
    for a in parts:
        out = out + a.astype(f32)
    return out


def scatter_rows(partial, between=None, total=sum_rows, later=None):
    send = partial(1, None)
    got = swap_core(send)
    if later is not None:
        got = after(got, later)
    low = partial(0, got)
    if between is not None:
        between(send, low)
    return total(low)


def rows_of(halves, weight, dims):
    def partial(half, more):
        total = matmul(halves[half], weight, dims)
        if more is not None:
            total = total + more.astype(f32)
        return total.astype(bf16)

    return partial


def halves_of(a):
    return a[:HALF], a[HALF:]


def matmul(a, b, dims=((1,), (0,))):
    return lax.dot_general(a, b, (dims, ((), ())), preferred_element_type=f32)


def iota(shape, dim):
    return lax.broadcasted_iota(jnp.int32, shape, dim)


def sides_of(kind, head):
    base = (kind * LOCAL_HEADS + head) * FEAT
    row = iota((QK, PHI), 0) - base
    col = iota((QK, PHI), 1)
    a = col % FEAT
    pair = col < 136
    one = (row == a) & (pair | ((col >= 144) & (col < PHI_ROWS)))
    two = (row == (a + col // FEAT) % FEAT) & pair
    return one.astype(f32).astype(bf16), two.astype(f32).astype(bf16)


def feature_rows():
    col = iota((1, PHI), 1)
    only = (col == 136).astype(f32)
    linear = ((col >= 144) & (col < PHI_ROWS)).astype(f32)
    square = (col < FEAT).astype(f32)
    cross_term = ((col >= FEAT) & (col < 136)).astype(f32)
    scale = (
        only
        + linear * FEAT ** (-0.25)
        + (square + cross_term * 2.0**0.5) * (2.0 * FEAT) ** (-0.5)
    )
    return only, only + linear, scale


def mover(kind, head):
    base = (kind * LOCAL_HEADS + head) * FEAT
    other = ((1 - kind) * LOCAL_HEADS + head) * FEAT
    row = iota((QK, QK), 0)
    col = iota((QK, QK), 1)
    hit = (row - base == col - other) & (row >= base) & (row < base + FEAT)
    return (hit.astype(f32) * FEAT ** (-0.5)).astype(bf16)


def doc_at(info_ref, pos):
    return sum((pos >= info_ref[8 + i]).astype(jnp.int32) for i in range(3))


def doc_column(info_ref, lo, hi):
    return doc_at(info_ref, info_ref[11] + lo + iota((hi - lo, 1), 0))


def is_last(info_ref, lo, hi):
    return (doc_column(info_ref, lo, hi) == info_ref[12]).astype(f32)


def continues(info_ref, lo, hi):
    return (doc_column(info_ref, lo, hi) == info_ref[13]).astype(f32)


def allowed_at(info_ref, r, end):
    at = r + iota((TILE, end), 0)
    of = iota((TILE, end), 1)
    doc_row = doc_at(info_ref, info_ref[11] + iota((1, end), 1))
    return (of <= at) & (doc_column(info_ref, r, end) == doc_row)


def split(a):
    hi = a.astype(bf16)
    return hi, (a - hi.astype(f32)).astype(bf16)


def dot_low(a, b, dims):
    hi, lo = split(a)
    return matmul(hi, b, dims) + matmul(lo, b, dims)


def dot_full(a, b, dims):
    ah, al = split(a)
    bh, bl = split(b)
    return matmul(ah, bh, dims) + (matmul(al, bh, dims) + matmul(ah, bl, dims))


def side(u, kind, head):
    left, right = sides_of(kind, head)
    one, two, scale = feature_rows()
    return matmul(u, left) + one, matmul(u, right) + two, scale


def to_order(idx_ref, src_ref, dst):
    for i in range(8):
        dst[pl.ds(i * CHUNK, CHUNK), :] = src_ref[
            pl.ds(pl.multiple_of(idx_ref[i] * CHUNK, CHUNK), CHUNK), :
        ]


def from_order(idx_ref, i, dst_ref, block):
    dst_ref[pl.ds(pl.multiple_of(idx_ref[i] * CHUNK, CHUNK), CHUNK), :] = block


def state_rows(ref, head):
    base = head * HEAD_ROWS
    mat = jnp.concatenate(
        [ref[base : base + PHI_ROWS, :], jnp.zeros((PHI - PHI_ROWS, DV), f32)], axis=0
    )
    vec = jnp.concatenate(
        [ref[base + PHI_ROWS : base + PHI_ROWS + 1, :], ref[base + PHI_ROWS + 1 : base + PHI_ROWS + 2, :]],
        axis=1,
    )
    return mat, vec


def store_state(ref, head, mat, vec):
    base = head * HEAD_ROWS
    ref[base : base + PHI_ROWS, :] = mat[:PHI_ROWS]
    tail = jnp.concatenate(
        [vec[:, :DV], vec[:, DV:], jnp.zeros((HEAD_ROWS - PHI_ROWS - 2, DV), f32)], axis=0
    )
    ref[base + PHI_ROWS : base + HEAD_ROWS, :] = tail


def key_state_kernel(idx_ref, p_ref, out_ref, scr):
    to_order(idx_ref, p_ref, scr)
    for head in range(LOCAL_HEADS):
        mat = jnp.zeros((PHI, DV), f32)
        vec = jnp.zeros((1, PHI), f32)
        for r in range(0, ROWS, TILE):
            u = scr[r : r + TILE, VW:PW]
            v = scr[r : r + TILE, head * DV : (head + 1) * DV]
            one, two, scale = side(u, 1, head)
            phi = one * two * scale * is_last(idx_ref, r, r + TILE)
            mat = mat + dot_low(phi, v, ((0,), (0,)))
            vec = vec + jnp.sum(phi, axis=0, keepdims=True)
        store_state(out_ref, head, mat, vec)


def attend_inside_kernel(
    idx_ref, p_ref, num_ref, den_ref, scr,
):
    to_order(idx_ref, p_ref, scr)
    u_all = scr[:, VW:PW]
    for head in range(LOCAL_HEADS):
        cols = slice(head * DV, (head + 1) * DV)
        v_all = scr[:, cols]
        for r in range(0, ROWS, TILE):
            end = r + TILE
            moved = matmul(scr[r:end, VW:PW], mover(0, head)).astype(bf16)
            s = matmul(moved, u_all[:end], ((1,), (1,)))
            allowed = allowed_at(idx_ref, r, end)
            kern = jnp.where(allowed, 1.0 + s + 0.5 * s * s, 0.0)
            num_ref[r:end, cols] = matmul(kern.astype(bf16), v_all[:end])
            den_ref[r:end, head : head + 1] = jnp.sum(kern, axis=1, keepdims=True)


def attend_kernel(
    idx_ref, p_ref, num_ref, den_in_ref, state_ref,
    att_ref, den_ref, low_ref, scr,
):
    to_order(idx_ref, p_ref, scr)
    for head in range(LOCAL_HEADS):
        cols = slice(head * DV, (head + 1) * DV)
        mat, vec = state_rows(state_ref, head)
        for r in range(0, ROWS, TILE):
            end = r + TILE
            cont = continues(idx_ref, r, end)
            one, two, scale = side(scr[r:end, VW:PW], 0, head)
            phi = one * two * scale
            num = num_ref[r:end, cols] + cont * dot_full(phi, mat, ((1,), (0,)))
            den = den_in_ref[r:end, head : head + 1] + cont * jnp.sum(phi * vec, axis=1, keepdims=True)
            att_ref[r:end, cols] = num / den
            den_ref[r:end, head : head + 1] = den
    for i in range(8):
        from_order(idx_ref, i, low_ref, att_ref[i * CHUNK : (i + 1) * CHUNK, :].astype(bf16))


def query_state_kernel(
    idx_ref, p_ref, ga_ref, att_ref, den_ref,
    out_ref, gn_ref, gd_ref, scr, gscr,
):
    to_order(idx_ref, p_ref, scr)
    to_order(idx_ref, ga_ref, gscr)
    for head in range(LOCAL_HEADS):
        mat = jnp.zeros((PHI, DV), f32)
        vec = jnp.zeros((1, PHI), f32)
        cols = slice(head * DV, (head + 1) * DV)
        for r in range(0, ROWS, TILE):
            end = r + TILE
            den = den_ref[r:end, head : head + 1]
            ga = gscr[r:end, cols].astype(f32)
            gn = ga / den
            gd = -jnp.sum(ga * att_ref[r:end, cols], axis=1, keepdims=True) / den
            gn_ref[r:end, cols] = gn
            gd_ref[r:end, head : head + 1] = gd
            one, two, scale = side(scr[r:end, VW:PW], 0, head)
            phi = one * two * scale * continues(idx_ref, r, end)
            mat = mat + dot_full(phi, gn, ((0,), (0,)))
            vec = vec + jnp.sum(phi * gd, axis=0, keepdims=True)
        store_state(out_ref, head, mat, vec)


def attend_back_inside_kernel(
    idx_ref, p_ref, gn_ref, gd_ref, gqk, gv, scr,
):
    to_order(idx_ref, p_ref, scr)
    u_all = scr[:, VW:PW]
    gqk[...] = jnp.zeros((ROWS, QK), f32)
    gv[...] = jnp.zeros((ROWS, VW), f32)
    for head in range(LOCAL_HEADS):
        cols = slice(head * DV, (head + 1) * DV)
        v_all = scr[:, cols]
        back_all = matmul(u_all, mover(1, head)).astype(bf16)
        for r in range(0, ROWS, TILE):
            end = r + TILE
            low_gn = gn_ref[r:end, cols].astype(bf16)
            gd = gd_ref[r:end, head : head + 1]
            moved = matmul(scr[r:end, VW:PW], mover(0, head)).astype(bf16)
            s = matmul(moved, u_all[:end], ((1,), (1,)))
            allowed = allowed_at(idx_ref, r, end)
            kern = jnp.where(allowed, 1.0 + s + 0.5 * s * s, 0.0).astype(bf16)
            gk = matmul(low_gn, v_all[:end], ((1,), (1,))) + gd
            gs = jnp.where(allowed, gk * (1.0 + s), 0.0).astype(bf16)
            gqk[r:end, :] = gqk[r:end, :] + matmul(gs, back_all[:end])
            gqk[:end, :] = gqk[:end, :] + matmul(gs, moved, ((0,), (0,)))
            gv[:end, cols] = gv[:end, cols] + matmul(kern, low_gn, ((0,), (0,)))


def attend_back_kernel(
    idx_ref, p_ref, gn_ref, gd_ref, gqk_ref, gv_ref, state_ref, grad_state_ref,
    out_ref, scr, gqk, gv,
):
    to_order(idx_ref, p_ref, scr)
    for head in range(LOCAL_HEADS):
        cols = slice(head * DV, (head + 1) * DV)
        mat, vec = state_rows(state_ref, head)
        gmat, gvec = state_rows(grad_state_ref, head)
        for r in range(0, ROWS, TILE):
            end = r + TILE
            u = scr[r:end, VW:PW]
            cont = continues(idx_ref, r, end)
            in_last = is_last(idx_ref, r, end)
            gn = gn_ref[r:end, cols]
            gd = gd_ref[r:end, head : head + 1]
            one, two, scale = side(u, 0, head)
            left, right = sides_of(0, head)
            grad = (dot_low_right(gn.astype(bf16), mat) + gd * vec) * cont * scale
            acc = matmul((grad * two).astype(bf16), left, ((1,), (1,)))
            acc = acc + matmul((grad * one).astype(bf16), right, ((1,), (1,)))
            one, two, scale = side(u, 1, head)
            left, right = sides_of(1, head)
            grad = (dot_low_right(scr[r:end, cols], gmat) + gvec) * in_last * scale
            acc = acc + matmul((grad * two).astype(bf16), left, ((1,), (1,)))
            acc = acc + matmul((grad * one).astype(bf16), right, ((1,), (1,)))
            phi = one * two * scale * in_last
            before = gqk_ref if head == 0 else gqk
            gqk[r:end, :] = before[r:end, :] + acc
            gv[r:end, cols] = gv_ref[r:end, cols] + dot_low(phi, gmat.astype(bf16), ((1,), (0,)))
    for i in range(8):
        chunk = slice(i * CHUNK, (i + 1) * CHUNK)
        from_order(
            idx_ref, i, out_ref,
            jnp.concatenate([gv[chunk, :], gqk[chunk, :]], axis=1).astype(bf16),
        )


def dot_low_right(a, b):
    hi, lo = split(b)
    return matmul(a, hi, ((1,), (1,))) + matmul(a, lo, ((1,), (1,)))


def call(kernel, outs, scratch, n_in):
    return pl.pallas_call(
        kernel,
        out_shape=outs,
        in_specs=[pl.BlockSpec(memory_space=pltpu.SMEM)]
        + [pl.BlockSpec(memory_space=pltpu.VMEM)] * (n_in - 1),
        out_specs=[pl.BlockSpec(memory_space=pltpu.VMEM)] * len(outs),
        scratch_shapes=scratch,
        compiler_params=pltpu.CompilerParams(vmem_limit_bytes=48 * 1024 * 1024),
    )


def adam_step(weight, moment_one, moment_two, reduced, step_rate):
    new_one = beta_one * moment_one + (1.0 - beta_one) * reduced
    new_two = beta_two * moment_two + (1.0 - beta_two) * reduced * reduced
    corrected_one = new_one / (1.0 - beta_one**STEP)
    corrected_two = new_two / (1.0 - beta_two**STEP)
    master = weight - step_rate * (
        corrected_one / (jnp.sqrt(corrected_two) + adam_eps) + weight_decay * weight
    )
    return (new_one, new_two, master)


def nothing_kernel(other_ref, a_ref, out_ref):
    pass


def after(a, other):
    return pl.pallas_call(
        nothing_kernel,
        out_shape=jax.ShapeDtypeStruct(a.shape, a.dtype),
        in_specs=[pl.BlockSpec(memory_space=pl.ANY)] * 2,
        out_specs=pl.BlockSpec(memory_space=pl.ANY),
        input_output_aliases={1: 0},
    )(other, a)


def pack_first_kernel(value_ref, feature_ref, output_ref, gain_row_ref, gain_col_ref, out_ref):
    def low(a):
        return a.astype(bf16).astype(f32)

    out_ref[:, :VW] = low(output_ref[...]).T.astype(bf16)
    out_ref[:, VW : 2 * VW] = (low(value_ref[...]) * gain_col_ref[:, 0:1]).astype(bf16)
    out_ref[:, 2 * VW : VW + PW] = (low(feature_ref[...]) * gain_row_ref[0:1]).T.astype(bf16)
    out_ref[:, VW + PW :] = jnp.zeros((CHUNK, AW - VW - PW), bf16)


def pack_mlp_kernel(gateup_ref, down_ref, gain_row_ref, out_ref):
    def low(a):
        return a.astype(bf16).astype(f32)

    def wide(a):
        return jnp.concatenate([a, jnp.zeros((FFP - FFL, CHUNK), f32)], axis=0).T.astype(bf16)

    out_ref[:, :FFP] = wide(low(gateup_ref[0]) * gain_row_ref[1:2])
    out_ref[:, FFP : 2 * FFP] = wide(low(gateup_ref[1]) * gain_row_ref[1:2])
    out_ref[:, 2 * FFP :] = wide(low(down_ref[...]))


def adam_store(weight, first, second, grad, rate, outs, at=()):
    place = at if at else (slice(None), slice(None))
    for ref, new in zip(outs, adam_step(weight[place], first[place], second[place], grad, rate)):
        ref[place] = new


def adam_mlp_kernel(
    grad_ref, gain_row_ref, gw, gf, gs, dw, df, ds, g1, g2, g3, d1, d2, d3
):
    for part in range(2):
        grad = grad_ref[part * FFP : part * FFP + FFL].astype(f32)
        adam_store(
            gw, gf, gs, grad * gain_row_ref[1:2], D ** (-0.5), (g1, g2, g3),
            (part, slice(None), slice(None)),
        )
    adam_store(dw, df, ds, grad_ref[2 * FFP : 2 * FFP + FFL].astype(f32), FF ** (-0.5), (d1, d2, d3))


def adam_attn_kernel(
    grad_ref, gain_row_ref,
    fw, ff, fs, vw, vf, vs, ow, of, os, f1, f2, f3, v1, v2, v3, o1, o2, o3,
):
    grad = (grad_ref[VW : 2 * VW].astype(f32) * gain_row_ref[0:1]).T
    adam_store(vw, vf, vs, grad, D ** (-0.5), (v1, v2, v3))
    grad = grad_ref[2 * VW :].astype(f32) * gain_row_ref[0:1]
    adam_store(fw, ff, fs, grad, D ** (-0.5), (f1, f2, f3))
    grad = grad_ref[:VW].astype(f32)
    adam_store(ow, of, os, grad, (HEADS * DV // 64) ** (-0.5), (o1, o2, o3))


def turned(a):
    return a.astype(f32).T.astype(bf16)


def store_owners(out_ref, lo, hi, tile):
    for k in range(2):
        out_ref[k, 0, lo:hi, :] = tile[:, k * CHUNK : (k + 1) * CHUNK].astype(bf16)


def mlp_grads_kernel(other_ref, a0, a1, g0, g1, gu0, gu1, h0, h1, out_ref, scr):
    @pl.when(pl.program_id(0) == 0)
    def turn():
        for half, (gu, h) in enumerate(((gu0, h0), (gu1, h1))):
            cols = slice(half * HALF, (half + 1) * HALF)
            scr[:FFP, cols] = turned(gu[:, :FFP])
            scr[FFP : 2 * FFP, cols] = turned(gu[:, FFP:])
            scr[2 * FFP :, cols] = turned(h[...])

    for lo, hi, left, right in ((0, 2 * FFP, a0, a1), (2 * FFP, 3 * FFP, g0, g1)):
        tile = matmul(scr[lo:hi, :HALF], left[...]) + matmul(scr[lo:hi, HALF:], right[...])
        store_owners(out_ref, lo, hi, tile)


def out_grads_kernel(other_ref, g0, g1, rows_ref, out_ref, scr):
    @pl.when(pl.program_id(0) == 0)
    def turn():
        scr[...] = turned(rows_ref[...])

    tile = matmul(scr[:, :HALF], g0[...]) + matmul(scr[:, HALF:], g1[...])
    store_owners(out_ref, 0, VW, tile)


def proj_grads_kernel(other_ref, a0, a1, out_grad_ref, proj_ref, out_ref, scr):
    @pl.when(pl.program_id(0) == 0)
    def turn():
        scr[:VW] = turned(proj_ref[:, :VW])
        scr[VW:] = turned(proj_ref[:, VW:])

    tile = matmul(scr[:, :HALF], a0[...]) + matmul(scr[:, HALF:], a1[...])
    out_ref[:, 0, :VW, :] = out_grad_ref[:, 0]
    store_owners(out_ref, VW, VW + PW, tile)


def grads(kernel, height, other, tiled, whole, turned_rows, blocks=()):
    def by_owner(n):
        return pl.BlockSpec((2, 1, n, CHUNK), lambda i: (0, i, 0, 0))

    def full(a):
        return pl.BlockSpec(a.shape, lambda i: (0,) * a.ndim)

    return pl.pallas_call(
        kernel,
        grid=(D // TILE,),
        out_shape=jax.ShapeDtypeStruct((2, 8, height, CHUNK), bf16),
        in_specs=[pl.BlockSpec(memory_space=pl.ANY)]
        + [pl.BlockSpec((HALF, TILE), lambda i: (0, i))] * len(tiled)
        + [by_owner(a.shape[2]) for a in blocks]
        + [full(a) for a in whole],
        out_specs=by_owner(height),
        scratch_shapes=[pltpu.VMEM((turned_rows, ROWS), bf16)],
        compiler_params=pltpu.CompilerParams(vmem_limit_bytes=48 * 1024 * 1024),
    )(other, *tiled, *blocks, *whole)


def project_kernel(core_ref, a0, a1, w_ref, out_ref, acc):
    step = pl.program_id(0)

    @pl.when(step == 0)
    def start():
        acc[...] = jnp.zeros_like(acc)

    weight = w_ref[0].reshape(TILE, AW)[:, VW : VW + PW]
    acc[:HALF] += matmul(a0[...], weight)
    acc[HALF:] += matmul(a1[...], weight)

    @pl.when(step == D // TILE - 1)
    def end():
        out_ref[...] = acc[...].astype(bf16)


def project(core, acts, every):
    return pl.pallas_call(
        project_kernel,
        grid_spec=pltpu.PrefetchScalarGridSpec(
            num_scalar_prefetch=1,
            grid=(D // TILE,),
            in_specs=[pl.BlockSpec((HALF, TILE), lambda i, core: (0, i))] * 2
            + [pl.BlockSpec((1, 2, CHUNK, AW), lambda i, core: (core[0], i, 0, 0))],
            out_specs=pl.BlockSpec((ROWS, PW), lambda i, core: (0, 0)),
            scratch_shapes=[pltpu.VMEM((ROWS, PW), f32)],
        ),
        out_shape=jax.ShapeDtypeStruct((ROWS, PW), bf16),
        compiler_params=pltpu.CompilerParams(vmem_limit_bytes=48 * 1024 * 1024),
    )(core, *acts, every)


def plain(kernel, outs, *args):
    return pl.pallas_call(
        kernel,
        out_shape=outs,
        compiler_params=pltpu.CompilerParams(vmem_limit_bytes=48 * 1024 * 1024),
    )(*args)


def same(*arrays):
    return [jax.ShapeDtypeStruct(a.shape, f32) for a in arrays]


def unit_norm(rows):
    inv = lax.rsqrt(jnp.mean(rows * rows, axis=-1, keepdims=True) + norm_eps)
    return rows * inv, inv


def unit_norm_back(shaped, unit, inv):
    return inv * (shaped - unit * jnp.mean(shaped * unit, axis=-1, keepdims=True))


def exchange(a):
    return lax.all_to_all(a, GROUPS, 0, 0)


def shards(
    tokens, cotangent, row_lengths, gains, gain_first, gain_second,
    feature_weight, feature_first, feature_second,
    value_weight, value_first, value_second,
    output_weight, output_first, output_second,
    gateup_weight, gateup_first, gateup_second,
    down_weight, down_first, down_second,
):
    core = lax.axis_index("core")
    group = (lax.axis_index("x_lo") * 4 + lax.axis_index("z")) * 2 + lax.axis_index("x_hi")
    gain_low = gains.astype(bf16).astype(f32)
    place = jnp.reshape(core, (1,)).astype(jnp.int32)

    gain_col = gain_low.T
    flat = [jnp.transpose(a, (1, 2, 0)) for a in (gateup_weight, gateup_first, gateup_second)]
    thin = [
        jnp.transpose(a, (1, 2, 0)).reshape(QK, CHUNK)
        for a in (feature_weight, feature_first, feature_second)
    ]
    first_part = plain(
        pack_first_kernel,
        jax.ShapeDtypeStruct((CHUNK, AW), bf16),
        value_weight, thin[0], output_weight, gain_low, gain_col,
    )
    gateup_part = plain(
        pack_mlp_kernel,
        jax.ShapeDtypeStruct((CHUNK, 3 * FFP), bf16),
        flat[0], down_weight, gain_low,
    )

    def gather_weights(part):
        every = lax.all_gather(part, ("x_hi", "x_lo", "z", "core"))
        return every.reshape(2, N_GROUPS, CHUNK, part.shape[1])

    def own_slice(every):
        return lax.dynamic_index_in_dim(every, core, 0, False)

    owner = (lax.axis_index("x_lo") * 4 + lax.axis_index("z")) * 2 + lax.axis_index("x_hi")
    every_attn = gather_weights(first_part)
    both = cross(jnp.stack([tokens, cotangent]))
    tokens = both[0]
    cot = both[1]
    inputs = tokens.astype(f32)
    unit_one, inv_one = unit_norm(inputs)
    acts_one = gather_rows(unit_one.astype(bf16))
    grad_mlp = gather_rows(after(cot, acts_one[0]))
    every_mlp = gather_weights(after(gateup_part, acts_one[0]))
    proj = project(place, acts_one, every_attn)
    attn_w = own_slice(after(every_attn, proj))
    first_own = lax.dynamic_index_in_dim(attn_w, owner, 0, False)[:, VW : VW + PW].astype(f32).T
    attn_w = attn_w.reshape(D, AW)
    out_w = attn_w[:, :VW]
    proj_w = attn_w[:, VW : VW + PW]
    mlp_w = own_slice(every_mlp).reshape(D, 3 * FFP)
    gateup_w = mlp_w[:, : 2 * FFP]
    down_w = mlp_w[:, 2 * FFP :]
    gateup_own = lax.dynamic_slice(
        every_mlp, (core, owner, 0, 0), (1, 1, CHUNK, 2 * FFP)
    ).reshape(CHUNK, 2 * FFP)
    gateup_own = gateup_own.T

    ends = jnp.cumsum(row_lengths)

    def doc_of(pos):
        return jnp.sum((pos[..., None] >= ends).astype(jnp.int32), axis=-1)

    places = jnp.arange(N_GROUPS, dtype=jnp.int32)
    group_ids = (places % 8) * 2 + places // 8
    doc_end = doc_of(group_ids * ROWS + (ROWS - 1))
    doc_before = jnp.where(group_ids > 0, doc_of(group_ids * ROWS - 1), -1)
    last_doc = doc_of(group * ROWS + (ROWS - 1))
    before = jnp.where(group > 0, doc_of(group * ROWS - 1), -1)
    carry = ((group_ids[None, :] < group_ids[:, None]) & (doc_end[None, :] == doc_before[:, None])).astype(f32)
    back = ((group_ids[None, :] > group_ids[:, None]) & (doc_before[None, :] == doc_end[:, None])).astype(f32)
    chunk_ids = jnp.arange(8, dtype=jnp.int32)
    idx = ((chunk_ids % 2) ^ core) * 4 + chunk_ids // 2
    idx = jnp.concatenate([idx, ends, jnp.stack([group * ROWS, last_doc, before])]).astype(jnp.int32)

    own_state = call(
        key_state_kernel,
        [jax.ShapeDtypeStruct((STATE_ROWS, DV), f32)],
        [pltpu.VMEM((ROWS, PW), bf16)],
        2,
    )(idx, proj)[0]
    slices = exchange(after(own_state, grad_mlp[0]).reshape(N_GROUPS, STATE_ROWS // N_GROUPS, DV))
    slices = jnp.sum(carry[:, :, None, None] * slices[None], axis=1)
    state = exchange(slices).reshape(STATE_ROWS, DV)
    num, den = call(
        attend_inside_kernel,
        [jax.ShapeDtypeStruct((ROWS, VW), f32), jax.ShapeDtypeStruct((ROWS, LOCAL_HEADS), f32)],
        [pltpu.VMEM((ROWS, PW), bf16)],
        2,
    )(idx, proj)
    att, den, attn_rows = call(
        attend_kernel,
        [
            jax.ShapeDtypeStruct((ROWS, VW), f32),
            jax.ShapeDtypeStruct((ROWS, LOCAL_HEADS), f32),
            jax.ShapeDtypeStruct((ROWS, VW), bf16),
        ],
        [pltpu.VMEM((ROWS, PW), bf16)],
        5,
    )(idx, proj, num, after(den, attn_w), state)

    middle = after(inputs, mlp_w) + scatter_rows(
        rows_of(halves_of(attn_rows), out_w, ((1,), (1,)))
    )
    unit_two, inv_two = unit_norm(middle)
    acts_two = gather_rows(unit_two.astype(bf16))
    hidden = []
    grad_gate_up = []
    for acts, grad in zip(acts_two, grad_mlp):
        gate_up = matmul(acts, gateup_w)
        grad_hidden = matmul(grad, down_w)
        gate = gate_up[:, :FFP]
        up = gate_up[:, FFP:]
        sigmoid = jax.nn.sigmoid(gate)
        silu = gate * sigmoid
        hidden.append((silu * up).astype(bf16))
        dsilu = sigmoid * (1.0 + gate * (1.0 - sigmoid))
        grad_gate_up.append(
            jnp.concatenate([grad_hidden * up * dsilu, grad_hidden * silu], axis=1).astype(bf16)
        )

    late = []

    def mlp_grads(send, low):
        mlp_grad = grads(
            mlp_grads_kernel, 3 * FFP, low, acts_two + grad_mlp, (*grad_gate_up, *hidden), 3 * FFP
        ).reshape(N_GROUPS * 3 * FFP, CHUNK)
        late.append(mlp_grad)

    shaped_two = scatter_rows(
        rows_of(grad_gate_up, gateup_w, ((1,), (1,))), mlp_grads
    )
    mlp_grad = lax.psum_scatter(after(late[0], shaped_two), GROUPS, scatter_dimension=0, tiled=True)
    grad_out = cot.astype(f32)
    grad_mid = grad_out + unit_norm_back(shaped_two, unit_two, inv_two)
    grad_attn = gather_rows(grad_mid.astype(bf16))

    mixed_own, mixed_other = [
        matmul(after(hidden[half], shaped_two), down_w, ((1,), (1,))).astype(bf16) for half in (0, 1)
    ]
    grad_low = jnp.concatenate([matmul(a, out_w).astype(bf16) for a in grad_attn])
    grad_low = after(after(grad_low, mixed_own), mixed_other)
    mixed_other = swap_core(mixed_other)
    mixed_low = (mixed_own.astype(f32) + mixed_other.astype(f32)).astype(bf16)
    mixed = middle + sum_rows_apart(after(mixed_low, grad_attn[1]))
    own_grad, gn, gd = call(
        query_state_kernel,
        [
            jax.ShapeDtypeStruct((STATE_ROWS, DV), f32),
            jax.ShapeDtypeStruct((ROWS, VW), f32),
            jax.ShapeDtypeStruct((ROWS, LOCAL_HEADS), f32),
        ],
        [pltpu.VMEM((ROWS, PW), bf16), pltpu.VMEM((ROWS, VW), bf16)],
        5,
    )(idx, proj, grad_low, att, den)
    den_part = jnp.sum(jnp.abs(den))
    slices = exchange(
        jnp.concatenate(
            [
                own_grad.reshape(N_GROUPS, STATE_ROWS // N_GROUPS, DV),
                jnp.full((N_GROUPS, 8, DV), den_part, f32),
            ],
            axis=1,
        )
    )
    den_group = jnp.sum(slices[:, STATE_ROWS // N_GROUPS :], axis=0)
    slices = jnp.sum(back[:, :, None, None] * slices[None, :, : STATE_ROWS // N_GROUPS], axis=1)
    output_grad = grads(out_grads_kernel, VW, own_grad, grad_attn, (attn_rows,), VW)
    grad_state = exchange(slices).reshape(STATE_ROWS, DV)
    mlp_grad_own = cross(after(mlp_grad, grad_state))
    gqk, gv = call(
        attend_back_inside_kernel,
        [jax.ShapeDtypeStruct((ROWS, QK), f32), jax.ShapeDtypeStruct((ROWS, VW), f32)],
        [pltpu.VMEM((ROWS, PW), bf16)],
        4,
    )(idx, proj, gn, gd)
    grad_proj = call(
        attend_back_kernel,
        [jax.ShapeDtypeStruct((ROWS, PW), bf16)],
        [pltpu.VMEM((ROWS, PW), bf16), pltpu.VMEM((ROWS, QK), f32), pltpu.VMEM((ROWS, VW), f32)],
        8,
    )(idx, proj, gn, after(after(gd, output_grad), mixed), gqk, gv, state, grad_state)[0]

    def proj_grads(send, low):
        attn_grad = grads(
            proj_grads_kernel, VW + PW, send, acts_one, (grad_proj,), PW, (output_grad,)
        ).reshape(N_GROUPS, VW + PW, CHUNK)
        late.append(exchange(attn_grad))

    mixed = cross(mixed.astype(bf16))
    shaped_one = scatter_rows(rows_of(halves_of(grad_proj), proj_w, ((1,), (1,))), proj_grads, sum_rows_apart)
    grad_tokens = grad_mid + unit_norm_back(shaped_one, unit_one, inv_one)
    grad_tokens = cross(grad_tokens.astype(bf16)).astype(f32)
    deep = plain(
        adam_mlp_kernel,
        same(*flat, down_weight, down_first, down_second),
        mlp_grad_own, gain_low, *flat, down_weight, down_first, down_second,
    )
    attn_grad = jnp.sum(after(late[1], deep[0]).astype(f32), axis=0)
    gain_one = jnp.sum(attn_grad[VW:] * first_own, axis=0)
    gain_two = jnp.sum(mlp_grad[: 2 * FFP].astype(f32) * gateup_own.astype(f32), axis=0)
    small = jnp.concatenate([gain_one[None], gain_two[None], den_group[:6]], axis=0)
    parts = lax.all_to_all(
        jnp.broadcast_to(small[None], (16, 8, CHUNK)), ("core", "y", "x_hi"), 0, 0
    ).reshape(8, 2, 8, CHUNK)
    small = jnp.sum(jnp.where(core == 0, parts[:, 0], parts[:, 1]), axis=0)
    attn_grad = cross(attn_grad.astype(bf16))

    gain_total = small[:2] / gain_low
    den_mean = small[2, 0] / (N_GROUPS * ROWS * HEADS)
    near = (*thin, value_weight, value_first, value_second, output_weight, output_first, output_second)
    near = plain(adam_attn_kernel, same(*near), attn_grad, gain_low, *near)
    news = list(adam_step(gains, gain_first, gain_second, gain_total, gain_rate))
    news += [jnp.transpose(a.reshape(2, QK // 2, CHUNK), (2, 0, 1)) for a in near[:3]]
    news += near[3:]
    news += [jnp.transpose(a, (2, 0, 1)) for a in deep[:3]]
    news += deep[3:]
    return (mixed, grad_tokens, den_mean) + tuple(news)


def solution(mesh):
    fine = jax.sharding.Mesh(mesh.devices.reshape(2, 4, 2, 4, 2), FINE)
    dp = ("x_lo", "z", "core")
    tensor = ("y", "x_hi")
    rows = P(FINE, None)
    gain = P(None, dp)
    deep = P(dp, None, tensor)
    down = P(dp, tensor)
    across = P(tensor, dp)
    return jax.shard_map(
        shards,
        mesh=fine,
        in_specs=(rows, rows, P())
        + (gain,) * 3
        + (deep,) * 3
        + (down,) * 3
        + (across,) * 3
        + (deep,) * 3
        + (across,) * 3,
        out_specs=(rows, rows, P())
        + (gain,) * 3
        + (deep,) * 3
        + (down,) * 3
        + (across,) * 3
        + (deep,) * 3
        + (across,) * 3,
        check_vma=False,
    )
```

```python
import functools

import jax
import jax.numpy as jnp
import numpy as np
from jax import lax
from jax.experimental import pallas as pl
from jax.experimental.pallas import tpu as pltpu
from jax.sharding import PartitionSpec as P

D = 2048
HEADS = 16
FEAT = 16
DV = 128
FF = 5504
STEP = 10
FINE = ("x_lo", "z", "core", "y", "x_hi")
GROUPS = ("x_hi", "x_lo", "z")
N_GROUPS = 16
ROWS = 1024
CHUNK = 128
HALF = ROWS // 2
LOCAL_HEADS = 2
QK = 2 * LOCAL_HEADS * FEAT
VW = LOCAL_HEADS * DV
PW = VW + QK
FFL = 688
FFP = 768
AW = 640
PHI = 256
PHI_ROWS = 160
HEAD_ROWS = 192
STATE_ROWS = LOCAL_HEADS * HEAD_ROWS
TILE = 256

norm_eps = 1e-05
beta_one = 0.5
beta_two = 0.5
adam_eps = 1e-08
weight_decay = 0.01
gain_rate = 0.5

f32 = jnp.float32
bf16 = jnp.bfloat16


FLIP = [(0, 1), (1, 0)]
CROSS = [(0, 0), (1, 2), (2, 1), (3, 3)]


def cross(a):
    return lax.ppermute(a, ("core", "x_hi"), CROSS)


def swap_core(a):
    return lax.ppermute(a, "core", FLIP)


def over_y(a):
    return lax.all_to_all(a, "y", 0, 0)


def spread(mine):
    return jnp.broadcast_to(mine[None], (4,) + mine.shape)


def to_y(a, step):
    return lax.ppermute(a, "y", [(i, (i + step) % 4) for i in range(4)])


def gather_rows(spread_rows):
    own = over_y(spread_rows).reshape(HALF, -1)
    return own, swap_core(own)


def parts_of_rows(low):
    return over_y(low.reshape(4, CHUNK, D))


def norm_kernel(parts_ref, inputs_ref, middle_ref, out_ref):
    middle = inputs_ref[...].astype(f32)
    for k in range(4):
        middle = middle + parts_ref[k].astype(f32)
    middle_ref[...] = middle
    inv = lax.rsqrt(jnp.mean(middle * middle, axis=-1, keepdims=True) + norm_eps)
    low = (middle * inv).astype(bf16)
    for k in range(4):
        out_ref[k] = low


def norm_back_kernel(parts_ref, middle_ref, cot_ref, grad_ref, out_ref):
    middle = middle_ref[...]
    inv = lax.rsqrt(jnp.mean(middle * middle, axis=-1, keepdims=True) + norm_eps)
    unit = middle * inv
    shaped = parts_ref[0].astype(f32)
    for k in range(1, 4):
        shaped = shaped + parts_ref[k].astype(f32)
    grad = cot_ref[...].astype(f32) + inv * (
        shaped - unit * jnp.mean(shaped * unit, axis=-1, keepdims=True)
    )
    grad_ref[...] = grad
    low = grad.astype(bf16)
    for k in range(4):
        out_ref[k] = low


def on_rows(kernel, *args):
    return pl.pallas_call(
        kernel,
        out_shape=[
            jax.ShapeDtypeStruct((CHUNK, D), f32),
            jax.ShapeDtypeStruct((4, CHUNK, D), bf16),
        ],
        compiler_params=pltpu.CompilerParams(vmem_limit_bytes=32 * 1024 * 1024),
    )(*args)


def sum_rows_apart(low):
    y = lax.axis_index("y")

    def part(step):
        return lax.dynamic_slice(low, ((y + step) % 4 * CHUNK, 0), (CHUNK, D))

    parts = [to_y(part(step), step) for step in (1, 2, 3)]
    out = part(0).astype(f32)
    for a in parts:
        out = out + a.astype(f32)
    return out


def scatter_rows(partial, between=None, total=parts_of_rows, later=None):
    send = partial(1, None)
    got = swap_core(send)
    if later is not None:
        got = after(got, later)
    low = partial(0, got)
    if between is not None:
        between(send, low)
    return total(low)


def rows_of(halves, weight, dims):
    def partial(half, more):
        total = matmul(halves[half], weight, dims)
        if more is not None:
            total = total + more.astype(f32)
        return total.astype(bf16)

    return partial


def halves_of(a):
    return a[:HALF], a[HALF:]


def matmul(a, b, dims=((1,), (0,))):
    return lax.dot_general(a, b, (dims, ((), ())), preferred_element_type=f32)


def iota(shape, dim):
    return lax.broadcasted_iota(jnp.int32, shape, dim)


def sides_of(kind, head):
    base = (kind * LOCAL_HEADS + head) * FEAT
    row = iota((QK, PHI), 0) - base
    col = iota((QK, PHI), 1)
    a = col % FEAT
    pair = col < 136
    one = (row == a) & (pair | ((col >= 144) & (col < PHI_ROWS)))
    two = (row == (a + col // FEAT) % FEAT) & pair
    return one.astype(f32).astype(bf16), two.astype(f32).astype(bf16)


def feature_rows():
    col = iota((1, PHI), 1)
    only = (col == 136).astype(f32)
    linear = ((col >= 144) & (col < PHI_ROWS)).astype(f32)
    square = (col < FEAT).astype(f32)
    cross_term = ((col >= FEAT) & (col < 136)).astype(f32)
    scale = (
        only
        + linear * FEAT ** (-0.25)
        + (square + cross_term * 2.0**0.5) * (2.0 * FEAT) ** (-0.5)
    )
    return only, only + linear, scale


def mover(kind, head):
    base = (kind * LOCAL_HEADS + head) * FEAT
    other = ((1 - kind) * LOCAL_HEADS + head) * FEAT
    row = iota((QK, QK), 0)
    col = iota((QK, QK), 1)
    hit = (row - base == col - other) & (row >= base) & (row < base + FEAT)
    return (hit.astype(f32) * FEAT ** (-0.5)).astype(bf16)


def doc_at(info_ref, pos):
    return sum((pos >= info_ref[8 + i]).astype(jnp.int32) for i in range(3))


def doc_column(info_ref, lo, hi):
    return doc_at(info_ref, info_ref[11] + lo + iota((hi - lo, 1), 0))


def is_last(info_ref, lo, hi):
    return (doc_column(info_ref, lo, hi) == info_ref[12]).astype(f32)


def continues(info_ref, lo, hi):
    return (doc_column(info_ref, lo, hi) == info_ref[13]).astype(f32)


def allowed_at(info_ref, r, end):
    at = r + iota((TILE, end), 0)
    of = iota((TILE, end), 1)
    doc_row = doc_at(info_ref, info_ref[11] + iota((1, end), 1))
    return (of <= at) & (doc_column(info_ref, r, end) == doc_row)


def split(a):
    hi = a.astype(bf16)
    return hi, (a - hi.astype(f32)).astype(bf16)


def dot_low(a, b, dims):
    hi, lo = split(a)
    return matmul(hi, b, dims) + matmul(lo, b, dims)


def dot_full(a, b, dims):
    ah, al = split(a)
    bh, bl = split(b)
    return matmul(ah, bh, dims) + (matmul(al, bh, dims) + matmul(ah, bl, dims))


def side(u, kind, head):
    left, right = sides_of(kind, head)
    one, two, scale = feature_rows()
    return matmul(u, left) + one, matmul(u, right) + two, scale


def to_order(idx_ref, src_ref, dst):
    for i in range(8):
        dst[pl.ds(i * CHUNK, CHUNK), :] = src_ref[
            pl.ds(pl.multiple_of(idx_ref[i] * CHUNK, CHUNK), CHUNK), :
        ]


def from_order(idx_ref, i, dst_ref, block):
    dst_ref[pl.ds(pl.multiple_of(idx_ref[i] * CHUNK, CHUNK), CHUNK), :] = block


def state_rows(ref, head):
    base = head * HEAD_ROWS
    mat = jnp.concatenate(
        [ref[base : base + PHI_ROWS, :], jnp.zeros((PHI - PHI_ROWS, DV), f32)], axis=0
    )
    vec = jnp.concatenate(
        [ref[base + PHI_ROWS : base + PHI_ROWS + 1, :], ref[base + PHI_ROWS + 1 : base + PHI_ROWS + 2, :]],
        axis=1,
    )
    return mat, vec


def store_state(ref, head, mat, vec):
    base = head * HEAD_ROWS
    ref[base : base + PHI_ROWS, :] = mat[:PHI_ROWS]
    tail = jnp.concatenate(
        [vec[:, :DV], vec[:, DV:], jnp.zeros((HEAD_ROWS - PHI_ROWS - 2, DV), f32)], axis=0
    )
    ref[base + PHI_ROWS : base + HEAD_ROWS, :] = tail


def key_state_kernel(idx_ref, p_ref, out_ref, scr):
    to_order(idx_ref, p_ref, scr)
    for head in range(LOCAL_HEADS):
        mat = jnp.zeros((PHI, DV), f32)
        vec = jnp.zeros((1, PHI), f32)
        for r in range(0, ROWS, TILE):
            u = scr[r : r + TILE, VW:PW]
            v = scr[r : r + TILE, head * DV : (head + 1) * DV]
            one, two, scale = side(u, 1, head)
            phi = one * two * scale * is_last(idx_ref, r, r + TILE)
            mat = mat + dot_low(phi, v, ((0,), (0,)))
            vec = vec + jnp.sum(phi, axis=0, keepdims=True)
        store_state(out_ref, head, mat, vec)


def attend_inside_kernel(
    idx_ref, p_ref, num_ref, den_ref, scr,
):
    to_order(idx_ref, p_ref, scr)
    u_all = scr[:, VW:PW]
    for head in range(LOCAL_HEADS):
        cols = slice(head * DV, (head + 1) * DV)
        v_all = scr[:, cols]
        for r in range(0, ROWS, TILE):
            end = r + TILE
            moved = matmul(scr[r:end, VW:PW], mover(0, head)).astype(bf16)
            s = matmul(moved, u_all[:end], ((1,), (1,)))
            allowed = allowed_at(idx_ref, r, end)
            kern = jnp.where(allowed, 1.0 + s + 0.5 * s * s, 0.0)
            num_ref[r:end, cols] = matmul(kern.astype(bf16), v_all[:end])
            den_ref[r:end, head : head + 1] = jnp.sum(kern, axis=1, keepdims=True)


def attend_kernel(
    idx_ref, p_ref, num_ref, den_in_ref, state_ref,
    att_ref, den_ref, low_ref, scr,
):
    to_order(idx_ref, p_ref, scr)
    for head in range(LOCAL_HEADS):
        cols = slice(head * DV, (head + 1) * DV)
        mat, vec = state_rows(state_ref, head)
        for r in range(0, ROWS, TILE):
            end = r + TILE
            cont = continues(idx_ref, r, end)
            one, two, scale = side(scr[r:end, VW:PW], 0, head)
            phi = one * two * scale
            num = num_ref[r:end, cols] + cont * dot_full(phi, mat, ((1,), (0,)))
            den = den_in_ref[r:end, head : head + 1] + cont * jnp.sum(phi * vec, axis=1, keepdims=True)
            att_ref[r:end, cols] = num / den
            den_ref[r:end, head : head + 1] = den
    for i in range(8):
        from_order(idx_ref, i, low_ref, att_ref[i * CHUNK : (i + 1) * CHUNK, :].astype(bf16))


def query_state_kernel(
    idx_ref, p_ref, ga_ref, att_ref, den_ref,
    out_ref, gn_ref, gd_ref, scr, gscr,
):
    to_order(idx_ref, p_ref, scr)
    to_order(idx_ref, ga_ref, gscr)
    for head in range(LOCAL_HEADS):
        mat = jnp.zeros((PHI, DV), f32)
        vec = jnp.zeros((1, PHI), f32)
        cols = slice(head * DV, (head + 1) * DV)
        for r in range(0, ROWS, TILE):
            end = r + TILE
            den = den_ref[r:end, head : head + 1]
            ga = gscr[r:end, cols].astype(f32)
            gn = ga / den
            gd = -jnp.sum(ga * att_ref[r:end, cols], axis=1, keepdims=True) / den
            gn_ref[r:end, cols] = gn
            gd_ref[r:end, head : head + 1] = gd
            one, two, scale = side(scr[r:end, VW:PW], 0, head)
            phi = one * two * scale * continues(idx_ref, r, end)
            mat = mat + dot_full(phi, gn, ((0,), (0,)))
            vec = vec + jnp.sum(phi * gd, axis=0, keepdims=True)
        store_state(out_ref, head, mat, vec)


def attend_back_inside_kernel(
    idx_ref, p_ref, gn_ref, gd_ref, gqk, gv, scr,
):
    to_order(idx_ref, p_ref, scr)
    u_all = scr[:, VW:PW]
    gqk[...] = jnp.zeros((ROWS, QK), f32)
    gv[...] = jnp.zeros((ROWS, VW), f32)
    for head in range(LOCAL_HEADS):
        cols = slice(head * DV, (head + 1) * DV)
        v_all = scr[:, cols]
        back_all = matmul(u_all, mover(1, head)).astype(bf16)
        for r in range(0, ROWS, TILE):
            end = r + TILE
            low_gn = gn_ref[r:end, cols].astype(bf16)
            gd = gd_ref[r:end, head : head + 1]
            moved = matmul(scr[r:end, VW:PW], mover(0, head)).astype(bf16)
            s = matmul(moved, u_all[:end], ((1,), (1,)))
            allowed = allowed_at(idx_ref, r, end)
            kern = jnp.where(allowed, 1.0 + s + 0.5 * s * s, 0.0).astype(bf16)
            gk = matmul(low_gn, v_all[:end], ((1,), (1,))) + gd
            gs = jnp.where(allowed, gk * (1.0 + s), 0.0).astype(bf16)
            gqk[r:end, :] = gqk[r:end, :] + matmul(gs, back_all[:end])
            gqk[:end, :] = gqk[:end, :] + matmul(gs, moved, ((0,), (0,)))
            gv[:end, cols] = gv[:end, cols] + matmul(kern, low_gn, ((0,), (0,)))


def attend_back_kernel(
    idx_ref, p_ref, gn_ref, gd_ref, gqk_ref, gv_ref, state_ref, grad_state_ref,
    out_ref, scr, gqk, gv,
):
    to_order(idx_ref, p_ref, scr)
    for head in range(LOCAL_HEADS):
        cols = slice(head * DV, (head + 1) * DV)
        mat, vec = state_rows(state_ref, head)
        gmat, gvec = state_rows(grad_state_ref, head)
        for r in range(0, ROWS, TILE):
            end = r + TILE
            u = scr[r:end, VW:PW]
            cont = continues(idx_ref, r, end)
            in_last = is_last(idx_ref, r, end)
            gn = gn_ref[r:end, cols]
            gd = gd_ref[r:end, head : head + 1]
            one, two, scale = side(u, 0, head)
            left, right = sides_of(0, head)
            grad = (dot_low_right(gn.astype(bf16), mat) + gd * vec) * cont * scale
            acc = matmul((grad * two).astype(bf16), left, ((1,), (1,)))
            acc = acc + matmul((grad * one).astype(bf16), right, ((1,), (1,)))
            one, two, scale = side(u, 1, head)
            left, right = sides_of(1, head)
            grad = (dot_low_right(scr[r:end, cols], gmat) + gvec) * in_last * scale
            acc = acc + matmul((grad * two).astype(bf16), left, ((1,), (1,)))
            acc = acc + matmul((grad * one).astype(bf16), right, ((1,), (1,)))
            phi = one * two * scale * in_last
            before = gqk_ref if head == 0 else gqk
            gqk[r:end, :] = before[r:end, :] + acc
            gv[r:end, cols] = gv_ref[r:end, cols] + dot_low(phi, gmat.astype(bf16), ((1,), (0,)))
    for i in range(8):
        chunk = slice(i * CHUNK, (i + 1) * CHUNK)
        from_order(
            idx_ref, i, out_ref,
            jnp.concatenate([gv[chunk, :], gqk[chunk, :]], axis=1).astype(bf16),
        )


def dot_low_right(a, b):
    hi, lo = split(b)
    return matmul(a, hi, ((1,), (1,))) + matmul(a, lo, ((1,), (1,)))


def call(kernel, outs, scratch, n_in):
    return pl.pallas_call(
        kernel,
        out_shape=outs,
        in_specs=[pl.BlockSpec(memory_space=pltpu.SMEM)]
        + [pl.BlockSpec(memory_space=pltpu.VMEM)] * (n_in - 1),
        out_specs=[pl.BlockSpec(memory_space=pltpu.VMEM)] * len(outs),
        scratch_shapes=scratch,
        compiler_params=pltpu.CompilerParams(vmem_limit_bytes=48 * 1024 * 1024),
    )


def adam_step(weight, moment_one, moment_two, reduced, step_rate):
    new_one = beta_one * moment_one + (1.0 - beta_one) * reduced
    new_two = beta_two * moment_two + (1.0 - beta_two) * reduced * reduced
    corrected_one = new_one / (1.0 - beta_one**STEP)
    corrected_two = new_two / (1.0 - beta_two**STEP)
    master = weight - step_rate * (
        corrected_one / (jnp.sqrt(corrected_two) + adam_eps) + weight_decay * weight
    )
    return (new_one, new_two, master)


def nothing_kernel(other_ref, a_ref, out_ref):
    pass


def after(a, other):
    return pl.pallas_call(
        nothing_kernel,
        out_shape=jax.ShapeDtypeStruct(a.shape, a.dtype),
        in_specs=[pl.BlockSpec(memory_space=pl.ANY)] * 2,
        out_specs=pl.BlockSpec(memory_space=pl.ANY),
        input_output_aliases={1: 0},
    )(other, a)


def pack_first_kernel(value_ref, feature_ref, output_ref, gain_row_ref, gain_col_ref, out_ref):
    def low(a):
        return a.astype(bf16).astype(f32)

    out_ref[:, :VW] = low(output_ref[...]).T.astype(bf16)
    out_ref[:, VW : 2 * VW] = (low(value_ref[...]) * gain_col_ref[:, 0:1]).astype(bf16)
    out_ref[:, 2 * VW : VW + PW] = (low(feature_ref[...]) * gain_row_ref[0:1]).T.astype(bf16)
    out_ref[:, VW + PW :] = jnp.zeros((CHUNK, AW - VW - PW), bf16)


def pack_mlp_kernel(gateup_ref, down_ref, gain_row_ref, out_ref):
    def low(a):
        return a.astype(bf16).astype(f32)

    def wide(a):
        return jnp.concatenate([a, jnp.zeros((FFP - FFL, CHUNK), f32)], axis=0).T.astype(bf16)

    out_ref[:, :FFP] = wide(low(gateup_ref[0]) * gain_row_ref[1:2])
    out_ref[:, FFP : 2 * FFP] = wide(low(gateup_ref[1]) * gain_row_ref[1:2])
    out_ref[:, 2 * FFP :] = wide(low(down_ref[...]))


def adam_store(weight, first, second, grad, rate, outs, at=()):
    place = at if at else (slice(None), slice(None))
    for ref, new in zip(outs, adam_step(weight[place], first[place], second[place], grad, rate)):
        ref[place] = new


def adam_mlp_kernel(
    grad_ref, gain_row_ref, gw, gf, gs, dw, df, ds, g1, g2, g3, d1, d2, d3
):
    for part in range(2):
        grad = grad_ref[part * FFP : part * FFP + FFL].astype(f32)
        adam_store(
            gw, gf, gs, grad * gain_row_ref[1:2], D ** (-0.5), (g1, g2, g3),
            (part, slice(None), slice(None)),
        )
    adam_store(dw, df, ds, grad_ref[2 * FFP : 2 * FFP + FFL].astype(f32), FF ** (-0.5), (d1, d2, d3))


def adam_attn_kernel(
    grad_ref, gain_row_ref,
    fw, ff, fs, vw, vf, vs, ow, of, os, f1, f2, f3, v1, v2, v3, o1, o2, o3,
):
    grad = (grad_ref[VW : 2 * VW].astype(f32) * gain_row_ref[0:1]).T
    adam_store(vw, vf, vs, grad, D ** (-0.5), (v1, v2, v3))
    grad = grad_ref[2 * VW :].astype(f32) * gain_row_ref[0:1]
    adam_store(fw, ff, fs, grad, D ** (-0.5), (f1, f2, f3))
    grad = grad_ref[:VW].astype(f32)
    adam_store(ow, of, os, grad, (HEADS * DV // 64) ** (-0.5), (o1, o2, o3))


def turned(a):
    return a.astype(f32).T.astype(bf16)


def store_owners(out_ref, lo, hi, tile):
    for k in range(2):
        out_ref[k, 0, lo:hi, :] = tile[:, k * CHUNK : (k + 1) * CHUNK].astype(bf16)


def mlp_grads_kernel(core_ref, other_ref, a0, a1, g0, g1, gu0, gu1, h0, h1, out_ref, scr):
    @pl.when(pl.program_id(0) == 0)
    def turn():
        for half, (gu, h) in enumerate(((gu0, h0), (gu1, h1))):
            cols = slice(half * HALF, (half + 1) * HALF)
            for j in range(FFP // TILE):
                rows = slice(j * TILE, (j + 1) * TILE)
                later = slice(FFP + j * TILE, FFP + (j + 1) * TILE)
                scr[rows, cols] = turned(gu[:, 2 * j * TILE : (2 * j + 1) * TILE])
                scr[later, cols] = turned(gu[:, (2 * j + 1) * TILE : (2 * j + 2) * TILE])
            scr[2 * FFP :, cols] = turned(h[...])

    for lo, hi, left, right in ((0, 2 * FFP, a0, a1), (2 * FFP, 3 * FFP, g0.at[0], g1.at[0])):
        tile = matmul(scr[lo:hi, :HALF], left[...]) + matmul(scr[lo:hi, HALF:], right[...])
        store_owners(out_ref, lo, hi, tile)


def out_grads_kernel(core_ref, other_ref, g0, g1, rows_ref, out_ref, scr):
    @pl.when(pl.program_id(0) == 0)
    def turn():
        scr[...] = turned(rows_ref[...])

    tile = matmul(scr[:, :HALF], g0[...]) + matmul(scr[:, HALF:], g1[...])
    store_owners(out_ref, 0, VW, tile)


def proj_grads_kernel(core_ref, other_ref, a0, a1, out_grad_ref, proj_ref, out_ref, scr):
    @pl.when(pl.program_id(0) == 0)
    def turn():
        scr[:VW] = turned(proj_ref[:, :VW])
        scr[VW:] = turned(proj_ref[:, VW:])

    tile = matmul(scr[:, :HALF], a0[...]) + matmul(scr[:, HALF:], a1[...])
    out_ref[:, 0, :VW, :] = out_grad_ref[:, 0]
    store_owners(out_ref, VW, VW + PW, tile)


def grads(kernel, height, place, other, tiled, whole, turned_rows, blocks=(), split=()):
    def by_owner(n):
        return pl.BlockSpec((2, 1, n, CHUNK), lambda i, core: (0, i, 0, 0))

    def full(a):
        return pl.BlockSpec(a.shape, lambda i, core: (0,) * a.ndim)

    in_specs = [pl.BlockSpec(memory_space=pl.ANY)]
    in_specs += [pl.BlockSpec((HALF, TILE), lambda i, core: (0, i))] * len(tiled)
    operands = list(tiled)
    for a in split:
        in_specs += [
            pl.BlockSpec((1, HALF, TILE), lambda i, core: (core[0], 0, i)),
            pl.BlockSpec((1, HALF, TILE), lambda i, core: (1 - core[0], 0, i)),
        ]
        operands += [a, a]
    in_specs += [by_owner(a.shape[2]) for a in blocks] + [full(a) for a in whole]
    return pl.pallas_call(
        kernel,
        grid_spec=pltpu.PrefetchScalarGridSpec(
            num_scalar_prefetch=1,
            grid=(D // TILE,),
            in_specs=in_specs,
            out_specs=by_owner(height),
            scratch_shapes=[pltpu.VMEM((turned_rows, ROWS), bf16)],
        ),
        out_shape=jax.ShapeDtypeStruct((2, 8, height, CHUNK), bf16),
        compiler_params=pltpu.CompilerParams(vmem_limit_bytes=48 * 1024 * 1024),
    )(place, other, *operands, *blocks, *whole)


def mlp_kernel(
    core_ref, a0, a1, g0, g1, gate_ref, up_ref, down_ref,
    h0, h1, gu0, gu1, gateup_out, down_out,
):
    weights = [ref[0].reshape(D, TILE) for ref in (gate_ref, up_ref, down_ref)]
    gateup_out[:, :TILE] = weights[0]
    gateup_out[:, TILE:] = weights[1]
    down_out[...] = weights[2]
    for a, g, h, gu in ((a0, g0, h0, gu0), (a1, g1, h1, gu1)):
        gate = matmul(a[...], weights[0])
        up = matmul(a[...], weights[1])
        grad = matmul(g[0], weights[2])
        sigmoid = jax.nn.sigmoid(gate)
        silu = gate * sigmoid
        h[...] = (silu * up).astype(bf16)
        gu[:, :TILE] = (grad * up * (sigmoid * (1.0 + gate * (1.0 - sigmoid)))).astype(bf16)
        gu[:, TILE:] = (grad * silu).astype(bf16)


def mlp(place, acts, grad, every):
    steps = FFP // TILE

    def cols(part):
        return pl.BlockSpec(
            (1, N_GROUPS, CHUNK, TILE), lambda j, core: (core[0], 0, 0, part * steps + j)
        )

    hidden = pl.BlockSpec((HALF, TILE), lambda j, core: (0, j))

    def wide(n, width):
        return pl.BlockSpec((n, width), lambda j, core: (0, j))

    return pl.pallas_call(
        mlp_kernel,
        grid_spec=pltpu.PrefetchScalarGridSpec(
            num_scalar_prefetch=1,
            grid=(steps,),
            in_specs=[pl.BlockSpec((HALF, D), lambda j, core: (0, 0))] * 2
            + [
                pl.BlockSpec((1, HALF, D), lambda j, core: (core[0], 0, 0)),
                pl.BlockSpec((1, HALF, D), lambda j, core: (1 - core[0], 0, 0)),
                cols(0), cols(1), cols(2),
            ],
            out_specs=[hidden] * 2 + [wide(HALF, 2 * TILE)] * 2 + [wide(D, 2 * TILE), wide(D, TILE)],
        ),
        out_shape=[jax.ShapeDtypeStruct((HALF, FFP), bf16)] * 2
        + [jax.ShapeDtypeStruct((HALF, 2 * FFP), bf16)] * 2
        + [jax.ShapeDtypeStruct((D, 2 * FFP), bf16), jax.ShapeDtypeStruct((D, FFP), bf16)],
        compiler_params=pltpu.CompilerParams(vmem_limit_bytes=56 * 1024 * 1024),
    )(place, *acts, grad, grad, every, every, every)


def project_kernel(core_ref, a0, a1, w_ref, out_ref, acc):
    step = pl.program_id(0)

    @pl.when(step == 0)
    def start():
        acc[...] = jnp.zeros_like(acc)

    weight = w_ref[0].reshape(TILE, AW)[:, VW : VW + PW]
    acc[:HALF] += matmul(a0[...], weight)
    acc[HALF:] += matmul(a1[...], weight)

    @pl.when(step == D // TILE - 1)
    def end():
        out_ref[...] = acc[...].astype(bf16)


def project(core, acts, every):
    return pl.pallas_call(
        project_kernel,
        grid_spec=pltpu.PrefetchScalarGridSpec(
            num_scalar_prefetch=1,
            grid=(D // TILE,),
            in_specs=[pl.BlockSpec((HALF, TILE), lambda i, core: (0, i))] * 2
            + [pl.BlockSpec((1, 2, CHUNK, AW), lambda i, core: (core[0], i, 0, 0))],
            out_specs=pl.BlockSpec((ROWS, PW), lambda i, core: (0, 0)),
            scratch_shapes=[pltpu.VMEM((ROWS, PW), f32)],
        ),
        out_shape=jax.ShapeDtypeStruct((ROWS, PW), bf16),
        compiler_params=pltpu.CompilerParams(vmem_limit_bytes=48 * 1024 * 1024),
    )(core, *acts, every)


def plain(kernel, outs, *args):
    return pl.pallas_call(
        kernel,
        out_shape=outs,
        compiler_params=pltpu.CompilerParams(vmem_limit_bytes=48 * 1024 * 1024),
    )(*args)


def same(*arrays):
    return [jax.ShapeDtypeStruct(a.shape, f32) for a in arrays]


def unit_norm(rows):
    inv = lax.rsqrt(jnp.mean(rows * rows, axis=-1, keepdims=True) + norm_eps)
    return rows * inv, inv


def unit_norm_back(shaped, unit, inv):
    return inv * (shaped - unit * jnp.mean(shaped * unit, axis=-1, keepdims=True))


def exchange(a):
    return lax.all_to_all(a, GROUPS, 0, 0)


def shards(
    tokens, cotangent, row_lengths, gains, gain_first, gain_second,
    feature_weight, feature_first, feature_second,
    value_weight, value_first, value_second,
    output_weight, output_first, output_second,
    gateup_weight, gateup_first, gateup_second,
    down_weight, down_first, down_second,
):
    core = lax.axis_index("core")
    group = (lax.axis_index("x_lo") * 4 + lax.axis_index("z")) * 2 + lax.axis_index("x_hi")
    gain_low = gains.astype(bf16).astype(f32)
    place = jnp.reshape(core, (1,)).astype(jnp.int32)

    gain_col = gain_low.T
    flat = [jnp.transpose(a, (1, 2, 0)) for a in (gateup_weight, gateup_first, gateup_second)]
    thin = [
        jnp.transpose(a, (1, 2, 0)).reshape(QK, CHUNK)
        for a in (feature_weight, feature_first, feature_second)
    ]
    first_part = plain(
        pack_first_kernel,
        jax.ShapeDtypeStruct((CHUNK, AW), bf16),
        value_weight, thin[0], output_weight, gain_low, gain_col,
    )
    gateup_part = plain(
        pack_mlp_kernel,
        jax.ShapeDtypeStruct((CHUNK, 3 * FFP), bf16),
        flat[0], down_weight, gain_low,
    )

    def gather_weights(part):
        every = lax.all_gather(part, ("x_hi", "x_lo", "z", "core"))
        return every.reshape(2, N_GROUPS, CHUNK, part.shape[1])

    def own_slice(every):
        return lax.dynamic_index_in_dim(every, core, 0, False)

    owner = (lax.axis_index("x_lo") * 4 + lax.axis_index("z")) * 2 + lax.axis_index("x_hi")
    every_attn = gather_weights(first_part)
    both = cross(jnp.stack([tokens, cotangent]))
    tokens = both[0]
    cot = both[1]
    inputs = tokens.astype(f32)
    unit_one, inv_one = unit_norm(inputs)
    acts_one = gather_rows(spread(unit_one.astype(bf16)))
    grad_mlp = lax.all_gather(after(after(cot, acts_one[0]), every_attn), ("core", "y")).reshape(2, HALF, D)
    proj = project(place, acts_one, every_attn)
    attn_w = own_slice(after(every_attn, proj))
    first_own = lax.dynamic_index_in_dim(attn_w, owner, 0, False)[:, VW : VW + PW].astype(f32).T
    attn_w = attn_w.reshape(D, AW)
    out_w = attn_w[:, :VW]
    proj_w = attn_w[:, VW : VW + PW]

    ends = jnp.cumsum(row_lengths)

    def doc_of(pos):
        return jnp.sum((pos[..., None] >= ends).astype(jnp.int32), axis=-1)

    places = jnp.arange(N_GROUPS, dtype=jnp.int32)
    group_ids = (places % 8) * 2 + places // 8
    doc_end = doc_of(group_ids * ROWS + (ROWS - 1))
    doc_before = jnp.where(group_ids > 0, doc_of(group_ids * ROWS - 1), -1)
    last_doc = doc_of(group * ROWS + (ROWS - 1))
    before = jnp.where(group > 0, doc_of(group * ROWS - 1), -1)
    carry = ((group_ids[None, :] < group_ids[:, None]) & (doc_end[None, :] == doc_before[:, None])).astype(f32)
    back = ((group_ids[None, :] > group_ids[:, None]) & (doc_before[None, :] == doc_end[:, None])).astype(f32)
    chunk_ids = jnp.arange(8, dtype=jnp.int32)
    idx = ((chunk_ids % 2) ^ core) * 4 + chunk_ids // 2
    idx = jnp.concatenate([idx, ends, jnp.stack([group * ROWS, last_doc, before])]).astype(jnp.int32)

    own_state = call(
        key_state_kernel,
        [jax.ShapeDtypeStruct((STATE_ROWS, DV), f32)],
        [pltpu.VMEM((ROWS, PW), bf16)],
        2,
    )(idx, proj)[0]
    every_mlp = gather_weights(after(gateup_part, own_state))
    gateup_own = lax.dynamic_slice(
        every_mlp, (core, owner, 0, 0), (1, 1, CHUNK, 2 * FFP)
    ).reshape(CHUNK, 2 * FFP)
    gateup_own = gateup_own.T
    slices = exchange(own_state.reshape(N_GROUPS, STATE_ROWS // N_GROUPS, DV))
    slices = jnp.sum(carry[:, :, None, None] * slices[None], axis=1)
    state = exchange(slices).reshape(STATE_ROWS, DV)
    num, den = call(
        attend_inside_kernel,
        [jax.ShapeDtypeStruct((ROWS, VW), f32), jax.ShapeDtypeStruct((ROWS, LOCAL_HEADS), f32)],
        [pltpu.VMEM((ROWS, PW), bf16)],
        2,
    )(idx, proj)
    att, den, attn_rows = call(
        attend_kernel,
        [
            jax.ShapeDtypeStruct((ROWS, VW), f32),
            jax.ShapeDtypeStruct((ROWS, LOCAL_HEADS), f32),
            jax.ShapeDtypeStruct((ROWS, VW), bf16),
        ],
        [pltpu.VMEM((ROWS, PW), bf16)],
        5,
    )(idx, proj, num, after(den, attn_w), state)

    middle, spread_two = on_rows(
        norm_kernel, scatter_rows(rows_of(halves_of(attn_rows), out_w, ((1,), (1,)))), inputs
    )
    acts_two = gather_rows(spread_two)
    hid0, hid1, gu0, gu1, gateup_w, down_w = mlp(place, acts_two, grad_mlp, every_mlp)
    hidden = [hid0, hid1]
    grad_gate_up = [gu0, gu1]

    late = []

    def mlp_grads(send, low):
        mlp_grad = grads(
            mlp_grads_kernel, 3 * FFP, place, low, acts_two, (*grad_gate_up, *hidden), 3 * FFP,
            split=(grad_mlp,),
        ).reshape(N_GROUPS * 3 * FFP, CHUNK)
        late.append(mlp_grad)

    grad_mid, spread_grad = on_rows(
        norm_back_kernel, scatter_rows(rows_of(grad_gate_up, gateup_w, ((1,), (1,))), mlp_grads), middle, cot
    )
    mlp_grad = lax.psum_scatter(after(late[0], grad_mid), GROUPS, scatter_dimension=0, tiled=True)
    grad_attn = gather_rows(spread_grad)
    grad_low = jnp.concatenate([matmul(a, out_w).astype(bf16) for a in grad_attn])
    own_grad, gn, gd = call(
        query_state_kernel,
        [
            jax.ShapeDtypeStruct((STATE_ROWS, DV), f32),
            jax.ShapeDtypeStruct((ROWS, VW), f32),
            jax.ShapeDtypeStruct((ROWS, LOCAL_HEADS), f32),
        ],
        [pltpu.VMEM((ROWS, PW), bf16), pltpu.VMEM((ROWS, VW), bf16)],
        5,
    )(idx, proj, grad_low, att, den)
    den_part = jnp.sum(jnp.abs(den))
    slices = exchange(
        jnp.concatenate(
            [
                own_grad.reshape(N_GROUPS, STATE_ROWS // N_GROUPS, DV),
                jnp.full((N_GROUPS, 8, DV), den_part, f32),
            ],
            axis=1,
        )
    )
    den_group = jnp.sum(slices[:, STATE_ROWS // N_GROUPS :], axis=0)
    slices = jnp.sum(back[:, :, None, None] * slices[None, :, : STATE_ROWS // N_GROUPS], axis=1)
    output_grad = grads(out_grads_kernel, VW, place, slices, grad_attn, (attn_rows,), VW)
    grad_state = exchange(slices).reshape(STATE_ROWS, DV)
    gqk, gv = call(
        attend_back_inside_kernel,
        [jax.ShapeDtypeStruct((ROWS, QK), f32), jax.ShapeDtypeStruct((ROWS, VW), f32)],
        [pltpu.VMEM((ROWS, PW), bf16)],
        4,
    )(idx, proj, gn, gd)
    mlp_grad_own = cross(after(mlp_grad, grad_state))
    grad_proj = call(
        attend_back_kernel,
        [jax.ShapeDtypeStruct((ROWS, PW), bf16)],
        [pltpu.VMEM((ROWS, PW), bf16), pltpu.VMEM((ROWS, QK), f32), pltpu.VMEM((ROWS, VW), f32)],
        8,
    )(idx, proj, gn, after(gd, output_grad), gqk, gv, state, grad_state)[0]

    def proj_grads(send, low):
        attn_grad = grads(
            proj_grads_kernel, VW + PW, place, place, acts_one, (grad_proj,), PW, (output_grad,)
        ).reshape(N_GROUPS, VW + PW, CHUNK)
        late.append(exchange(attn_grad))
        mixed_parts = [
            matmul(after(a, low), down_w, ((1,), (1,))).astype(bf16) for a in hidden
        ]
        other = swap_core(mixed_parts[1])
        late.append((mixed_parts[0].astype(f32) + other.astype(f32)).astype(bf16))


    shaped_one = scatter_rows(rows_of(halves_of(grad_proj), proj_w, ((1,), (1,))), proj_grads, sum_rows_apart)
    mixed = middle + sum_rows_apart(after(late[2], shaped_one))
    mixed = cross(mixed.astype(bf16))
    grad_tokens = grad_mid + unit_norm_back(shaped_one, unit_one, inv_one)
    grad_tokens = cross(grad_tokens.astype(bf16)).astype(f32)
    deep = plain(
        adam_mlp_kernel,
        same(*flat, down_weight, down_first, down_second),
        mlp_grad_own, gain_low, *flat, down_weight, down_first, down_second,
    )
    attn_grad = jnp.sum(after(late[1], deep[0]).astype(f32), axis=0)
    gain_one = jnp.sum(attn_grad[VW:] * first_own, axis=0)
    gain_two = jnp.sum(mlp_grad[: 2 * FFP].astype(f32) * gateup_own.astype(f32), axis=0)
    small = jnp.concatenate([gain_one[None], gain_two[None], den_group[:6]], axis=0)
    parts = lax.all_to_all(
        jnp.broadcast_to(small[None], (16, 8, CHUNK)), ("core", "y", "x_hi"), 0, 0
    ).reshape(8, 2, 8, CHUNK)
    small = jnp.sum(jnp.where(core == 0, parts[:, 0], parts[:, 1]), axis=0)
    attn_grad = cross(attn_grad.astype(bf16))

    gain_total = small[:2] / gain_low
    den_mean = small[2, 0] / (N_GROUPS * ROWS * HEADS)
    near = (*thin, value_weight, value_first, value_second, output_weight, output_first, output_second)
    near = plain(adam_attn_kernel, same(*near), attn_grad, gain_low, *near)
    news = list(adam_step(gains, gain_first, gain_second, gain_total, gain_rate))
    news += [jnp.transpose(a.reshape(2, QK // 2, CHUNK), (2, 0, 1)) for a in near[:3]]
    news += near[3:]
    news += [jnp.transpose(a, (2, 0, 1)) for a in deep[:3]]
    news += deep[3:]
    return (mixed, grad_tokens, den_mean) + tuple(news)


def solution(mesh):
    fine = jax.sharding.Mesh(mesh.devices.reshape(2, 4, 2, 4, 2), FINE)
    dp = ("x_lo", "z", "core")
    tensor = ("y", "x_hi")
    rows = P(FINE, None)
    gain = P(None, dp)
    deep = P(dp, None, tensor)
    down = P(dp, tensor)
    across = P(tensor, dp)
    return jax.shard_map(
        shards,
        mesh=fine,
        in_specs=(rows, rows, P())
        + (gain,) * 3
        + (deep,) * 3
        + (down,) * 3
        + (across,) * 3
        + (deep,) * 3
        + (across,) * 3,
        out_specs=(rows, rows, P())
        + (gain,) * 3
        + (deep,) * 3
        + (down,) * 3
        + (across,) * 3
        + (deep,) * 3
        + (across,) * 3,
        check_vma=False,
    )
```

```python
import functools

import jax
import jax.numpy as jnp
import numpy as np
from jax import lax
from jax.experimental import pallas as pl
from jax.experimental.pallas import tpu as pltpu
from jax.sharding import PartitionSpec as P

D = 2048
HEADS = 16
FEAT = 16
DV = 128
FF = 5504
STEP = 10
FINE = ("x_lo", "z", "core", "y", "x_hi")
GROUPS = ("x_hi", "x_lo", "z")
N_GROUPS = 16
ROWS = 1024
CHUNK = 128
HALF = ROWS // 2
LOCAL_HEADS = 2
QK = 2 * LOCAL_HEADS * FEAT
VW = LOCAL_HEADS * DV
PW = VW + QK
FFL = 688
FFP = 768
AW = 640
PHI = 256
PHI_ROWS = 160
HEAD_ROWS = 192
STATE_ROWS = LOCAL_HEADS * HEAD_ROWS
TILE = 256

norm_eps = 1e-05
beta_one = 0.5
beta_two = 0.5
adam_eps = 1e-08
weight_decay = 0.01
gain_rate = 0.5

f32 = jnp.float32
bf16 = jnp.bfloat16


FLIP = [(0, 1), (1, 0)]
CROSS = [(0, 0), (1, 2), (2, 1), (3, 3)]


def cross(a):
    return lax.ppermute(a, ("core", "x_hi"), CROSS)


def swap_core(a):
    return lax.ppermute(a, "core", FLIP)


def over_y(a):
    return lax.all_to_all(a, "y", 0, 0)


def spread(mine):
    return jnp.broadcast_to(mine[None], (4,) + mine.shape)


def to_y(a, step):
    return lax.ppermute(a, "y", [(i, (i + step) % 4) for i in range(4)])


def gather_rows(spread_rows):
    own = over_y(spread_rows).reshape(HALF, -1)
    return own, swap_core(own)


def parts_of_rows(low):
    return over_y(low.reshape(4, CHUNK, D))


def norm_kernel(parts_ref, inputs_ref, middle_ref, out_ref):
    middle = inputs_ref[...].astype(f32)
    for k in range(4):
        middle = middle + parts_ref[k].astype(f32)
    middle_ref[...] = middle
    inv = lax.rsqrt(jnp.mean(middle * middle, axis=-1, keepdims=True) + norm_eps)
    low = (middle * inv).astype(bf16)
    for k in range(4):
        out_ref[k] = low


def norm_back_kernel(parts_ref, middle_ref, cot_ref, grad_ref, out_ref):
    middle = middle_ref[...]
    inv = lax.rsqrt(jnp.mean(middle * middle, axis=-1, keepdims=True) + norm_eps)
    unit = middle * inv
    shaped = parts_ref[0].astype(f32)
    for k in range(1, 4):
        shaped = shaped + parts_ref[k].astype(f32)
    grad = cot_ref[...].astype(f32) + inv * (
        shaped - unit * jnp.mean(shaped * unit, axis=-1, keepdims=True)
    )
    grad_ref[...] = grad
    low = grad.astype(bf16)
    for k in range(4):
        out_ref[k] = low


def on_rows(kernel, *args):
    return pl.pallas_call(
        kernel,
        out_shape=[
            jax.ShapeDtypeStruct((CHUNK, D), f32),
            jax.ShapeDtypeStruct((4, CHUNK, D), bf16),
        ],
        compiler_params=pltpu.CompilerParams(vmem_limit_bytes=32 * 1024 * 1024),
    )(*args)


def sum_rows_apart(low):
    y = lax.axis_index("y")

    def part(step):
        return lax.dynamic_slice(low, ((y + step) % 4 * CHUNK, 0), (CHUNK, D))

    parts = [to_y(part(step), step) for step in (1, 2, 3)]
    out = part(0).astype(f32)
    for a in parts:
        out = out + a.astype(f32)
    return out


def scatter_rows(partial, between=None, total=parts_of_rows, later=None):
    send = partial(1, None)
    got = swap_core(send)
    if later is not None:
        got = after(got, later)
    low = partial(0, got)
    if between is not None:
        between(send, low)
    return total(low)


def rows_of(halves, weight, dims):
    def partial(half, more):
        total = matmul(halves[half], weight, dims)
        if more is not None:
            total = total + more.astype(f32)
        return total.astype(bf16)

    return partial


def halves_of(a):
    return a[:HALF], a[HALF:]


def matmul(a, b, dims=((1,), (0,))):
    return lax.dot_general(a, b, (dims, ((), ())), preferred_element_type=f32)


def iota(shape, dim):
    return lax.broadcasted_iota(jnp.int32, shape, dim)


def sides_of(kind, head):
    base = (kind * LOCAL_HEADS + head) * FEAT
    row = iota((QK, PHI), 0) - base
    col = iota((QK, PHI), 1)
    a = col % FEAT
    pair = col < 136
    one = (row == a) & (pair | ((col >= 144) & (col < PHI_ROWS)))
    two = (row == (a + col // FEAT) % FEAT) & pair
    return one.astype(f32).astype(bf16), two.astype(f32).astype(bf16)


def feature_rows():
    col = iota((1, PHI), 1)
    only = (col == 136).astype(f32)
    linear = ((col >= 144) & (col < PHI_ROWS)).astype(f32)
    square = (col < FEAT).astype(f32)
    cross_term = ((col >= FEAT) & (col < 136)).astype(f32)
    scale = (
        only
        + linear * FEAT ** (-0.25)
        + (square + cross_term * 2.0**0.5) * (2.0 * FEAT) ** (-0.5)
    )
    return only, only + linear, scale


def mover(kind, head):
    base = (kind * LOCAL_HEADS + head) * FEAT
    other = ((1 - kind) * LOCAL_HEADS + head) * FEAT
    row = iota((QK, QK), 0)
    col = iota((QK, QK), 1)
    hit = (row - base == col - other) & (row >= base) & (row < base + FEAT)
    return (hit.astype(f32) * FEAT ** (-0.5)).astype(bf16)


def doc_at(info_ref, pos):
    return sum((pos >= info_ref[8 + i]).astype(jnp.int32) for i in range(3))


def doc_column(info_ref, lo, hi):
    return doc_at(info_ref, info_ref[11] + lo + iota((hi - lo, 1), 0))


def is_last(info_ref, lo, hi):
    return (doc_column(info_ref, lo, hi) == info_ref[12]).astype(f32)


def continues(info_ref, lo, hi):
    return (doc_column(info_ref, lo, hi) == info_ref[13]).astype(f32)


def allowed_at(info_ref, r, end):
    at = r + iota((TILE, end), 0)
    of = iota((TILE, end), 1)
    doc_row = doc_at(info_ref, info_ref[11] + iota((1, end), 1))
    return (of <= at) & (doc_column(info_ref, r, end) == doc_row)


def split(a):
    hi = a.astype(bf16)
    return hi, (a - hi.astype(f32)).astype(bf16)


def dot_low(a, b, dims):
    hi, lo = split(a)
    return matmul(hi, b, dims) + matmul(lo, b, dims)


def dot_full(a, b, dims):
    ah, al = split(a)
    bh, bl = split(b)
    return matmul(ah, bh, dims) + (matmul(al, bh, dims) + matmul(ah, bl, dims))


def side(u, kind, head):
    left, right = sides_of(kind, head)
    one, two, scale = feature_rows()
    return matmul(u, left) + one, matmul(u, right) + two, scale


def to_order(idx_ref, src_ref, dst):
    for i in range(8):
        dst[pl.ds(i * CHUNK, CHUNK), :] = src_ref[
            pl.ds(pl.multiple_of(idx_ref[i] * CHUNK, CHUNK), CHUNK), :
        ]


def from_order(idx_ref, i, dst_ref, block):
    dst_ref[pl.ds(pl.multiple_of(idx_ref[i] * CHUNK, CHUNK), CHUNK), :] = block


def state_rows(ref, head):
    base = head * HEAD_ROWS
    mat = jnp.concatenate(
        [ref[base : base + PHI_ROWS, :], jnp.zeros((PHI - PHI_ROWS, DV), f32)], axis=0
    )
    vec = jnp.concatenate(
        [ref[base + PHI_ROWS : base + PHI_ROWS + 1, :], ref[base + PHI_ROWS + 1 : base + PHI_ROWS + 2, :]],
        axis=1,
    )
    return mat, vec


def store_state(ref, head, mat, vec):
    base = head * HEAD_ROWS
    ref[base : base + PHI_ROWS, :] = mat[:PHI_ROWS]
    tail = jnp.concatenate(
        [vec[:, :DV], vec[:, DV:], jnp.zeros((HEAD_ROWS - PHI_ROWS - 2, DV), f32)], axis=0
    )
    ref[base + PHI_ROWS : base + HEAD_ROWS, :] = tail


def key_state_kernel(idx_ref, p_ref, out_ref, scr):
    to_order(idx_ref, p_ref, scr)
    for head in range(LOCAL_HEADS):
        mat = jnp.zeros((PHI, DV), f32)
        vec = jnp.zeros((1, PHI), f32)
        for r in range(0, ROWS, TILE):
            u = scr[r : r + TILE, VW:PW]
            v = scr[r : r + TILE, head * DV : (head + 1) * DV]
            one, two, scale = side(u, 1, head)
            phi = one * two * scale * is_last(idx_ref, r, r + TILE)
            mat = mat + dot_low(phi, v, ((0,), (0,)))
            vec = vec + jnp.sum(phi, axis=0, keepdims=True)
        store_state(out_ref, head, mat, vec)


def attend_inside_kernel(
    idx_ref, p_ref, num_ref, den_ref, scr,
):
    to_order(idx_ref, p_ref, scr)
    u_all = scr[:, VW:PW]
    for head in range(LOCAL_HEADS):
        cols = slice(head * DV, (head + 1) * DV)
        v_all = scr[:, cols]
        for r in range(0, ROWS, TILE):
            end = r + TILE
            moved = matmul(scr[r:end, VW:PW], mover(0, head)).astype(bf16)
            s = matmul(moved, u_all[:end], ((1,), (1,)))
            allowed = allowed_at(idx_ref, r, end)
            kern = jnp.where(allowed, 1.0 + s + 0.5 * s * s, 0.0)
            num_ref[r:end, cols] = matmul(kern.astype(bf16), v_all[:end])
            den_ref[r:end, head : head + 1] = jnp.sum(kern, axis=1, keepdims=True)


def attend_kernel(
    idx_ref, p_ref, num_ref, den_in_ref, state_ref,
    att_ref, den_ref, low_ref, scr,
):
    to_order(idx_ref, p_ref, scr)
    for head in range(LOCAL_HEADS):
        cols = slice(head * DV, (head + 1) * DV)
        mat, vec = state_rows(state_ref, head)
        for r in range(0, ROWS, TILE):
            end = r + TILE
            cont = continues(idx_ref, r, end)
            one, two, scale = side(scr[r:end, VW:PW], 0, head)
            phi = one * two * scale
            num = num_ref[r:end, cols] + cont * dot_full(phi, mat, ((1,), (0,)))
            den = den_in_ref[r:end, head : head + 1] + cont * jnp.sum(phi * vec, axis=1, keepdims=True)
            att_ref[r:end, cols] = num / den
            den_ref[r:end, head : head + 1] = den
    for i in range(8):
        from_order(idx_ref, i, low_ref, att_ref[i * CHUNK : (i + 1) * CHUNK, :].astype(bf16))


def query_state_kernel(
    idx_ref, p_ref, ga_ref, att_ref, den_ref,
    out_ref, gn_ref, gd_ref, scr, gscr,
):
    to_order(idx_ref, p_ref, scr)
    to_order(idx_ref, ga_ref, gscr)
    for head in range(LOCAL_HEADS):
        mat = jnp.zeros((PHI, DV), f32)
        vec = jnp.zeros((1, PHI), f32)
        cols = slice(head * DV, (head + 1) * DV)
        for r in range(0, ROWS, TILE):
            end = r + TILE
            den = den_ref[r:end, head : head + 1]
            ga = gscr[r:end, cols].astype(f32)
            gn = ga / den
            gd = -jnp.sum(ga * att_ref[r:end, cols], axis=1, keepdims=True) / den
            gn_ref[r:end, cols] = gn.astype(bf16)
            gd_ref[r:end, head : head + 1] = gd
            one, two, scale = side(scr[r:end, VW:PW], 0, head)
            phi = one * two * scale * continues(idx_ref, r, end)
            mat = mat + dot_full(phi, gn, ((0,), (0,)))
            vec = vec + jnp.sum(phi * gd, axis=0, keepdims=True)
        store_state(out_ref, head, mat, vec)


def attend_back_inside_kernel(
    idx_ref, p_ref, gn_ref, gd_ref, gqk, gv, scr,
):
    to_order(idx_ref, p_ref, scr)
    u_all = scr[:, VW:PW]
    gqk[...] = jnp.zeros((ROWS, QK), f32)
    gv[...] = jnp.zeros((ROWS, VW), f32)
    for head in range(LOCAL_HEADS):
        cols = slice(head * DV, (head + 1) * DV)
        v_all = scr[:, cols]
        back_all = matmul(u_all, mover(1, head)).astype(bf16)
        for r in range(0, ROWS, TILE):
            end = r + TILE
            low_gn = gn_ref[r:end, cols]
            gd = gd_ref[r:end, head : head + 1]
            moved = matmul(scr[r:end, VW:PW], mover(0, head)).astype(bf16)
            s = matmul(moved, u_all[:end], ((1,), (1,)))
            allowed = allowed_at(idx_ref, r, end)
            kern = jnp.where(allowed, 1.0 + s + 0.5 * s * s, 0.0).astype(bf16)
            gk = matmul(low_gn, v_all[:end], ((1,), (1,))) + gd
            gs = jnp.where(allowed, gk * (1.0 + s), 0.0).astype(bf16)
            gqk[r:end, :] = gqk[r:end, :] + matmul(gs, back_all[:end])
            gqk[:end, :] = gqk[:end, :] + matmul(gs, moved, ((0,), (0,)))
            gv[:end, cols] = gv[:end, cols] + matmul(kern, low_gn, ((0,), (0,)))


def attend_back_kernel(
    idx_ref, p_ref, gn_ref, gd_ref, gqk_ref, gv_ref, state_ref, grad_state_ref,
    out_ref, scr, gqk, gv,
):
    to_order(idx_ref, p_ref, scr)
    for head in range(LOCAL_HEADS):
        cols = slice(head * DV, (head + 1) * DV)
        mat, vec = state_rows(state_ref, head)
        gmat, gvec = state_rows(grad_state_ref, head)
        for r in range(0, ROWS, TILE):
            end = r + TILE
            u = scr[r:end, VW:PW]
            cont = continues(idx_ref, r, end)
            in_last = is_last(idx_ref, r, end)
            gn = gn_ref[r:end, cols]
            gd = gd_ref[r:end, head : head + 1]
            one, two, scale = side(u, 0, head)
            left, right = sides_of(0, head)
            grad = (dot_low_right(gn, mat) + gd * vec) * cont * scale
            acc = matmul((grad * two).astype(bf16), left, ((1,), (1,)))
            acc = acc + matmul((grad * one).astype(bf16), right, ((1,), (1,)))
            one, two, scale = side(u, 1, head)
            left, right = sides_of(1, head)
            grad = (dot_low_right(scr[r:end, cols], gmat) + gvec) * in_last * scale
            acc = acc + matmul((grad * two).astype(bf16), left, ((1,), (1,)))
            acc = acc + matmul((grad * one).astype(bf16), right, ((1,), (1,)))
            phi = one * two * scale * in_last
            before = gqk_ref if head == 0 else gqk
            gqk[r:end, :] = before[r:end, :] + acc
            gv[r:end, cols] = gv_ref[r:end, cols] + dot_low(phi, gmat.astype(bf16), ((1,), (0,)))
    for i in range(8):
        chunk = slice(i * CHUNK, (i + 1) * CHUNK)
        from_order(
            idx_ref, i, out_ref,
            jnp.concatenate([gv[chunk, :], gqk[chunk, :]], axis=1).astype(bf16),
        )


def dot_low_right(a, b):
    hi, lo = split(b)
    return matmul(a, hi, ((1,), (1,))) + matmul(a, lo, ((1,), (1,)))


def call(kernel, outs, scratch, n_in):
    return pl.pallas_call(
        kernel,
        out_shape=outs,
        in_specs=[pl.BlockSpec(memory_space=pltpu.SMEM)]
        + [pl.BlockSpec(memory_space=pltpu.VMEM)] * (n_in - 1),
        out_specs=[pl.BlockSpec(memory_space=pltpu.VMEM)] * len(outs),
        scratch_shapes=scratch,
        compiler_params=pltpu.CompilerParams(vmem_limit_bytes=48 * 1024 * 1024),
    )


def adam_step(weight, moment_one, moment_two, reduced, step_rate):
    new_one = beta_one * moment_one + (1.0 - beta_one) * reduced
    new_two = beta_two * moment_two + (1.0 - beta_two) * reduced * reduced
    corrected_one = new_one / (1.0 - beta_one**STEP)
    corrected_two = new_two / (1.0 - beta_two**STEP)
    master = weight - step_rate * (
        corrected_one / (jnp.sqrt(corrected_two) + adam_eps) + weight_decay * weight
    )
    return (new_one, new_two, master)


def nothing_kernel(other_ref, a_ref, out_ref):
    pass


def after(a, other):
    return pl.pallas_call(
        nothing_kernel,
        out_shape=jax.ShapeDtypeStruct(a.shape, a.dtype),
        in_specs=[pl.BlockSpec(memory_space=pl.ANY)] * 2,
        out_specs=pl.BlockSpec(memory_space=pl.ANY),
        input_output_aliases={1: 0},
    )(other, a)


def pack_first_kernel(value_ref, feature_ref, output_ref, gain_row_ref, gain_col_ref, out_ref):
    def low(a):
        return a.astype(bf16).astype(f32)

    out_ref[:, :VW] = low(output_ref[...]).T.astype(bf16)
    out_ref[:, VW : 2 * VW] = (low(value_ref[...]) * gain_col_ref[:, 0:1]).astype(bf16)
    out_ref[:, 2 * VW : VW + PW] = (low(feature_ref[...]) * gain_row_ref[0:1]).T.astype(bf16)
    out_ref[:, VW + PW :] = jnp.zeros((CHUNK, AW - VW - PW), bf16)


def pack_mlp_kernel(gateup_ref, down_ref, gain_row_ref, out_ref):
    def low(a):
        return a.astype(bf16).astype(f32)

    def wide(a):
        return jnp.concatenate([a, jnp.zeros((FFP - FFL, CHUNK), f32)], axis=0).T.astype(bf16)

    out_ref[:, :FFP] = wide(low(gateup_ref[0]) * gain_row_ref[1:2])
    out_ref[:, FFP : 2 * FFP] = wide(low(gateup_ref[1]) * gain_row_ref[1:2])
    out_ref[:, 2 * FFP :] = wide(low(down_ref[...]))


def adam_store(weight, first, second, grad, rate, outs, at=()):
    place = at if at else (slice(None), slice(None))
    for ref, new in zip(outs, adam_step(weight[place], first[place], second[place], grad, rate)):
        ref[place] = new


def adam_mlp_kernel(
    grad_ref, gain_row_ref, gw, gf, gs, dw, df, ds, g1, g2, g3, d1, d2, d3
):
    for part in range(2):
        grad = grad_ref[part * FFP : part * FFP + FFL].astype(f32)
        adam_store(
            gw, gf, gs, grad * gain_row_ref[1:2], D ** (-0.5), (g1, g2, g3),
            (part, slice(None), slice(None)),
        )
    adam_store(dw, df, ds, grad_ref[2 * FFP : 2 * FFP + FFL].astype(f32), FF ** (-0.5), (d1, d2, d3))


def adam_attn_kernel(
    grad_ref, gain_row_ref,
    fw, ff, fs, vw, vf, vs, ow, of, os, f1, f2, f3, v1, v2, v3, o1, o2, o3,
):
    grad = (grad_ref[VW : 2 * VW].astype(f32) * gain_row_ref[0:1]).T
    adam_store(vw, vf, vs, grad, D ** (-0.5), (v1, v2, v3))
    grad = grad_ref[2 * VW :].astype(f32) * gain_row_ref[0:1]
    adam_store(fw, ff, fs, grad, D ** (-0.5), (f1, f2, f3))
    grad = grad_ref[:VW].astype(f32)
    adam_store(ow, of, os, grad, (HEADS * DV // 64) ** (-0.5), (o1, o2, o3))


def turned(a):
    return a.astype(f32).T.astype(bf16)


def store_owners(out_ref, lo, hi, tile):
    for k in range(2):
        out_ref[k, 0, lo:hi, :] = tile[:, k * CHUNK : (k + 1) * CHUNK].astype(bf16)


def mlp_grads_kernel(core_ref, other_ref, a0, a1, g0, g1, gu0, gu1, h0, h1, out_ref, scr):
    @pl.when(pl.program_id(0) == 0)
    def turn():
        for half, (gu, h) in enumerate(((gu0, h0), (gu1, h1))):
            cols = slice(half * HALF, (half + 1) * HALF)
            for j in range(FFP // TILE):
                rows = slice(j * TILE, (j + 1) * TILE)
                later = slice(FFP + j * TILE, FFP + (j + 1) * TILE)
                scr[rows, cols] = turned(gu[:, 2 * j * TILE : (2 * j + 1) * TILE])
                scr[later, cols] = turned(gu[:, (2 * j + 1) * TILE : (2 * j + 2) * TILE])
            scr[2 * FFP :, cols] = turned(h[...])

    for lo, hi, left, right in ((0, 2 * FFP, a0, a1), (2 * FFP, 3 * FFP, g0.at[0], g1.at[0])):
        tile = matmul(scr[lo:hi, :HALF], left[...]) + matmul(scr[lo:hi, HALF:], right[...])
        store_owners(out_ref, lo, hi, tile)


def attn_grads_kernel(core_ref, other_ref, a0, a1, g0, g1, rows_ref, proj_ref, out_ref, scr):
    @pl.when(pl.program_id(0) == 0)
    def turn():
        scr[:VW] = turned(rows_ref[...])
        scr[VW : 2 * VW] = turned(proj_ref[:, :VW])
        scr[2 * VW :] = turned(proj_ref[:, VW:])

    for lo, hi, left, right in ((0, VW, g0, g1), (VW, VW + PW, a0, a1)):
        tile = matmul(scr[lo:hi, :HALF], left[...]) + matmul(scr[lo:hi, HALF:], right[...])
        store_owners(out_ref, lo, hi, tile)


def grads(kernel, height, place, other, tiled, whole, turned_rows, blocks=(), split=()):
    def by_owner(n):
        return pl.BlockSpec((2, 1, n, CHUNK), lambda i, core: (0, i, 0, 0))

    def full(a):
        return pl.BlockSpec(a.shape, lambda i, core: (0,) * a.ndim)

    in_specs = [pl.BlockSpec(memory_space=pl.ANY)]
    in_specs += [pl.BlockSpec((HALF, TILE), lambda i, core: (0, i))] * len(tiled)
    operands = list(tiled)
    for a in split:
        in_specs += [
            pl.BlockSpec((1, HALF, TILE), lambda i, core: (core[0], 0, i)),
            pl.BlockSpec((1, HALF, TILE), lambda i, core: (1 - core[0], 0, i)),
        ]
        operands += [a, a]
    in_specs += [by_owner(a.shape[2]) for a in blocks] + [full(a) for a in whole]
    return pl.pallas_call(
        kernel,
        grid_spec=pltpu.PrefetchScalarGridSpec(
            num_scalar_prefetch=1,
            grid=(D // TILE,),
            in_specs=in_specs,
            out_specs=by_owner(height),
            scratch_shapes=[pltpu.VMEM((turned_rows, ROWS), bf16)],
        ),
        out_shape=jax.ShapeDtypeStruct((2, 8, height, CHUNK), bf16),
        compiler_params=pltpu.CompilerParams(vmem_limit_bytes=48 * 1024 * 1024),
    )(place, other, *operands, *blocks, *whole)


def mlp_kernel(
    core_ref, a0, a1, g0, g1, gate_ref, up_ref, down_ref,
    h0, h1, gu0, gu1, gateup_out, down_out,
):
    weights = [ref[0].reshape(D, TILE) for ref in (gate_ref, up_ref, down_ref)]
    gateup_out[:, :TILE] = weights[0]
    gateup_out[:, TILE:] = weights[1]
    down_out[...] = weights[2]
    for a, g, h, gu in ((a0, g0, h0, gu0), (a1, g1, h1, gu1)):
        gate = matmul(a[...], weights[0])
        up = matmul(a[...], weights[1])
        grad = matmul(g[0], weights[2])
        sigmoid = jax.nn.sigmoid(gate)
        silu = gate * sigmoid
        h[...] = (silu * up).astype(bf16)
        gu[:, :TILE] = (grad * up * (sigmoid * (1.0 + gate * (1.0 - sigmoid)))).astype(bf16)
        gu[:, TILE:] = (grad * silu).astype(bf16)


def mlp(place, acts, grad, every):
    steps = FFP // TILE

    def cols(part):
        return pl.BlockSpec(
            (1, N_GROUPS, CHUNK, TILE), lambda j, core: (core[0], 0, 0, part * steps + j)
        )

    hidden = pl.BlockSpec((HALF, TILE), lambda j, core: (0, j))

    def wide(n, width):
        return pl.BlockSpec((n, width), lambda j, core: (0, j))

    return pl.pallas_call(
        mlp_kernel,
        grid_spec=pltpu.PrefetchScalarGridSpec(
            num_scalar_prefetch=1,
            grid=(steps,),
            in_specs=[pl.BlockSpec((HALF, D), lambda j, core: (0, 0))] * 2
            + [
                pl.BlockSpec((1, HALF, D), lambda j, core: (core[0], 0, 0)),
                pl.BlockSpec((1, HALF, D), lambda j, core: (1 - core[0], 0, 0)),
                cols(0), cols(1), cols(2),
            ],
            out_specs=[hidden] * 2 + [wide(HALF, 2 * TILE)] * 2 + [wide(D, 2 * TILE), wide(D, TILE)],
        ),
        out_shape=[jax.ShapeDtypeStruct((HALF, FFP), bf16)] * 2
        + [jax.ShapeDtypeStruct((HALF, 2 * FFP), bf16)] * 2
        + [jax.ShapeDtypeStruct((D, 2 * FFP), bf16), jax.ShapeDtypeStruct((D, FFP), bf16)],
        compiler_params=pltpu.CompilerParams(vmem_limit_bytes=56 * 1024 * 1024),
    )(place, *acts, grad, grad, every, every, every)


def project_kernel(core_ref, a0, a1, w_ref, out_ref, acc):
    step = pl.program_id(0)

    @pl.when(step == 0)
    def start():
        acc[...] = jnp.zeros_like(acc)

    weight = w_ref[0].reshape(TILE, AW)[:, VW : VW + PW]
    acc[:HALF] += matmul(a0[...], weight)
    acc[HALF:] += matmul(a1[...], weight)

    @pl.when(step == D // TILE - 1)
    def end():
        out_ref[...] = acc[...].astype(bf16)


def project(core, acts, every):
    return pl.pallas_call(
        project_kernel,
        grid_spec=pltpu.PrefetchScalarGridSpec(
            num_scalar_prefetch=1,
            grid=(D // TILE,),
            in_specs=[pl.BlockSpec((HALF, TILE), lambda i, core: (0, i))] * 2
            + [pl.BlockSpec((1, 2, CHUNK, AW), lambda i, core: (core[0], i, 0, 0))],
            out_specs=pl.BlockSpec((ROWS, PW), lambda i, core: (0, 0)),
            scratch_shapes=[pltpu.VMEM((ROWS, PW), f32)],
        ),
        out_shape=jax.ShapeDtypeStruct((ROWS, PW), bf16),
        compiler_params=pltpu.CompilerParams(vmem_limit_bytes=48 * 1024 * 1024),
    )(core, *acts, every)


def plain(kernel, outs, *args):
    return pl.pallas_call(
        kernel,
        out_shape=outs,
        compiler_params=pltpu.CompilerParams(vmem_limit_bytes=48 * 1024 * 1024),
    )(*args)


def same(*arrays):
    return [jax.ShapeDtypeStruct(a.shape, f32) for a in arrays]


def unit_norm(rows):
    inv = lax.rsqrt(jnp.mean(rows * rows, axis=-1, keepdims=True) + norm_eps)
    return rows * inv, inv


def unit_norm_back(shaped, unit, inv):
    return inv * (shaped - unit * jnp.mean(shaped * unit, axis=-1, keepdims=True))


def exchange(a):
    return lax.all_to_all(a, GROUPS, 0, 0)


def shards(
    tokens, cotangent, row_lengths, gains, gain_first, gain_second,
    feature_weight, feature_first, feature_second,
    value_weight, value_first, value_second,
    output_weight, output_first, output_second,
    gateup_weight, gateup_first, gateup_second,
    down_weight, down_first, down_second,
):
    core = lax.axis_index("core")
    group = (lax.axis_index("x_lo") * 4 + lax.axis_index("z")) * 2 + lax.axis_index("x_hi")
    gain_low = gains.astype(bf16).astype(f32)
    place = jnp.reshape(core, (1,)).astype(jnp.int32)

    gain_col = gain_low.T
    flat = [jnp.transpose(a, (1, 2, 0)) for a in (gateup_weight, gateup_first, gateup_second)]
    thin = [
        jnp.transpose(a, (1, 2, 0)).reshape(QK, CHUNK)
        for a in (feature_weight, feature_first, feature_second)
    ]
    first_part = plain(
        pack_first_kernel,
        jax.ShapeDtypeStruct((CHUNK, AW), bf16),
        value_weight, thin[0], output_weight, gain_low, gain_col,
    )
    gateup_part = plain(
        pack_mlp_kernel,
        jax.ShapeDtypeStruct((CHUNK, 3 * FFP), bf16),
        flat[0], down_weight, gain_low,
    )

    def gather_weights(part):
        every = lax.all_gather(part, ("x_hi", "x_lo", "z", "core"))
        return every.reshape(2, N_GROUPS, CHUNK, part.shape[1])

    def own_slice(every):
        return lax.dynamic_index_in_dim(every, core, 0, False)

    owner = (lax.axis_index("x_lo") * 4 + lax.axis_index("z")) * 2 + lax.axis_index("x_hi")
    every_attn = gather_weights(first_part)
    both = cross(jnp.stack([tokens, cotangent]))
    tokens = both[0]
    cot = both[1]
    inputs = tokens.astype(f32)
    unit_one, inv_one = unit_norm(inputs)
    acts_one = gather_rows(spread(unit_one.astype(bf16)))
    grad_mlp = lax.all_gather(after(after(cot, acts_one[0]), every_attn), ("core", "y")).reshape(2, HALF, D)
    proj = project(place, acts_one, every_attn)
    attn_w = own_slice(after(every_attn, proj))
    first_own = lax.dynamic_index_in_dim(attn_w, owner, 0, False)[:, VW : VW + PW].astype(f32).T
    attn_w = attn_w.reshape(D, AW)
    out_w = attn_w[:, :VW]
    proj_w = attn_w[:, VW : VW + PW]

    ends = jnp.cumsum(row_lengths)

    def doc_of(pos):
        return jnp.sum((pos[..., None] >= ends).astype(jnp.int32), axis=-1)

    places = jnp.arange(N_GROUPS, dtype=jnp.int32)
    group_ids = (places % 8) * 2 + places // 8
    doc_end = doc_of(group_ids * ROWS + (ROWS - 1))
    doc_before = jnp.where(group_ids > 0, doc_of(group_ids * ROWS - 1), -1)
    last_doc = doc_of(group * ROWS + (ROWS - 1))
    before = jnp.where(group > 0, doc_of(group * ROWS - 1), -1)
    carry = ((group_ids[None, :] < group_ids[:, None]) & (doc_end[None, :] == doc_before[:, None])).astype(f32)
    back = ((group_ids[None, :] > group_ids[:, None]) & (doc_before[None, :] == doc_end[:, None])).astype(f32)
    chunk_ids = jnp.arange(8, dtype=jnp.int32)
    idx = ((chunk_ids % 2) ^ core) * 4 + chunk_ids // 2
    idx = jnp.concatenate([idx, ends, jnp.stack([group * ROWS, last_doc, before])]).astype(jnp.int32)

    own_state = call(
        key_state_kernel,
        [jax.ShapeDtypeStruct((STATE_ROWS, DV), f32)],
        [pltpu.VMEM((ROWS, PW), bf16)],
        2,
    )(idx, proj)[0]
    every_mlp = gather_weights(after(gateup_part, own_state))
    gateup_own = lax.dynamic_slice(
        every_mlp, (core, owner, 0, 0), (1, 1, CHUNK, 2 * FFP)
    ).reshape(CHUNK, 2 * FFP)
    gateup_own = gateup_own.T
    slices = exchange(own_state.reshape(N_GROUPS, STATE_ROWS // N_GROUPS, DV))
    slices = jnp.sum(carry[:, :, None, None] * slices[None], axis=1)
    state = exchange(slices).reshape(STATE_ROWS, DV)
    num, den = call(
        attend_inside_kernel,
        [jax.ShapeDtypeStruct((ROWS, VW), f32), jax.ShapeDtypeStruct((ROWS, LOCAL_HEADS), f32)],
        [pltpu.VMEM((ROWS, PW), bf16)],
        2,
    )(idx, proj)
    att, den, attn_rows = call(
        attend_kernel,
        [
            jax.ShapeDtypeStruct((ROWS, VW), f32),
            jax.ShapeDtypeStruct((ROWS, LOCAL_HEADS), f32),
            jax.ShapeDtypeStruct((ROWS, VW), bf16),
        ],
        [pltpu.VMEM((ROWS, PW), bf16)],
        5,
    )(idx, proj, num, after(den, attn_w), state)

    middle, spread_two = on_rows(
        norm_kernel, scatter_rows(rows_of(halves_of(attn_rows), out_w, ((1,), (1,)))), inputs
    )
    acts_two = gather_rows(spread_two)
    hid0, hid1, gu0, gu1, gateup_w, down_w = mlp(place, acts_two, grad_mlp, every_mlp)
    hidden = [hid0, hid1]
    grad_gate_up = [gu0, gu1]

    late = []

    def mlp_grads(send, low):
        mlp_grad = grads(
            mlp_grads_kernel, 3 * FFP, place, low, acts_two, (*grad_gate_up, *hidden), 3 * FFP,
            split=(grad_mlp,),
        ).reshape(N_GROUPS * 3 * FFP, CHUNK)
        late.append(mlp_grad)

    grad_mid, spread_grad = on_rows(
        norm_back_kernel, scatter_rows(rows_of(grad_gate_up, gateup_w, ((1,), (1,))), mlp_grads), middle, cot
    )
    mlp_grad = lax.psum_scatter(after(late[0], grad_mid), GROUPS, scatter_dimension=0, tiled=True)
    grad_attn = gather_rows(spread_grad)
    grad_low = jnp.concatenate([matmul(a, out_w).astype(bf16) for a in grad_attn])
    own_grad, gn, gd = call(
        query_state_kernel,
        [
            jax.ShapeDtypeStruct((STATE_ROWS, DV), f32),
            jax.ShapeDtypeStruct((ROWS, VW), bf16),
            jax.ShapeDtypeStruct((ROWS, LOCAL_HEADS), f32),
        ],
        [pltpu.VMEM((ROWS, PW), bf16), pltpu.VMEM((ROWS, VW), bf16)],
        5,
    )(idx, proj, grad_low, att, den)
    den_part = jnp.sum(jnp.abs(den))
    slices = exchange(
        jnp.concatenate(
            [
                own_grad.reshape(N_GROUPS, STATE_ROWS // N_GROUPS, DV),
                jnp.full((N_GROUPS, 8, DV), den_part, f32),
            ],
            axis=1,
        )
    )
    den_group = jnp.sum(slices[:, STATE_ROWS // N_GROUPS :], axis=0)
    slices = jnp.sum(back[:, :, None, None] * slices[None, :, : STATE_ROWS // N_GROUPS], axis=1)
    grad_state = exchange(slices).reshape(STATE_ROWS, DV)
    gqk, gv = call(
        attend_back_inside_kernel,
        [jax.ShapeDtypeStruct((ROWS, QK), f32), jax.ShapeDtypeStruct((ROWS, VW), f32)],
        [pltpu.VMEM((ROWS, PW), bf16)],
        4,
    )(idx, proj, gn, gd)
    mlp_grad_own = cross(after(mlp_grad, grad_state))
    grad_proj = call(
        attend_back_kernel,
        [jax.ShapeDtypeStruct((ROWS, PW), bf16)],
        [pltpu.VMEM((ROWS, PW), bf16), pltpu.VMEM((ROWS, QK), f32), pltpu.VMEM((ROWS, VW), f32)],
        8,
    )(idx, proj, gn, gd, gqk, gv, state, grad_state)[0]

    def proj_grads(send, low):
        attn_grad = grads(
            attn_grads_kernel, VW + PW, place, place, acts_one + grad_attn,
            (attn_rows, grad_proj), VW + PW,
        ).reshape(N_GROUPS, VW + PW, CHUNK)
        late.append(exchange(attn_grad))
        mixed_parts = [
            matmul(after(a, low), down_w, ((1,), (1,))).astype(bf16) for a in hidden
        ]
        other = swap_core(mixed_parts[1])
        late.append((mixed_parts[0].astype(f32) + other.astype(f32)).astype(bf16))


    shaped_one = scatter_rows(rows_of(halves_of(grad_proj), proj_w, ((1,), (1,))), proj_grads, sum_rows_apart)
    mixed = middle + sum_rows_apart(after(late[2], shaped_one))
    mixed = cross(mixed.astype(bf16))
    grad_tokens = grad_mid + unit_norm_back(shaped_one, unit_one, inv_one)
    grad_tokens = cross(grad_tokens.astype(bf16)).astype(f32)
    deep = plain(
        adam_mlp_kernel,
        same(*flat, down_weight, down_first, down_second),
        mlp_grad_own, gain_low, *flat, down_weight, down_first, down_second,
    )
    attn_grad = jnp.sum(after(late[1], deep[0]).astype(f32), axis=0)
    gain_one = jnp.sum(attn_grad[VW:] * first_own, axis=0)
    gain_two = jnp.sum(mlp_grad[: 2 * FFP].astype(f32) * gateup_own.astype(f32), axis=0)
    small = jnp.concatenate([gain_one[None], gain_two[None], den_group[:6]], axis=0)
    parts = lax.all_to_all(
        jnp.broadcast_to(small[None], (16, 8, CHUNK)), ("core", "y", "x_hi"), 0, 0
    ).reshape(8, 2, 8, CHUNK)
    small = jnp.sum(jnp.where(core == 0, parts[:, 0], parts[:, 1]), axis=0)
    attn_grad = cross(attn_grad.astype(bf16))

    gain_total = small[:2] / gain_low
    den_mean = small[2, 0] / (N_GROUPS * ROWS * HEADS)
    near = (*thin, value_weight, value_first, value_second, output_weight, output_first, output_second)
    near = plain(adam_attn_kernel, same(*near), attn_grad, gain_low, *near)
    news = list(adam_step(gains, gain_first, gain_second, gain_total, gain_rate))
    news += [jnp.transpose(a.reshape(2, QK // 2, CHUNK), (2, 0, 1)) for a in near[:3]]
    news += near[3:]
    news += [jnp.transpose(a, (2, 0, 1)) for a in deep[:3]]
    news += deep[3:]
    return (mixed, grad_tokens, den_mean) + tuple(news)


def solution(mesh):
    fine = jax.sharding.Mesh(mesh.devices.reshape(2, 4, 2, 4, 2), FINE)
    dp = ("x_lo", "z", "core")
    tensor = ("y", "x_hi")
    rows = P(FINE, None)
    gain = P(None, dp)
    deep = P(dp, None, tensor)
    down = P(dp, tensor)
    across = P(tensor, dp)
    return jax.shard_map(
        shards,
        mesh=fine,
        in_specs=(rows, rows, P())
        + (gain,) * 3
        + (deep,) * 3
        + (down,) * 3
        + (across,) * 3
        + (deep,) * 3
        + (across,) * 3,
        out_specs=(rows, rows, P())
        + (gain,) * 3
        + (deep,) * 3
        + (down,) * 3
        + (across,) * 3
        + (deep,) * 3
        + (across,) * 3,
        check_vma=False,
    )
```

```python
import functools

import jax
import jax.numpy as jnp
import numpy as np
from jax import lax
from jax.experimental import pallas as pl
from jax.experimental.pallas import tpu as pltpu
from jax.sharding import PartitionSpec as P

D = 2048
HEADS = 16
FEAT = 16
DV = 128
FF = 5504
STEP = 10
FINE = ("x_lo", "z", "core", "y", "x_hi")
GROUPS = ("x_hi", "x_lo", "z")
N_GROUPS = 16
ROWS = 1024
CHUNK = 128
HALF = ROWS // 2
LOCAL_HEADS = 2
QK = 2 * LOCAL_HEADS * FEAT
VW = LOCAL_HEADS * DV
PW = VW + QK
FFL = 688
FFP = 768
AW = 640
PHI = 256
PHI_ROWS = 160
HEAD_ROWS = 192
STATE_ROWS = LOCAL_HEADS * HEAD_ROWS
TILE = 256
WIDE = 512

norm_eps = 1e-05
beta_one = 0.5
beta_two = 0.5
adam_eps = 1e-08
weight_decay = 0.01
gain_rate = 0.5

f32 = jnp.float32
bf16 = jnp.bfloat16


FLIP = [(0, 1), (1, 0)]
CROSS = [(0, 0), (1, 2), (2, 1), (3, 3)]


def cross(a):
    return lax.ppermute(a, ("core", "x_hi"), CROSS)


def swap_core(a):
    return lax.ppermute(a, "core", FLIP)


def over_y(a):
    return lax.all_to_all(a, "y", 0, 0)


def spread(mine):
    return jnp.broadcast_to(mine[None], (4,) + mine.shape)


def to_y(a, step):
    return lax.ppermute(a, "y", [(i, (i + step) % 4) for i in range(4)])


def gather_rows(spread_rows):
    own = over_y(spread_rows).reshape(HALF, -1)
    return own, swap_core(own)


def parts_of_rows(low):
    return over_y(low.reshape(4, CHUNK, D))


def norm_kernel(parts_ref, inputs_ref, middle_ref, out_ref):
    middle = inputs_ref[...].astype(f32)
    for k in range(4):
        middle = middle + parts_ref[k].astype(f32)
    middle_ref[...] = middle
    inv = lax.rsqrt(jnp.mean(middle * middle, axis=-1, keepdims=True) + norm_eps)
    low = (middle * inv).astype(bf16)
    for k in range(4):
        out_ref[k] = low


def norm_back_kernel(parts_ref, middle_ref, cot_ref, grad_ref, out_ref):
    middle = middle_ref[...]
    inv = lax.rsqrt(jnp.mean(middle * middle, axis=-1, keepdims=True) + norm_eps)
    unit = middle * inv
    shaped = parts_ref[0].astype(f32)
    for k in range(1, 4):
        shaped = shaped + parts_ref[k].astype(f32)
    grad = cot_ref[...].astype(f32) + inv * (
        shaped - unit * jnp.mean(shaped * unit, axis=-1, keepdims=True)
    )
    grad_ref[...] = grad
    low = grad.astype(bf16)
    for k in range(4):
        out_ref[k] = low


def on_rows(kernel, *args):
    return pl.pallas_call(
        kernel,
        out_shape=[
            jax.ShapeDtypeStruct((CHUNK, D), f32),
            jax.ShapeDtypeStruct((4, CHUNK, D), bf16),
        ],
        compiler_params=pltpu.CompilerParams(vmem_limit_bytes=32 * 1024 * 1024),
    )(*args)


def sum_rows_apart(low):
    y = lax.axis_index("y")

    def part(step):
        return lax.dynamic_slice(low, ((y + step) % 4 * CHUNK, 0), (CHUNK, D))

    parts = [to_y(part(step), step) for step in (1, 2, 3)]
    out = part(0).astype(f32)
    for a in parts:
        out = out + a.astype(f32)
    return out


def scatter_rows(partial, between=None, total=parts_of_rows, later=None):
    send = partial(1, None)
    got = swap_core(send)
    if later is not None:
        got = after(got, later)
    low = partial(0, got)
    if between is not None:
        between(send, low)
    return total(low)


def rows_of(halves, weight, dims):
    def partial(half, more):
        total = matmul(halves[half], weight, dims)
        if more is not None:
            total = total + more.astype(f32)
        return total.astype(bf16)

    return partial


def halves_of(a):
    return a[:HALF], a[HALF:]


def matmul(a, b, dims=((1,), (0,))):
    return lax.dot_general(a, b, (dims, ((), ())), preferred_element_type=f32)


def iota(shape, dim):
    return lax.broadcasted_iota(jnp.int32, shape, dim)


def sides_of(kind, head):
    base = (kind * LOCAL_HEADS + head) * FEAT
    row = iota((QK, PHI), 0) - base
    col = iota((QK, PHI), 1)
    a = col % FEAT
    pair = col < 136
    one = (row == a) & (pair | ((col >= 144) & (col < PHI_ROWS)))
    two = (row == (a + col // FEAT) % FEAT) & pair
    return one.astype(f32).astype(bf16), two.astype(f32).astype(bf16)


def feature_rows():
    col = iota((1, PHI), 1)
    only = (col == 136).astype(f32)
    linear = ((col >= 144) & (col < PHI_ROWS)).astype(f32)
    square = (col < FEAT).astype(f32)
    cross_term = ((col >= FEAT) & (col < 136)).astype(f32)
    scale = (
        only
        + linear * FEAT ** (-0.25)
        + (square + cross_term * 2.0**0.5) * (2.0 * FEAT) ** (-0.5)
    )
    return only, only + linear, scale


def mover(kind, head):
    base = (kind * LOCAL_HEADS + head) * FEAT
    other = ((1 - kind) * LOCAL_HEADS + head) * FEAT
    row = iota((QK, QK), 0)
    col = iota((QK, QK), 1)
    hit = (row - base == col - other) & (row >= base) & (row < base + FEAT)
    return (hit.astype(f32) * FEAT ** (-0.5)).astype(bf16)


def doc_at(info_ref, pos):
    return sum((pos >= info_ref[8 + i]).astype(jnp.int32) for i in range(3))


def doc_column(info_ref, lo, hi):
    return doc_at(info_ref, info_ref[11] + lo + iota((hi - lo, 1), 0))


def is_last(info_ref, lo, hi):
    return (doc_column(info_ref, lo, hi) == info_ref[12]).astype(f32)


def continues(info_ref, lo, hi):
    return (doc_column(info_ref, lo, hi) == info_ref[13]).astype(f32)


def allowed_at(info_ref, r, end):
    at = r + iota((TILE, end), 0)
    of = iota((TILE, end), 1)
    doc_row = doc_at(info_ref, info_ref[11] + iota((1, end), 1))
    return (of <= at) & (doc_column(info_ref, r, end) == doc_row)


def split(a):
    hi = a.astype(bf16)
    return hi, (a - hi.astype(f32)).astype(bf16)


def dot_low(a, b, dims):
    hi, lo = split(a)
    return matmul(hi, b, dims) + matmul(lo, b, dims)


def dot_full(a, b, dims):
    ah, al = split(a)
    bh, bl = split(b)
    return matmul(ah, bh, dims) + (matmul(al, bh, dims) + matmul(ah, bl, dims))


def side(u, kind, head):
    left, right = sides_of(kind, head)
    one, two, scale = feature_rows()
    return matmul(u, left) + one, matmul(u, right) + two, scale


def to_order(idx_ref, src_ref, dst):
    for i in range(8):
        dst[pl.ds(i * CHUNK, CHUNK), :] = src_ref[
            pl.ds(pl.multiple_of(idx_ref[i] * CHUNK, CHUNK), CHUNK), :
        ]


def from_order(idx_ref, i, dst_ref, block):
    dst_ref[pl.ds(pl.multiple_of(idx_ref[i] * CHUNK, CHUNK), CHUNK), :] = block


def state_rows(ref, head):
    base = head * HEAD_ROWS
    mat = jnp.concatenate(
        [ref[base : base + PHI_ROWS, :], jnp.zeros((PHI - PHI_ROWS, DV), f32)], axis=0
    )
    vec = jnp.concatenate(
        [ref[base + PHI_ROWS : base + PHI_ROWS + 1, :], ref[base + PHI_ROWS + 1 : base + PHI_ROWS + 2, :]],
        axis=1,
    )
    return mat, vec


def store_state(ref, head, mat, vec):
    base = head * HEAD_ROWS
    ref[base : base + PHI_ROWS, :] = mat[:PHI_ROWS]
    tail = jnp.concatenate(
        [vec[:, :DV], vec[:, DV:], jnp.zeros((HEAD_ROWS - PHI_ROWS - 2, DV), f32)], axis=0
    )
    ref[base + PHI_ROWS : base + HEAD_ROWS, :] = tail


def key_state_kernel(idx_ref, p_ref, out_ref, scr):
    to_order(idx_ref, p_ref, scr)
    for head in range(LOCAL_HEADS):
        mat = jnp.zeros((PHI, DV), f32)
        vec = jnp.zeros((1, PHI), f32)
        for r in range(0, ROWS, TILE):
            u = scr[r : r + TILE, VW:PW]
            v = scr[r : r + TILE, head * DV : (head + 1) * DV]
            one, two, scale = side(u, 1, head)
            phi = one * two * scale * is_last(idx_ref, r, r + TILE)
            mat = mat + dot_low(phi, v, ((0,), (0,)))
            vec = vec + jnp.sum(phi, axis=0, keepdims=True)
        store_state(out_ref, head, mat, vec)


def attend_inside_kernel(
    idx_ref, p_ref, num_ref, den_ref, scr,
):
    to_order(idx_ref, p_ref, scr)
    u_all = scr[:, VW:PW]
    for head in range(LOCAL_HEADS):
        cols = slice(head * DV, (head + 1) * DV)
        v_all = scr[:, cols]
        for r in range(0, ROWS, TILE):
            end = r + TILE
            moved = matmul(scr[r:end, VW:PW], mover(0, head)).astype(bf16)
            s = matmul(moved, u_all[:end], ((1,), (1,)))
            allowed = allowed_at(idx_ref, r, end)
            kern = jnp.where(allowed, 1.0 + s + 0.5 * s * s, 0.0)
            num_ref[r:end, cols] = matmul(kern.astype(bf16), v_all[:end])
            den_ref[r:end, head : head + 1] = jnp.sum(kern, axis=1, keepdims=True)


def attend_kernel(
    idx_ref, p_ref, num_ref, den_in_ref, state_ref,
    att_ref, den_ref, low_ref, scr,
):
    to_order(idx_ref, p_ref, scr)
    for head in range(LOCAL_HEADS):
        cols = slice(head * DV, (head + 1) * DV)
        mat, vec = state_rows(state_ref, head)
        for r in range(0, ROWS, TILE):
            end = r + TILE
            cont = continues(idx_ref, r, end)
            one, two, scale = side(scr[r:end, VW:PW], 0, head)
            phi = one * two * scale
            num = num_ref[r:end, cols] + cont * dot_full(phi, mat, ((1,), (0,)))
            den = den_in_ref[r:end, head : head + 1] + cont * jnp.sum(phi * vec, axis=1, keepdims=True)
            att_ref[r:end, cols] = num / den
            den_ref[r:end, head : head + 1] = den
    for i in range(8):
        from_order(idx_ref, i, low_ref, att_ref[i * CHUNK : (i + 1) * CHUNK, :].astype(bf16))


def query_state_kernel(
    idx_ref, p_ref, ga_ref, att_ref, den_ref,
    out_ref, gn_ref, gd_ref, scr, gscr,
):
    to_order(idx_ref, p_ref, scr)
    to_order(idx_ref, ga_ref, gscr)
    for head in range(LOCAL_HEADS):
        mat = jnp.zeros((PHI, DV), f32)
        vec = jnp.zeros((1, PHI), f32)
        cols = slice(head * DV, (head + 1) * DV)
        for r in range(0, ROWS, TILE):
            end = r + TILE
            den = den_ref[r:end, head : head + 1]
            ga = gscr[r:end, cols].astype(f32)
            gn = ga / den
            gd = -jnp.sum(ga * att_ref[r:end, cols], axis=1, keepdims=True) / den
            gn_ref[r:end, cols] = gn.astype(bf16)
            gd_ref[r:end, head : head + 1] = gd
            one, two, scale = side(scr[r:end, VW:PW], 0, head)
            phi = one * two * scale * continues(idx_ref, r, end)
            mat = mat + dot_full(phi, gn, ((0,), (0,)))
            vec = vec + jnp.sum(phi * gd, axis=0, keepdims=True)
        store_state(out_ref, head, mat, vec)


def attend_back_inside_kernel(
    idx_ref, p_ref, gn_ref, gd_ref, gqk, gv, scr,
):
    to_order(idx_ref, p_ref, scr)
    u_all = scr[:, VW:PW]
    gqk[...] = jnp.zeros((ROWS, QK), f32)
    gv[...] = jnp.zeros((ROWS, VW), f32)
    for head in range(LOCAL_HEADS):
        cols = slice(head * DV, (head + 1) * DV)
        v_all = scr[:, cols]
        back_all = matmul(u_all, mover(1, head)).astype(bf16)
        for r in range(0, ROWS, TILE):
            end = r + TILE
            low_gn = gn_ref[r:end, cols]
            gd = gd_ref[r:end, head : head + 1]
            moved = matmul(scr[r:end, VW:PW], mover(0, head)).astype(bf16)
            s = matmul(moved, u_all[:end], ((1,), (1,)))
            allowed = allowed_at(idx_ref, r, end)
            kern = jnp.where(allowed, 1.0 + s + 0.5 * s * s, 0.0).astype(bf16)
            gk = matmul(low_gn, v_all[:end], ((1,), (1,))) + gd
            gs = jnp.where(allowed, gk * (1.0 + s), 0.0).astype(bf16)
            gqk[r:end, :] = gqk[r:end, :] + matmul(gs, back_all[:end])
            gqk[:end, :] = gqk[:end, :] + matmul(gs, moved, ((0,), (0,)))
            gv[:end, cols] = gv[:end, cols] + matmul(kern, low_gn, ((0,), (0,)))


def attend_back_kernel(
    idx_ref, p_ref, gn_ref, gd_ref, gqk_ref, gv_ref, state_ref, grad_state_ref,
    out_ref, scr, gqk, gv,
):
    to_order(idx_ref, p_ref, scr)
    for head in range(LOCAL_HEADS):
        cols = slice(head * DV, (head + 1) * DV)
        mat, vec = state_rows(state_ref, head)
        gmat, gvec = state_rows(grad_state_ref, head)
        for r in range(0, ROWS, TILE):
            end = r + TILE
            u = scr[r:end, VW:PW]
            cont = continues(idx_ref, r, end)
            in_last = is_last(idx_ref, r, end)
            gn = gn_ref[r:end, cols]
            gd = gd_ref[r:end, head : head + 1]
            one, two, scale = side(u, 0, head)
            left, right = sides_of(0, head)
            grad = (dot_low_right(gn, mat) + gd * vec) * cont * scale
            acc = matmul((grad * two).astype(bf16), left, ((1,), (1,)))
            acc = acc + matmul((grad * one).astype(bf16), right, ((1,), (1,)))
            one, two, scale = side(u, 1, head)
            left, right = sides_of(1, head)
            grad = (dot_low_right(scr[r:end, cols], gmat) + gvec) * in_last * scale
            acc = acc + matmul((grad * two).astype(bf16), left, ((1,), (1,)))
            acc = acc + matmul((grad * one).astype(bf16), right, ((1,), (1,)))
            phi = one * two * scale * in_last
            before = gqk_ref if head == 0 else gqk
            gqk[r:end, :] = before[r:end, :] + acc
            gv[r:end, cols] = gv_ref[r:end, cols] + dot_low(phi, gmat.astype(bf16), ((1,), (0,)))
    for i in range(8):
        chunk = slice(i * CHUNK, (i + 1) * CHUNK)
        from_order(
            idx_ref, i, out_ref,
            jnp.concatenate([gv[chunk, :], gqk[chunk, :]], axis=1).astype(bf16),
        )


def dot_low_right(a, b):
    hi, lo = split(b)
    return matmul(a, hi, ((1,), (1,))) + matmul(a, lo, ((1,), (1,)))


def call(kernel, outs, scratch, n_in):
    return pl.pallas_call(
        kernel,
        out_shape=outs,
        in_specs=[pl.BlockSpec(memory_space=pltpu.SMEM)]
        + [pl.BlockSpec(memory_space=pltpu.VMEM)] * (n_in - 1),
        out_specs=[pl.BlockSpec(memory_space=pltpu.VMEM)] * len(outs),
        scratch_shapes=scratch,
        compiler_params=pltpu.CompilerParams(vmem_limit_bytes=48 * 1024 * 1024),
    )


def adam_step(weight, moment_one, moment_two, reduced, step_rate):
    new_one = beta_one * moment_one + (1.0 - beta_one) * reduced
    new_two = beta_two * moment_two + (1.0 - beta_two) * reduced * reduced
    corrected_one = new_one / (1.0 - beta_one**STEP)
    corrected_two = new_two / (1.0 - beta_two**STEP)
    master = weight - step_rate * (
        corrected_one / (jnp.sqrt(corrected_two) + adam_eps) + weight_decay * weight
    )
    return (new_one, new_two, master)


def nothing_kernel(other_ref, a_ref, out_ref):
    pass


def after(a, other):
    return pl.pallas_call(
        nothing_kernel,
        out_shape=jax.ShapeDtypeStruct(a.shape, a.dtype),
        in_specs=[pl.BlockSpec(memory_space=pl.ANY)] * 2,
        out_specs=pl.BlockSpec(memory_space=pl.ANY),
        input_output_aliases={1: 0},
    )(other, a)


def pack_first_kernel(value_ref, feature_ref, output_ref, gain_row_ref, gain_col_ref, out_ref):
    def low(a):
        return a.astype(bf16).astype(f32)

    out_ref[:, :VW] = low(output_ref[...]).T.astype(bf16)
    out_ref[:, VW : 2 * VW] = (low(value_ref[...]) * gain_col_ref[:, 0:1]).astype(bf16)
    out_ref[:, 2 * VW : VW + PW] = (low(feature_ref[...]) * gain_row_ref[0:1]).T.astype(bf16)
    out_ref[:, VW + PW :] = jnp.zeros((CHUNK, AW - VW - PW), bf16)


def pack_mlp_kernel(gateup_ref, down_ref, gain_row_ref, out_ref):
    def low(a):
        return a.astype(bf16).astype(f32)

    def wide(a):
        return jnp.concatenate([a, jnp.zeros((FFP - FFL, CHUNK), f32)], axis=0).T.astype(bf16)

    out_ref[:, :FFP] = wide(low(gateup_ref[0]) * gain_row_ref[1:2])
    out_ref[:, FFP : 2 * FFP] = wide(low(gateup_ref[1]) * gain_row_ref[1:2])
    out_ref[:, 2 * FFP :] = wide(low(down_ref[...]))


def adam_store(weight, first, second, grad, rate, outs, at=()):
    place = at if at else (slice(None), slice(None))
    for ref, new in zip(outs, adam_step(weight[place], first[place], second[place], grad, rate)):
        ref[place] = new


def adam_mlp_kernel(
    grad_ref, gain_row_ref, gw, gf, gs, dw, df, ds, g1, g2, g3, d1, d2, d3
):
    for part in range(2):
        grad = grad_ref[part * FFP : part * FFP + FFL].astype(f32)
        adam_store(
            gw, gf, gs, grad * gain_row_ref[1:2], D ** (-0.5), (g1, g2, g3),
            (part, slice(None), slice(None)),
        )
    adam_store(dw, df, ds, grad_ref[2 * FFP : 2 * FFP + FFL].astype(f32), FF ** (-0.5), (d1, d2, d3))


def adam_attn_kernel(
    grad_ref, gain_row_ref,
    fw, ff, fs, vw, vf, vs, ow, of, os, f1, f2, f3, v1, v2, v3, o1, o2, o3,
):
    grad = (grad_ref[VW : 2 * VW].astype(f32) * gain_row_ref[0:1]).T
    adam_store(vw, vf, vs, grad, D ** (-0.5), (v1, v2, v3))
    grad = grad_ref[2 * VW :].astype(f32) * gain_row_ref[0:1]
    adam_store(fw, ff, fs, grad, D ** (-0.5), (f1, f2, f3))
    grad = grad_ref[:VW].astype(f32)
    adam_store(ow, of, os, grad, (HEADS * DV // 64) ** (-0.5), (o1, o2, o3))


def turned(a):
    return a.astype(f32).T.astype(bf16)


def store_owners(out_ref, lo, hi, tile):
    for k in range(2):
        out_ref[k, 0, lo:hi, :] = tile[:, k * CHUNK : (k + 1) * CHUNK].astype(bf16)


def mlp_grads_kernel(core_ref, other_ref, a0, a1, g0, g1, gu0, gu1, h0, h1, out_ref, scr):
    @pl.when(pl.program_id(0) == 0)
    def turn():
        for half, (gu, h) in enumerate(((gu0, h0), (gu1, h1))):
            cols = slice(half * HALF, (half + 1) * HALF)
            for j in range(FFP // TILE):
                rows = slice(j * TILE, (j + 1) * TILE)
                later = slice(FFP + j * TILE, FFP + (j + 1) * TILE)
                scr[rows, cols] = turned(gu[:, 2 * j * TILE : (2 * j + 1) * TILE])
                scr[later, cols] = turned(gu[:, (2 * j + 1) * TILE : (2 * j + 2) * TILE])
            scr[2 * FFP :, cols] = turned(h[...])

    for lo, hi, left, right in ((0, 2 * FFP, a0, a1), (2 * FFP, 3 * FFP, g0.at[0], g1.at[0])):
        tile = matmul(scr[lo:hi, :HALF], left[...]) + matmul(scr[lo:hi, HALF:], right[...])
        store_owners(out_ref, lo, hi, tile)


def attn_grads_kernel(core_ref, other_ref, a0, a1, g0, g1, rows_ref, proj_ref, out_ref, scr):
    @pl.when(pl.program_id(0) == 0)
    def turn():
        scr[:VW] = turned(rows_ref[...])
        scr[VW : 2 * VW] = turned(proj_ref[:, :VW])
        scr[2 * VW :] = turned(proj_ref[:, VW:])

    for lo, hi, left, right in ((0, VW, g0, g1), (VW, VW + PW, a0, a1)):
        tile = matmul(scr[lo:hi, :HALF], left[...]) + matmul(scr[lo:hi, HALF:], right[...])
        store_owners(out_ref, lo, hi, tile)


def grads(kernel, height, place, other, tiled, whole, turned_rows, blocks=(), split=()):
    def by_owner(n):
        return pl.BlockSpec((2, 1, n, CHUNK), lambda i, core: (0, i, 0, 0))

    def full(a):
        return pl.BlockSpec(a.shape, lambda i, core: (0,) * a.ndim)

    in_specs = [pl.BlockSpec(memory_space=pl.ANY)]
    in_specs += [pl.BlockSpec((HALF, TILE), lambda i, core: (0, i))] * len(tiled)
    operands = list(tiled)
    for a in split:
        in_specs += [
            pl.BlockSpec((1, HALF, TILE), lambda i, core: (core[0], 0, i)),
            pl.BlockSpec((1, HALF, TILE), lambda i, core: (1 - core[0], 0, i)),
        ]
        operands += [a, a]
    in_specs += [by_owner(a.shape[2]) for a in blocks] + [full(a) for a in whole]
    return pl.pallas_call(
        kernel,
        grid_spec=pltpu.PrefetchScalarGridSpec(
            num_scalar_prefetch=1,
            grid=(D // TILE,),
            in_specs=in_specs,
            out_specs=by_owner(height),
            scratch_shapes=[pltpu.VMEM((turned_rows, ROWS), bf16)],
        ),
        out_shape=jax.ShapeDtypeStruct((2, 8, height, CHUNK), bf16),
        compiler_params=pltpu.CompilerParams(vmem_limit_bytes=48 * 1024 * 1024),
    )(place, other, *operands, *blocks, *whole)


def mlp_kernel(
    core_ref, a0, a1, g0, g1, gate_ref, up_ref, down_ref,
    h0, h1, gu0, gu1, gateup_out, down_out,
):
    weights = [ref[0].reshape(D, TILE) for ref in (gate_ref, up_ref, down_ref)]
    gateup_out[:, :TILE] = weights[0]
    gateup_out[:, TILE:] = weights[1]
    down_out[...] = weights[2]
    for a, g, h, gu in ((a0, g0, h0, gu0), (a1, g1, h1, gu1)):
        gate = matmul(a[...], weights[0])
        up = matmul(a[...], weights[1])
        grad = matmul(g[0], weights[2])
        sigmoid = jax.nn.sigmoid(gate)
        silu = gate * sigmoid
        h[...] = (silu * up).astype(bf16)
        gu[:, :TILE] = (grad * up * (sigmoid * (1.0 + gate * (1.0 - sigmoid)))).astype(bf16)
        gu[:, TILE:] = (grad * silu).astype(bf16)


def mlp(place, acts, grad, every):
    steps = FFP // TILE

    def cols(part):
        return pl.BlockSpec(
            (1, N_GROUPS, CHUNK, TILE), lambda j, core: (core[0], 0, 0, part * steps + j)
        )

    hidden = pl.BlockSpec((HALF, TILE), lambda j, core: (0, j))

    def wide(n, width):
        return pl.BlockSpec((n, width), lambda j, core: (0, j))

    return pl.pallas_call(
        mlp_kernel,
        grid_spec=pltpu.PrefetchScalarGridSpec(
            num_scalar_prefetch=1,
            grid=(steps,),
            in_specs=[pl.BlockSpec((HALF, D), lambda j, core: (0, 0))] * 2
            + [
                pl.BlockSpec((1, HALF, D), lambda j, core: (core[0], 0, 0)),
                pl.BlockSpec((1, HALF, D), lambda j, core: (1 - core[0], 0, 0)),
                cols(0), cols(1), cols(2),
            ],
            out_specs=[hidden] * 2 + [wide(HALF, 2 * TILE)] * 2 + [wide(D, 2 * TILE), wide(D, TILE)],
        ),
        out_shape=[jax.ShapeDtypeStruct((HALF, FFP), bf16)] * 2
        + [jax.ShapeDtypeStruct((HALF, 2 * FFP), bf16)] * 2
        + [jax.ShapeDtypeStruct((D, 2 * FFP), bf16), jax.ShapeDtypeStruct((D, FFP), bf16)],
        compiler_params=pltpu.CompilerParams(vmem_limit_bytes=56 * 1024 * 1024),
    )(place, *acts, grad, grad, every, every, every)


def project_kernel(core_ref, a0, a1, w_ref, out_ref, acc):
    step = pl.program_id(0)

    @pl.when(step == 0)
    def start():
        acc[...] = jnp.zeros_like(acc)

    weight = w_ref[0].reshape(WIDE, AW)[:, VW : VW + PW]
    acc[:HALF] += matmul(a0[...], weight)
    acc[HALF:] += matmul(a1[...], weight)

    @pl.when(step == D // WIDE - 1)
    def end():
        out_ref[...] = acc[...].astype(bf16)


def project(core, acts, every):
    return pl.pallas_call(
        project_kernel,
        grid_spec=pltpu.PrefetchScalarGridSpec(
            num_scalar_prefetch=1,
            grid=(D // WIDE,),
            in_specs=[pl.BlockSpec((HALF, WIDE), lambda i, core: (0, i))] * 2
            + [pl.BlockSpec((1, WIDE // CHUNK, CHUNK, AW), lambda i, core: (core[0], i, 0, 0))],
            out_specs=pl.BlockSpec((ROWS, PW), lambda i, core: (0, 0)),
            scratch_shapes=[pltpu.VMEM((ROWS, PW), f32)],
        ),
        out_shape=jax.ShapeDtypeStruct((ROWS, PW), bf16),
        compiler_params=pltpu.CompilerParams(vmem_limit_bytes=48 * 1024 * 1024),
    )(core, *acts, every)


def plain(kernel, outs, *args):
    return pl.pallas_call(
        kernel,
        out_shape=outs,
        compiler_params=pltpu.CompilerParams(vmem_limit_bytes=48 * 1024 * 1024),
    )(*args)


def same(*arrays):
    return [jax.ShapeDtypeStruct(a.shape, f32) for a in arrays]


def unit_norm(rows):
    inv = lax.rsqrt(jnp.mean(rows * rows, axis=-1, keepdims=True) + norm_eps)
    return rows * inv, inv


def unit_norm_back(shaped, unit, inv):
    return inv * (shaped - unit * jnp.mean(shaped * unit, axis=-1, keepdims=True))


def exchange(a):
    return lax.all_to_all(a, GROUPS, 0, 0)


def shards(
    tokens, cotangent, row_lengths, gains, gain_first, gain_second,
    feature_weight, feature_first, feature_second,
    value_weight, value_first, value_second,
    output_weight, output_first, output_second,
    gateup_weight, gateup_first, gateup_second,
    down_weight, down_first, down_second,
):
    core = lax.axis_index("core")
    group = (lax.axis_index("x_lo") * 4 + lax.axis_index("z")) * 2 + lax.axis_index("x_hi")
    gain_low = gains.astype(bf16).astype(f32)
    place = jnp.reshape(core, (1,)).astype(jnp.int32)

    gain_col = gain_low.T
    flat = [jnp.transpose(a, (1, 2, 0)) for a in (gateup_weight, gateup_first, gateup_second)]
    thin = [
        jnp.transpose(a, (1, 2, 0)).reshape(QK, CHUNK)
        for a in (feature_weight, feature_first, feature_second)
    ]
    first_part = plain(
        pack_first_kernel,
        jax.ShapeDtypeStruct((CHUNK, AW), bf16),
        value_weight, thin[0], output_weight, gain_low, gain_col,
    )
    gateup_part = plain(
        pack_mlp_kernel,
        jax.ShapeDtypeStruct((CHUNK, 3 * FFP), bf16),
        flat[0], down_weight, gain_low,
    )

    def gather_weights(part):
        every = lax.all_gather(part, ("x_hi", "x_lo", "z", "core"))
        return every.reshape(2, N_GROUPS, CHUNK, part.shape[1])

    def own_slice(every):
        return lax.dynamic_index_in_dim(every, core, 0, False)

    owner = (lax.axis_index("x_lo") * 4 + lax.axis_index("z")) * 2 + lax.axis_index("x_hi")
    every_attn = gather_weights(first_part)
    both = cross(jnp.stack([tokens, cotangent]))
    tokens = both[0]
    cot = both[1]
    inputs = tokens.astype(f32)
    unit_one, inv_one = unit_norm(inputs)
    acts_one = gather_rows(spread(unit_one.astype(bf16)))
    grad_mlp = lax.all_gather(after(after(cot, acts_one[0]), every_attn), ("core", "y")).reshape(2, HALF, D)
    proj = project(place, acts_one, every_attn)
    attn_w = own_slice(after(every_attn, proj))
    first_own = lax.dynamic_index_in_dim(attn_w, owner, 0, False)[:, VW : VW + PW].astype(f32).T
    attn_w = attn_w.reshape(D, AW)
    out_w = attn_w[:, :VW]
    proj_w = attn_w[:, VW : VW + PW]

    ends = jnp.cumsum(row_lengths)

    def doc_of(pos):
        return jnp.sum((pos[..., None] >= ends).astype(jnp.int32), axis=-1)

    places = jnp.arange(N_GROUPS, dtype=jnp.int32)
    group_ids = (places % 8) * 2 + places // 8
    doc_end = doc_of(group_ids * ROWS + (ROWS - 1))
    doc_before = jnp.where(group_ids > 0, doc_of(group_ids * ROWS - 1), -1)
    last_doc = doc_of(group * ROWS + (ROWS - 1))
    before = jnp.where(group > 0, doc_of(group * ROWS - 1), -1)
    carry = ((group_ids[None, :] < group_ids[:, None]) & (doc_end[None, :] == doc_before[:, None])).astype(f32)
    back = ((group_ids[None, :] > group_ids[:, None]) & (doc_before[None, :] == doc_end[:, None])).astype(f32)
    chunk_ids = jnp.arange(8, dtype=jnp.int32)
    idx = ((chunk_ids % 2) ^ core) * 4 + chunk_ids // 2
    idx = jnp.concatenate([idx, ends, jnp.stack([group * ROWS, last_doc, before])]).astype(jnp.int32)

    own_state = call(
        key_state_kernel,
        [jax.ShapeDtypeStruct((STATE_ROWS, DV), f32)],
        [pltpu.VMEM((ROWS, PW), bf16)],
        2,
    )(idx, proj)[0]
    every_mlp = gather_weights(after(gateup_part, own_state))
    gateup_own = lax.dynamic_slice(
        every_mlp, (core, owner, 0, 0), (1, 1, CHUNK, 2 * FFP)
    ).reshape(CHUNK, 2 * FFP)
    gateup_own = gateup_own.T
    slices = exchange(own_state.reshape(N_GROUPS, STATE_ROWS // N_GROUPS, DV))
    slices = jnp.sum(carry[:, :, None, None] * slices[None], axis=1)
    state = exchange(slices).reshape(STATE_ROWS, DV)
    num, den = call(
        attend_inside_kernel,
        [jax.ShapeDtypeStruct((ROWS, VW), f32), jax.ShapeDtypeStruct((ROWS, LOCAL_HEADS), f32)],
        [pltpu.VMEM((ROWS, PW), bf16)],
        2,
    )(idx, proj)
    att, den, attn_rows = call(
        attend_kernel,
        [
            jax.ShapeDtypeStruct((ROWS, VW), f32),
            jax.ShapeDtypeStruct((ROWS, LOCAL_HEADS), f32),
            jax.ShapeDtypeStruct((ROWS, VW), bf16),
        ],
        [pltpu.VMEM((ROWS, PW), bf16)],
        5,
    )(idx, proj, num, after(den, attn_w), state)

    middle, spread_two = on_rows(
        norm_kernel, scatter_rows(rows_of(halves_of(attn_rows), out_w, ((1,), (1,)))), inputs
    )
    acts_two = gather_rows(spread_two)
    hid0, hid1, gu0, gu1, gateup_w, down_w = mlp(place, acts_two, grad_mlp, every_mlp)
    hidden = [hid0, hid1]
    grad_gate_up = [gu0, gu1]

    late = []

    def mlp_grads(send, low):
        mlp_grad = grads(
            mlp_grads_kernel, 3 * FFP, place, low, acts_two, (*grad_gate_up, *hidden), 3 * FFP,
            split=(grad_mlp,),
        ).reshape(N_GROUPS * 3 * FFP, CHUNK)
        late.append(mlp_grad)

    grad_mid, spread_grad = on_rows(
        norm_back_kernel, scatter_rows(rows_of(grad_gate_up, gateup_w, ((1,), (1,))), mlp_grads), middle, cot
    )
    mlp_grad = lax.psum_scatter(after(late[0], grad_mid), GROUPS, scatter_dimension=0, tiled=True)
    grad_attn = gather_rows(spread_grad)
    grad_low = jnp.concatenate([matmul(a, out_w).astype(bf16) for a in grad_attn])
    own_grad, gn, gd = call(
        query_state_kernel,
        [
            jax.ShapeDtypeStruct((STATE_ROWS, DV), f32),
            jax.ShapeDtypeStruct((ROWS, VW), bf16),
            jax.ShapeDtypeStruct((ROWS, LOCAL_HEADS), f32),
        ],
        [pltpu.VMEM((ROWS, PW), bf16), pltpu.VMEM((ROWS, VW), bf16)],
        5,
    )(idx, proj, grad_low, att, den)
    den_part = jnp.sum(jnp.abs(den))
    slices = exchange(
        jnp.concatenate(
            [
                own_grad.reshape(N_GROUPS, STATE_ROWS // N_GROUPS, DV),
                jnp.full((N_GROUPS, 8, DV), den_part, f32),
            ],
            axis=1,
        )
    )
    den_group = jnp.sum(slices[:, STATE_ROWS // N_GROUPS :], axis=0)
    slices = jnp.sum(back[:, :, None, None] * slices[None, :, : STATE_ROWS // N_GROUPS], axis=1)
    grad_state = exchange(slices).reshape(STATE_ROWS, DV)
    gqk, gv = call(
        attend_back_inside_kernel,
        [jax.ShapeDtypeStruct((ROWS, QK), f32), jax.ShapeDtypeStruct((ROWS, VW), f32)],
        [pltpu.VMEM((ROWS, PW), bf16)],
        4,
    )(idx, proj, gn, gd)
    mlp_grad_own = cross(after(mlp_grad, grad_state))
    grad_proj = call(
        attend_back_kernel,
        [jax.ShapeDtypeStruct((ROWS, PW), bf16)],
        [pltpu.VMEM((ROWS, PW), bf16), pltpu.VMEM((ROWS, QK), f32), pltpu.VMEM((ROWS, VW), f32)],
        8,
    )(idx, proj, gn, gd, gqk, gv, state, grad_state)[0]

    def proj_grads(send, low):
        attn_grad = grads(
            attn_grads_kernel, VW + PW, place, place, acts_one + grad_attn,
            (attn_rows, grad_proj), VW + PW,
        ).reshape(N_GROUPS, VW + PW, CHUNK)
        late.append(exchange(attn_grad))
        mixed_parts = [
            matmul(after(a, low), down_w, ((1,), (1,))).astype(bf16) for a in hidden
        ]
        other = swap_core(mixed_parts[1])
        late.append((mixed_parts[0].astype(f32) + other.astype(f32)).astype(bf16))


    shaped_one = scatter_rows(rows_of(halves_of(grad_proj), proj_w, ((1,), (1,))), proj_grads, sum_rows_apart)
    mixed = middle + sum_rows_apart(after(late[2], shaped_one))
    mixed = cross(mixed.astype(bf16))
    grad_tokens = grad_mid + unit_norm_back(shaped_one, unit_one, inv_one)
    grad_tokens = cross(grad_tokens.astype(bf16)).astype(f32)
    deep = plain(
        adam_mlp_kernel,
        same(*flat, down_weight, down_first, down_second),
        mlp_grad_own, gain_low, *flat, down_weight, down_first, down_second,
    )
    attn_grad = jnp.sum(after(late[1], deep[0]).astype(f32), axis=0)
    gain_one = jnp.sum(attn_grad[VW:] * first_own, axis=0)
    gain_two = jnp.sum(mlp_grad[: 2 * FFP].astype(f32) * gateup_own.astype(f32), axis=0)
    small = jnp.concatenate([gain_one[None], gain_two[None], den_group[:6]], axis=0)
    parts = lax.all_to_all(
        jnp.broadcast_to(small[None], (16, 8, CHUNK)), ("core", "y", "x_hi"), 0, 0
    ).reshape(8, 2, 8, CHUNK)
    small = jnp.sum(jnp.where(core == 0, parts[:, 0], parts[:, 1]), axis=0)
    attn_grad = cross(attn_grad.astype(bf16))

    gain_total = small[:2] / gain_low
    den_mean = small[2, 0] / (N_GROUPS * ROWS * HEADS)
    near = (*thin, value_weight, value_first, value_second, output_weight, output_first, output_second)
    near = plain(adam_attn_kernel, same(*near), attn_grad, gain_low, *near)
    news = list(adam_step(gains, gain_first, gain_second, gain_total, gain_rate))
    news += [jnp.transpose(a.reshape(2, QK // 2, CHUNK), (2, 0, 1)) for a in near[:3]]
    news += near[3:]
    news += [jnp.transpose(a, (2, 0, 1)) for a in deep[:3]]
    news += deep[3:]
    return (mixed, grad_tokens, den_mean) + tuple(news)


def solution(mesh):
    fine = jax.sharding.Mesh(mesh.devices.reshape(2, 4, 2, 4, 2), FINE)
    dp = ("x_lo", "z", "core")
    tensor = ("y", "x_hi")
    rows = P(FINE, None)
    gain = P(None, dp)
    deep = P(dp, None, tensor)
    down = P(dp, tensor)
    across = P(tensor, dp)
    return jax.shard_map(
        shards,
        mesh=fine,
        in_specs=(rows, rows, P())
        + (gain,) * 3
        + (deep,) * 3
        + (down,) * 3
        + (across,) * 3
        + (deep,) * 3
        + (across,) * 3,
        out_specs=(rows, rows, P())
        + (gain,) * 3
        + (deep,) * 3
        + (down,) * 3
        + (across,) * 3
        + (deep,) * 3
        + (across,) * 3,
        check_vma=False,
    )
```
